128 devices in a mesh: dp: 16 (over y, x), expert: 8 (over z, core).
Axes of the slice: x: 4, y: 4, z: 4, core: 2. Of those that a mesh axis runs over, the one named last changes fastest.
Arguments:
- tokens: bfloat16 [16384, 1024], P(('dp', 'expert')), may hold values from -24 to 24
- segments: int32 [16, 1024], P('dp'), may hold values from 0 to 6, as said below
- routes: int32 [16384, 8], P(('dp', 'expert')), may hold values from 0 to 31, all different within a row; in each aligned block of 128 rows (0 to 127, 128 to 255, ...) at most 48 rows name the same one
- gain_attn: bfloat16 [1024], P(('dp', 'expert')), may hold values from 0.5 to 1.5
- gain_ffn: bfloat16 [1024], P(('dp', 'expert')), may hold values from 0.5 to 1.5
- w_query: bfloat16 [1024, 1024], P(('dp', 'expert')), may hold values from -0.1875 to 0.1875
- w_key: bfloat16 [1024, 512], P(('dp', 'expert')), may hold values from -0.1875 to 0.1875
- w_value: bfloat16 [1024, 512], P(('dp', 'expert')), may hold values from -0.1875 to 0.1875
- w_out: bfloat16 [1024, 1024], P(('dp', 'expert')), may hold values from -0.75 to 0.75
- w_router: bfloat16 [1024, 32], P(('dp', 'expert')), may hold values from -0.09375 to 0.09375
- w_gate: bfloat16 [32, 1024, 512], P('expert'), may hold values from -0.1875 to 0.1875
- w_up: bfloat16 [32, 1024, 512], P('expert'), may hold values from -0.1875 to 0.1875
- w_down: bfloat16 [32, 512, 1024], P('expert'), may hold values from -1 to 1
- cotangent: bfloat16 [16384, 1024], P(('dp', 'expert')), may hold values from -6 to 6
Outputs:
- output: bfloat16 [16384, 1024], P(('dp', 'expert'))
- input_grad: float32 [16384, 1024], P(('dp', 'expert'))
- gain_attn_grad: float32 [1024], P(('dp', 'expert'))
- gain_ffn_grad: float32 [1024], P(('dp', 'expert'))
- w_query_grad: float32 [1024, 1024], P(('dp', 'expert'))
- w_key_grad: float32 [1024, 512], P(('dp', 'expert'))
- w_value_grad: float32 [1024, 512], P(('dp', 'expert'))
- w_out_grad: float32 [1024, 1024], P(('dp', 'expert'))
- w_router_grad: float32 [1024, 32], P(('dp', 'expert'))
- w_gate_grad: float32 [32, 1024, 512], P('expert', 'dp')
- w_up_grad: float32 [32, 1024, 512], P('expert', 'dp')
- w_down_grad: float32 [32, 512, 1024], P('expert', 'dp')
The draws below stay inside these ranges and needn't reach their ends.
Inputs may be any that keep to these rules, and one draw needn't show every extreme that they name: `segments`: along each row the numbers never fall and may skip values; one document covers at least positions 64 to 959, the others lie within the first and the last 64 positions. `routes`: each row names 8 different experts; within the rows of one device no expert is named more than 48 times, and in every draw some device's rows name some expert exactly 48 times.
All inputs are finite; a program needn't handle non-finite values.
Results may differ from the reference program's by a relative error of at most 0.02.
Values may be sent and summed in bfloat16 or wider, within the bound.
A program may use at most 128 MiB of HBM per device.

```python
import math
import jax
import jax.numpy as jnp
import numpy as np
from jax import lax

D = 1024
HEADS = 16
KV_HEADS = 8
HEAD = 64
FFE = 512
TOP = 8
TOK_DEV = 128
EXPERTS = 32
SEQ = 1024
TOKENS = 16384
CAP = 48
N_DP = 16


def draw_segments(key, part):
    key = jax.random.fold_in(key, 7)
    row_keys = jax.random.split(key, N_DP)

    def one_row(row_key):
        head_key, tail_key = jax.random.split(row_key)
        head_cuts = jax.random.randint(head_key, (3,), 1, TOK_DEV // 2 + 1, dtype=jnp.int32)
        tail_cuts = jax.random.randint(tail_key, (3,), SEQ - TOK_DEV // 2, SEQ, dtype=jnp.int32)
        cut_points = jnp.concatenate([head_cuts, tail_cuts])
        positions = jnp.arange(SEQ, dtype=jnp.int32)
        return jnp.sum((positions[:, None] >= cut_points[None, :]).astype(jnp.int32), axis=1, dtype=jnp.int32)
    return jax.vmap(one_row)(row_keys)


def raised(values, own_key, source, target, shards_of, factor):
    def block_of(position):
        return (jnp.arange(values.shape[position]) // (values.shape[position] // shards_of)).reshape((-1,) + (1,) * (values.ndim - 1 - position))

    first = jax.random.permutation(own_key, shards_of)[block_of(target)]
    far = (block_of(target) + shards_of // 2) % shards_of
    return jnp.where((block_of(source) == first) | (block_of(source) == far), factor * values, values)


def level_of(own_key, shape, pieces, smallest, high):
    def one(dim, shards_of):
        steps = jax.random.uniform(jax.random.fold_in(jax.random.fold_in(own_key, 6), dim), (shards_of,), jnp.float32, smallest / len(pieces), high / len(pieces))
        return jnp.repeat(jnp.exp(steps), shape[dim] // shards_of).reshape((-1,) + (1,) * (len(shape) - dim - 1))

    gain = one(*pieces[0])
    for cut in pieces[1:]:
        gain = gain * one(*cut)
    return gain


def deal_out(stream_key, own, number, rows, amount, top, reach, skew):
    order = jax.random.permutation(stream_key, amount)
    heavy_load, usual = load_shares(amount, rows * top, reach, skew, True), load_shares(amount, rows * top, reach, skew, False)
    places = jnp.arange(amount)

    def named(tallies, offset_by):
        used = int((tallies > 0).sum())
        fixed = max(1, used // 4)
        passed = fixed + (places - fixed + offset_by * (used - fixed)) % max(1, amount - fixed)
        return jnp.zeros((amount,), jnp.int32).at[order[jnp.where(places < fixed, places, passed)]].set(jnp.asarray(tallies, jnp.int32))

    tallies = jnp.where(number % 4 == 0, named(heavy_load, number // 4), named(usual, number - number // 4 - 1))
    mixed = jax.random.permutation(jax.random.fold_in(own, 3), amount)
    giver, receiver = mixed[0:amount // 2 * 2:2], mixed[1:amount // 2 * 2:2]
    room = jnp.minimum(tallies[giver] - 1, reach - tallies[receiver]) // 2
    room = jnp.where((giver == order[0]) | (receiver == order[0]) | (tallies[receiver] == 0), 0, jnp.maximum(room, 0))
    passed = jax.random.randint(jax.random.fold_in(own, 4), (amount // 2,), 0, 1 << 20) % (room + 1)
    tallies = tallies.at[giver].add(-passed).at[receiver].add(passed)
    items = jnp.searchsorted(jnp.cumsum(tallies), jnp.arange(rows * top), side="right").astype(jnp.int32)
    grid = items.reshape(top, rows).T
    grid = grid[jax.random.permutation(jax.random.fold_in(own, 1), rows)]
    offset_by = jax.random.randint(jax.random.fold_in(own, 2), (rows, 1), 0, top)
    return jnp.take_along_axis(grid, (jnp.arange(top)[None, :] + offset_by) % top, axis=1)


def load_shares(number_of, total, reach, lean, full):
    loads = [(1 << 20) // math.isqrt(rank ** lean) + 1 for rank in range(1, number_of + 1)]
    largest = reach if full else min(reach, max(-(-total // number_of), total * loads[0] // sum(loads)))
    least = 1 if total - largest >= number_of - 1 else 0
    holding, rest = [largest] + [least] * (number_of - 1), total - largest - least * (number_of - 1)
    while rest > 0:
        candidates = [i for i in range(1, number_of) if holding[i] < largest] or [i for i in range(1, number_of) if holding[i] < reach]
        whole, remaining = sum([loads[i] for i in candidates]), rest
        for i in candidates:
            more = min(reach - holding[i], max(1, remaining * loads[i] // whole), rest)
            holding[i] = holding[i] + more
            rest = rest - more
    return np.array(holding)


def gaussian(stream_key, dims, scale, reach, pieces=(), held_as=jnp.bfloat16):
    drawn = jax.random.normal(stream_key, dims, jnp.float32) * scale
    if len(pieces) > 0:
        drawn = level_of(stream_key, dims, pieces, -0.22, 0.18) * drawn
    return jnp.clip(drawn, min=-reach, max=reach).astype(held_as)


def bell_draw_with(rng, shape, deviation, most, cuts, heavy, kind=jnp.bfloat16):
    array = deviation * jax.random.normal(rng, shape, jnp.float32)
    if cuts:
        array = array * level_of(rng, shape, cuts, -0.22, 0.18)
    return jnp.clip(raised(array, jax.random.fold_in(rng, 3), *heavy), -most, most).astype(kind)


def setup_inputs(seed: int = 0) -> dict:
    key_list = jax.random.split(jax.random.key(seed), 15)
    tokens = bell_draw_with(key_list[0], (TOKENS, D), 1.0, 24.0, ((0, 128),), (0, 1, 128, 5.5))
    segments = draw_segments(jax.random.fold_in(key_list[14], 71), 0)
    routes_keys = jax.random.split(jax.random.fold_in(key_list[2], 1), TOKENS // TOK_DEV)
    routes_turns = jax.random.permutation(jax.random.fold_in(key_list[2], 3), TOKENS // TOK_DEV)
    routes = jax.vmap(lambda own, number: deal_out(jax.random.fold_in(key_list[2], 2), own, number, TOK_DEV, EXPERTS, TOP, CAP, 1))(routes_keys, routes_turns).reshape((TOKENS, TOP))
    gain_attn = jnp.clip(1.0 + 0.1 * jax.random.normal(key_list[3], (D,), jnp.float32), 0.5, 1.5).astype(jnp.bfloat16)
    gain_ffn = jnp.clip(1.0 + 0.1 * jax.random.normal(key_list[4], (D,), jnp.float32), 0.5, 1.5).astype(jnp.bfloat16)
    w_query = gaussian(key_list[5], (D, HEADS * HEAD), D ** -0.5, 0.1875, ((0, 128),))
    w_key = gaussian(key_list[6], (D, KV_HEADS * HEAD), D ** -0.5, 0.1875, ((0, 128),))
    w_value = gaussian(key_list[7], (D, KV_HEADS * HEAD), D ** -0.5, 0.1875, ((0, 128),))
    w_out = gaussian(key_list[8], (HEADS * HEAD, D), (HEADS * HEAD // 16) ** -0.5, 0.75, ((0, 128),))
    w_router = gaussian(key_list[9], (D, EXPERTS), (4 * D) ** -0.5, 0.09375, ((0, 128),))
    w_gate = gaussian(key_list[10], (EXPERTS, D, FFE), D ** -0.5, 0.1875, ((0, 8),))
    w_up = gaussian(key_list[11], (EXPERTS, D, FFE), D ** -0.5, 0.1875, ((0, 8),))
    w_down = gaussian(key_list[12], (EXPERTS, FFE, D), (FFE // 16) ** -0.5, 1.0, ((0, 8),))
    cotangent = gaussian(key_list[13], (TOKENS, D), 1.0, 6.0, ((0, 128),))
    return dict(tokens=tokens, segments=segments, routes=routes, gain_attn=gain_attn, gain_ffn=gain_ffn, w_query=w_query, w_key=w_key, w_value=w_value, w_out=w_out, w_router=w_router, w_gate=w_gate, w_up=w_up, w_down=w_down, cotangent=cotangent)


@jax.custom_vjp
def low(v):
    return lax.optimization_barrier(v.astype(jnp.bfloat16)).astype(jnp.float32)

@jax.custom_vjp
def low_back(v):
    return v

def low_keep(v):
    return (low(v), None)

def low_pass(kept, grad):
    return (grad,)

def back_keep(v):
    return (v, None)

def back_low(kept, grad):
    return (low(grad),)
low.defvjp(low_keep, low_pass)
low_back.defvjp(back_keep, back_low)
FULL_PRECISION = lax.Precision.HIGHEST
EPSILON = 1e-06

def matmul(factor_one, factor_two):
    return jnp.dot(factor_one, factor_two, precision=FULL_PRECISION, preferred_element_type=jnp.float32)

def normalize(values, norm_gain):
    inverse = lax.rsqrt(lax.optimization_barrier(jnp.mean(values * values, axis=-1, keepdims=True)) + EPSILON)
    return values * inverse * norm_gain

def rotary_tables(positions, half_width):
    inverse_freq = 10000.0 ** (-jnp.arange(half_width).astype(jnp.float32) / half_width)
    angles = positions.astype(jnp.float32)[:, None] * inverse_freq[None, :]
    return (jnp.cos(angles), jnp.sin(angles))

def rotate(values, cosine, sine_table):
    half_width = values.shape[-1] // 2
    first_half = values[..., :half_width]
    second_half = values[..., half_width:]
    cos_heads = cosine[:, None, :]
    sin_heads = sine_table[:, None, :]
    return jnp.concatenate([first_half * cos_heads - second_half * sin_heads, second_half * cos_heads + first_half * sin_heads], axis=-1)

def slot_tables(route_block, experts, capacity):
    entry_count = route_block.shape[0] * route_block.shape[1]
    flat_ids = route_block.reshape(-1).astype(jnp.int32)
    onehot = (flat_ids[:, None] == jnp.arange(experts, dtype=jnp.int32)[None, :]).astype(jnp.int32)
    slot_rank = lax.optimization_barrier(jnp.sum((jnp.cumsum(onehot, axis=0, dtype=jnp.int32) - 1) * onehot, axis=1, dtype=jnp.int32))
    entries = jnp.arange(entry_count, dtype=jnp.int32)
    slot_table = jnp.full((experts, capacity), entry_count, jnp.int32).at[flat_ids, slot_rank].set(entries)
    return (slot_table, slot_rank)

def group_forward(group_in, gain_attn, gain_ffn, w_query, w_key, w_value, w_out, w_router, w_gate, w_up, w_down, segment_row, route_group):
    length = group_in.shape[0]
    group_size = HEADS // KV_HEADS
    score_scale = HEAD ** (-0.5)
    hidden_one = low(normalize(group_in, gain_attn))
    positions = jnp.arange(length, dtype=jnp.int32)
    cosine, sine_table = rotary_tables(positions, HEAD // 2)
    query = low_back(matmul(hidden_one, w_query)).reshape(length, HEADS, HEAD)
    query = low(rotate(query, cosine, sine_table))
    rotated_key = low_back(matmul(hidden_one, w_key)).reshape(length, KV_HEADS, HEAD)
    rotated_key = low(rotate(rotated_key, cosine, sine_table))
    value_complete = low(low_back(matmul(hidden_one, w_value))).reshape(length, KV_HEADS, HEAD)
    block_rows = min(512, length)
    blocks = length // block_rows
    starts = jnp.arange(blocks, dtype=jnp.int32) * block_rows
    query_blocks = query.reshape(blocks, block_rows, KV_HEADS, group_size, HEAD)

    def one_block(block_args):
        query_slice, start = block_args
        attention_scores = jnp.einsum('oful,ifl->fuoi', query_slice, rotated_key, precision=FULL_PRECISION) * score_scale
        attention_scores = low_back(attention_scores)
        query_pos = start + jnp.arange(block_rows, dtype=jnp.int32)
        query_seg = lax.dynamic_slice_in_dim(segment_row, start, block_rows)
        allowed = (segment_row[None, :] == query_seg[:, None]) & (positions[None, :] <= query_pos[:, None])
        attention_scores = jnp.where(allowed[None, None], attention_scores, -1e+30)
        attention_weights = low(jax.nn.softmax(attention_scores, axis=-1))
        weighted_value_sum = jnp.einsum('iazd,diu->ziau', attention_weights, value_complete, precision=FULL_PRECISION)
        return weighted_value_sum.reshape(block_rows, HEADS * HEAD)
    attended = lax.map(jax.checkpoint(one_block), (query_blocks, starts))
    attended = low(low_back(attended.reshape(length, HEADS * HEAD)))
    residual = group_in + low_back(matmul(attended, w_out))
    hidden_two = low(normalize(residual, gain_ffn))
    logits = low_back(matmul(hidden_two, w_router))
    chosen = jnp.take_along_axis(logits, route_group, axis=1)
    gate_weights = jax.nn.softmax(chosen, axis=-1)
    sources = length // TOK_DEV
    route_blocks = route_group.reshape(sources, TOK_DEV, TOP)
    tables, slot_ranks = jax.vmap(lambda block_routes: slot_tables(block_routes, EXPERTS, CAP))(route_blocks)
    block_base = (jnp.arange(sources, dtype=jnp.int32) * TOK_DEV)[:, None, None]
    token_rows = jnp.where(tables < TOK_DEV * TOP, block_base + tables // TOP, length)
    token_rows = jnp.transpose(token_rows, (1, 0, 2)).reshape(EXPERTS, sources * CAP)
    padded = jnp.concatenate([hidden_two, jnp.zeros((1, hidden_two.shape[1]), jnp.float32)], axis=0)
    expert_in = low_back(padded[token_rows])
    gate_pre = low_back(jnp.einsum('emd,edf->emf', expert_in, w_gate, precision=FULL_PRECISION))
    up_pre = low_back(jnp.einsum('emd,edf->emf', expert_in, w_up, precision=FULL_PRECISION))
    product = low(jax.nn.silu(gate_pre) * up_pre)
    expert_out = low(low_back(jnp.einsum('emf,efd->emd', product, w_down, precision=FULL_PRECISION)))
    block_ids = jnp.arange(sources, dtype=jnp.int32)[:, None, None]
    route_index = route_blocks * (sources * CAP) + block_ids * CAP + slot_ranks.reshape(sources, TOK_DEV, TOP)
    returned = expert_out.reshape(EXPERTS * sources * CAP, -1)[route_index.reshape(length, TOP)]
    return residual + lax.optimization_barrier(jnp.sum(gate_weights[:, :, None] * returned, axis=1))

def reference(tokens, segments, routes, gain_attn, gain_ffn, w_query, w_key, w_value, w_out, w_router, w_gate, w_up, w_down, cotangent):
    params = [gain_attn.astype(jnp.float32), gain_ffn.astype(jnp.float32), w_query.astype(jnp.float32), w_key.astype(jnp.float32), w_value.astype(jnp.float32), w_out.astype(jnp.float32), w_router.astype(jnp.float32), w_gate.astype(jnp.float32), w_up.astype(jnp.float32), w_down.astype(jnp.float32)]
    token_groups = tokens.astype(jnp.float32).reshape(N_DP, SEQ, D)
    cot_groups = cotangent.astype(jnp.float32).reshape(N_DP, SEQ, D)
    route_groups = routes.reshape(N_DP, SEQ, TOP)

    def scan_step(totals, inputs):
        group_tokens, group_cot, segment_row, route_group = inputs

        def forward(group_in, *attention_weights):
            return group_forward(group_in, *attention_weights, segment_row, route_group)
        output, pullback = jax.vjp(forward, group_tokens, *params)
        gradients = pullback(group_cot)
        totals = tuple((running + addend for running, addend in zip(totals, gradients[1:])))
        return (totals, (output.astype(jnp.bfloat16), gradients[0]))
    zero_grads = tuple((jnp.zeros_like(parameter) for parameter in params))
    totals, outputs = lax.scan(scan_step, zero_grads, (token_groups, cot_groups, segments, route_groups))
    gain_attn_grad, gain_ffn_grad, w_query_grad, w_key_grad, w_value_grad, w_out_grad, w_router_grad, w_gate_grad, w_up_grad, w_down_grad = totals
    return (outputs[0].reshape(TOKENS, D), outputs[1].reshape(TOKENS, D), gain_attn_grad, gain_ffn_grad, w_query_grad, w_key_grad, w_value_grad, w_out_grad, w_router_grad, w_gate_grad, w_up_grad, w_down_grad)
```

```python
import functools
from types import SimpleNamespace

import jax
import jax.numpy as jnp
import numpy as np
from jax import lax
from jax.experimental import pallas as pl
from jax.experimental.pallas import tpu as pltpu
from jax.sharding import PartitionSpec as P

MESH = pl.DeviceIdType.MESH
LOW, WIDE = jnp.bfloat16, jnp.float32
EPSILON = 1e-06
SCALE = 64 ** (-0.5)
TOK, SEQ, D, SLOTS = 128, 1024, 1024, 384
Z_STEPS = (2, 1, 3)


def dot(one, two):
    return lax.dot_general(one, two, (((1,), (0,)), ((), ())), preferred_element_type=WIDE)


def tail_dot(one, two):
    return lax.dot_general(one, two, (((1,), (1,)), ((), ())), preferred_element_type=WIDE)


def lead_dot(one, two):
    return lax.dot_general(one, two, (((0,), (0,)), ((), ())), preferred_element_type=WIDE)


def place():
    i, j = lax.axis_index("dp"), lax.axis_index("expert")
    at = SimpleNamespace(i=i, j=j, x=lax.rem(i, 4), y=lax.div(i, 4), z=lax.div(j, 2), c=lax.rem(j, 2))
    at.sibling = (i, at.z * 2 + 1 - at.c)
    return at


def plus(value, step, size):
    return lax.rem(value + step, size)


def z_peer(at, step):
    return (at.i, plus(at.z, step, 4) * 2 + at.c)


def xy_peer(at, x_step, y_step):
    return (plus(at.y, y_step, 4) * 4 + plus(at.x, x_step, 4), at.j)


def send(source, target, sent, got, device):
    copy = pltpu.make_async_remote_copy(
        src_ref=source, dst_ref=target, send_sem=sent, recv_sem=got, device_id=device, device_id_type=MESH
    )
    copy.start()
    return copy


def rows(ref, block, size=TOK):
    return ref.at[pl.ds(pl.multiple_of(block * size, size), size)]


def columns(ref, block, size=128):
    return ref.at[:, pl.ds(pl.multiple_of(block * size, size), size)]


class Gather:
    def __init__(self, at, source, target, sent, got):
        self.at, self.source, self.target, self.sent, self.got = at, source, target, sent, got

    def start(self):
        at, mine = self.at, self.target(self.at.j)
        self.copies = [
            send(self.source, mine, self.sent.at[k], self.got.at[k], z_peer(at, step))
            for k, step in enumerate(Z_STEPS)
        ]
        self.copies.append(send(self.source, mine, self.sent.at[3], self.got.at[3], at.sibling))

    def forward(self):
        at = self.at
        for k, step in enumerate(Z_STEPS):
            self.copies[k].wait_recv()
            block = self.target(plus(at.z, 4 - step, 4) * 2 + at.c)
            self.copies.append(send(block, block, self.sent.at[4 + k], self.got.at[4 + k], at.sibling))

    def finish(self):
        for copy in self.copies[3:]:
            copy.wait_recv()
        for copy in self.copies:
            copy.wait_send()


def greet(devices):
    barrier = pltpu.get_barrier_semaphore()
    for device in devices:
        pl.semaphore_signal(barrier, inc=1, device_id=device, device_id_type=MESH)
    return lambda: pl.semaphore_wait(barrier, len(devices))


def expert_peers(at):
    return [(at.i, plus(at.j, step, 8)) for step in range(1, 8)]


def dp_peers(at):
    return [xy_peer(at, step % 4, step // 4) for step in range(1, 16)]


def lanes(shape):
    return lax.broadcasted_iota(jnp.int32, shape, len(shape) - 1)


def turn(values, cosine, signed_sine):
    lane = lanes(values.shape)
    swapped = jnp.where(
        lane % 64 < 32, pltpu.roll(values, 96, axis=1), pltpu.roll(values, 32, axis=1)
    )
    return values * cosine + swapped * signed_sine


def angles(r, here, shape):
    table = r.table[here, :]
    other, low_lanes = pltpu.roll(table, 64, axis=1), lanes(shape) < 64
    return jnp.where(low_lanes, table, other), jnp.where(low_lanes, other, table)


def both_heads(values, low_lanes):
    zero = jnp.zeros_like(values)
    return jnp.concatenate(
        [jnp.where(low_lanes, values, zero), jnp.where(low_lanes, zero, values)], axis=0
    )


def allowed_keys(r, token, start, length):
    query_segment, key_segment = r.seg_col[token, :], r.seg_row[:, 0:length].astype(WIDE)
    key_place = lax.broadcasted_iota(jnp.int32, (16, length), 1)
    query_place = lax.broadcasted_iota(jnp.int32, (16, length), 0) + start
    return (key_segment == query_segment) & (key_place <= query_place)


def front(r):
    at = place()
    ready = greet(expert_peers(at) + dp_peers(at))
    loads = []
    for n, (source, target) in enumerate(((r.gate_in, r.gate), (r.up_in, r.up), (r.down_in, r.down))):
        loads.append(pltpu.make_async_copy(source, target, r.load.at[n]))
        loads[-1].start()

    query_w, key_w = r.w_query[...].astype(WIDE), r.w_key[...].astype(WIDE)
    value_w, out_w, extra = r.w_value[...].astype(WIDE), r.w_out[...].astype(WIDE), r.extra[...]
    low_lanes = lanes((8, 128)) < 64
    for j in range(8):
        tile = slice(128 * (j // 2), 128 * (j // 2) + 128)
        key_part, value_part = key_w[:, tile], value_w[:, tile]
        if j % 2:
            key_part = pltpu.roll(key_part, 64, axis=1)
        else:
            value_part = pltpu.roll(value_part, 64, axis=1)
        head = slice(128 * j, 128 * j + 128)
        r.pack[j] = jnp.concatenate(
            [query_w[:, head], jnp.where(low_lanes, key_part, value_part), out_w[:, head], extra], axis=0
        ).astype(LOW)
    expert = lax.broadcasted_iota(jnp.int32, (128, TOK), 0)
    named = jnp.zeros((128, TOK), WIDE)
    for k in range(8):
        named = named + jnp.where(r.routes[k : k + 1, :] == expert, 1.0, 0.0)
    rows(r.named, at.j)[...] = jnp.transpose(named).astype(LOW)
    rows(r.hidden_one, at.j)[...] = r.tokens[...]
    r.stage[lax.div(at.j, 4), pl.ds(pl.multiple_of(lax.rem(at.j, 4) * 32, 32), 32)] = r.pack[at.j]
    for b in range(8):
        here = slice(TOK * b, TOK * (b + 1))
        across = jnp.broadcast_to(r.seg_row[:, here].astype(WIDE), (TOK, TOK))
        r.seg_col[here, :] = jnp.transpose(across)[:, 0:1]

    ready()
    tokens = Gather(at, r.tokens, lambda b: rows(r.hidden_one, b), r.x_sent, r.x_got)
    tokens.start()
    first = []
    place_in_stage = r.stage.at[lax.div(at.j, 4), pl.ds(pl.multiple_of(lax.rem(at.j, 4) * 32, 32), 32)]
    for step in range(1, 8):
        other = plus(at.j, step, 8)
        first.append(
            send(r.pack.at[other], place_in_stage, r.p_sent.at[step], r.p_got.at[step], (at.i, other))
        )
    marks = Gather(at, rows(r.named, at.j), lambda b: rows(r.named, b), r.n_sent, r.n_got)
    marks.start()
    for copy in first:
        copy.wait_recv()
    second = []
    for step in range(1, 16):
        second.append(
            send(
                r.stage, r.dense.at[:, at.y, at.x], r.w_sent.at[step], r.w_got.at[step],
                xy_peer(at, step % 4, step // 4),
            )
        )
    r.dense[:, at.y, at.x] = r.stage[...]
    tokens.forward()
    rows(r.upstream, at.j)[...] = r.cotangent[...]
    upstream = Gather(at, r.cotangent, lambda b: rows(r.upstream, b), r.g_sent, r.g_got)
    upstream.start()
    for copy in second:
        copy.wait_recv()

    def unpack(i, _):
        part = r.dense[:, lax.div(i, 4), lax.rem(i, 4)].reshape(8, 32, 128).astype(WIDE)
        here = pl.ds(pl.multiple_of(i * 64, 64), 64)
        r.w_qkv[here, 0:128] = part[:, 0:8, :].reshape(64, 128).astype(LOW)
        r.w_qkv[here, 128:256] = part[:, 8:16, :].reshape(64, 128).astype(LOW)
        r.w_out_part[here, :] = part[:, 16:24, :].reshape(64, 128).astype(LOW)
        r.extra_all[here, :] = part[:, 24:32, :].reshape(64, 128)
        return 0

    lax.fori_loop(0, 16, unpack, 0)
    out_weights = Gather(at, r.w_out_part, lambda b: columns(r.w_out_all, b), r.o_sent, r.o_got)
    out_weights.start()
    columns(r.w_out_all, at.j)[...] = r.w_out_part[...]
    r.gains[...] = extra_rows(r)
    r.router[...] = jnp.where(lanes((D, 128)) < 32, r.extra_all[...], 0.0).astype(LOW)
    tokens.finish()

    low_lanes = lanes((256, 128)) < 64

    def project(b, _):
        here = pl.ds(pl.multiple_of(b * 256, 256), 256)
        x = r.hidden_one[here, :].astype(WIDE)
        inverse = lax.rsqrt(jnp.mean(x * x, axis=-1, keepdims=True) + EPSILON)
        hidden = (x * inverse * r.gains[0:1, :]).astype(LOW)
        r.hidden_one[here, :] = hidden
        made = dot(hidden, r.w_qkv[...])
        cosine, sine = angles(r, here, (256, 128))
        r.queries[here, :] = turn(made[:, 0:128], cosine, sine).astype(LOW)
        pair = turn(
            made[:, 128:256], jnp.where(low_lanes, cosine, 1.0), jnp.where(low_lanes, sine, 0.0)
        )
        turned = pltpu.roll(pair, 64, axis=1)
        r.keys[here, :] = jnp.where(low_lanes, pair, turned).astype(LOW)
        r.values[here, :] = jnp.where(low_lanes, turned, pair).astype(LOW)
        return 0

    lax.fori_loop(0, 4, project, 0)
    marks.forward()
    hidden_save = pltpu.make_async_copy(r.hidden_one, r.hidden_far, r.load.at[3])
    hidden_save.start()

    low_lanes = lanes((TOK, 128)) < 64
    returned = []
    for b in range(8):
        length = TOK * (b + 1)
        both = both_heads(r.queries[TOK * b : TOK * (b + 1), :], low_lanes)
        r.scores[:, 0:length] = tail_dot(both, r.keys[0:length, :])

        def strip(t, _):
            token = pl.ds(pl.multiple_of(TOK * b + 16 * t, 16), 16)
            allowed = allowed_keys(r, token, TOK * b + 16 * t, length)
            logs = []
            for head in range(2):
                line = pl.ds(pl.multiple_of(TOK * head + 16 * t, 16), 16)
                scores = jnp.where(allowed, r.scores[line, 0:length] * SCALE, -1e30)
                top = jnp.max(scores, axis=-1, keepdims=True)
                powers = jnp.exp(scores - top)
                total = jnp.sum(powers, axis=-1, keepdims=True)
                r.probs[line, 0:length] = (powers * (1.0 / total)).astype(LOW)
                logs.append(top + jnp.log(total))
            lane = lanes((16, 128))
            r.log_total[token, :] = jnp.where(lane == 0, logs[0], jnp.where(lane == 1, logs[1], 0.0))
            return 0

        lax.fori_loop(0, 8, strip, 0)
        mixed = dot(r.probs[:, 0:length], r.values[0:length, :])
        r.attended_head[TOK * b : TOK * (b + 1), :] = jnp.where(low_lanes, mixed[0:TOK], mixed[TOK:]).astype(LOW)
        copy = pltpu.make_async_remote_copy(
            src_ref=r.attended_head.at[TOK * b : TOK * (b + 1)], dst_ref=columns(r.attended, at.j), send_sem=r.a_sent.at[b],
            recv_sem=r.a_got.at[at.j], device_id=(at.i, jnp.int32(b)), device_id_type=MESH,
        )
        returned.append(copy)

        @pl.when(at.j != b)
        def _():
            copy.start()

        @pl.when(at.j == b)
        def _():
            columns(r.attended, at.j)[...] = r.attended_head[TOK * b : TOK * (b + 1), :]

        if b == 3:
            upstream.forward()
        if b == 6:
            out_weights.forward()
    out_weights.finish()
    for b in range(8):

        @pl.when(at.j != b)
        def _():
            returned[b].wait_send()
            pltpu.make_async_remote_copy(
                src_ref=r.attended_head.at[TOK * b : TOK * (b + 1)], dst_ref=r.attended.at[:, 128 * b : 128 * b + 128],
                send_sem=r.a_sent.at[b], recv_sem=r.a_got.at[b], device_id=at.sibling, device_id_type=MESH,
            ).wait_recv()

    residual = r.tokens[...].astype(WIDE) + dot(r.attended[...], r.w_out_all[...])
    r.residual[...] = residual
    inverse = lax.rsqrt(jnp.mean(residual * residual, axis=-1, keepdims=True) + EPSILON)
    rows(r.hidden_two, at.j)[...] = (residual * inverse * r.gains[1:2, :]).astype(LOW)
    hidden = Gather(at, rows(r.hidden_two, at.j), lambda b: rows(r.hidden_two, b), r.h_sent, r.h_got)
    hidden.start()
    out_save = pltpu.make_async_copy(r.w_out_all, r.out_far, r.load.at[4])
    out_save.start()
    attended = Gather(at, r.attended, lambda b: rows(r.attended_all, b), r.t_sent, r.t_got)
    rows(r.attended_all, at.j)[...] = r.attended[...]
    for copy in first + second:
        copy.wait_send()
    upstream.finish()
    marks.finish()
    hidden_save.wait()
    out_save.wait()
    order_tokens(r, at)
    for copy in loads:
        copy.wait()
    lax.fori_loop(0, 4, lambda e, _: pick_upstream(r, at, e), 0)
    hidden.forward()
    hidden.finish()
    attended.start()
    return attended


def extra_rows(r):
    picked = [jnp.transpose(r.extra_all[TOK * b : TOK * (b + 1), :])[32:40, :] for b in range(8)]
    return jnp.concatenate(picked, axis=1)


def got(ref, semaphore, at):
    pltpu.make_async_remote_copy(
        src_ref=ref, dst_ref=ref, send_sem=semaphore, recv_sem=semaphore, device_id=at.sibling, device_id_type=MESH
    ).wait_recv()


def gone(ref, semaphore, at):
    pltpu.make_async_remote_copy(
        src_ref=ref, dst_ref=ref, send_sem=semaphore, recv_sem=semaphore, device_id=at.sibling, device_id_type=MESH
    ).wait_send()


class SumXY:
    def __init__(self, at, source, ways, sent, got_sems, x_first, height):
        self.at, self.source, self.ways, self.sent, self.got_sems = at, source, ways, sent, got_sems
        self.x_first, self.height = x_first, height
        self.f, self.s = (at.x, at.y) if x_first else (at.y, at.x)

    def block(self, first, second):
        return self.source.at[second, first] if self.x_first else self.source.at[first, second]

    def neighbour(self, along_first, step):
        return xy_peer(self.at, step, 0) if along_first == self.x_first else xy_peer(self.at, 0, step)

    def out(self, k, ref, target, along_first, step):
        send(ref, target, self.sent.at[k], self.got_sems.at[k], self.neighbour(along_first, step))

    def take(self, k, ref):
        got(ref, self.got_sems.at[k], self.at)

    def step1(self):
        far = plus(self.f, 2, 4)
        self.out(0, self.block(far, pl.ds(0, 2)), self.ways[0].at[0], True, 1)
        self.out(1, self.block(far, pl.ds(2, 2)), self.ways[0].at[1], True, 3)

    def step2(self):
        for k, step in enumerate((1, 3)):
            self.take(k, self.ways[0].at[k])
            near = plus(self.f, step, 4)
            part = self.block(near, pl.ds(2 * k, 2))
            part[...] = part[...] + self.ways[0][k]
            self.out(2 + k, self.block(near, pl.ds(0, 4)), self.ways[1].at[k], True, step)

    def step3(self):
        for k in range(2):
            self.take(2 + k, self.ways[1].at[k])
        mine = self.block(self.f, pl.ds(0, 4))
        mine[...] = mine[...] + (self.ways[1][0] + self.ways[1][1])
        half, far = self.height // 2, self.block(self.f, plus(self.s, 2, 4))
        self.out(4, far.at[pl.ds(0, half)], self.ways[2].at[0], False, 1)
        self.out(5, far.at[pl.ds(half, half)], self.ways[2].at[1], False, 3)

    def step4(self):
        half = self.height // 2
        for k, step in enumerate((1, 3)):
            self.take(4 + k, self.ways[2].at[k])
            near = self.block(self.f, plus(self.s, step, 4))
            part = near.at[pl.ds(half * k, half)]
            part[...] = part[...] + self.ways[2][k]
            self.out(6 + k, near, self.ways[3].at[k], False, step)

    def step5(self):
        for k in range(2):
            self.take(6 + k, self.ways[3].at[k])
        mine = self.block(self.f, self.s)
        return mine[...].astype(WIDE) + self.ways[3][0].astype(WIDE) + self.ways[3][1].astype(WIDE)

    def finish(self):
        far = plus(self.f, 2, 4)
        gone(self.block(far, pl.ds(0, 2)), self.sent.at[0], self.at)
        gone(self.block(far, pl.ds(2, 2)), self.sent.at[1], self.at)
        for k, step in enumerate((1, 3)):
            gone(self.block(plus(self.f, step, 4), pl.ds(0, 4)), self.sent.at[2 + k], self.at)
            part = self.block(self.f, plus(self.s, 2, 4)).at[pl.ds(self.height // 2 * k, self.height // 2)]
            gone(part, self.sent.at[4 + k], self.at)
            gone(self.block(self.f, plus(self.s, step, 4)), self.sent.at[6 + k], self.at)


class SumExpert:
    def __init__(self, at, r, pair_in, line_in, mine, sent, got_sems):
        self.at, self.r, self.pair_in, self.line_in = at, r, pair_in, line_in
        self.mine, self.sent, self.got_sems = mine, sent, got_sems

    def start(self, tiles):
        at, partial = self.at, self.r.partial

        def to_sibling(p, _):
            steps = (2 + p, 1 - p)
            blocks = [plus(at.z, step, 4) * 2 + 1 - at.c for step in steps]
            for n in range(4):
                part = slice(256 * n, 256 * (n + 1))
                made = tiles(*blocks, part)
                for k, step in enumerate(steps):
                    partial[step, :, part] = made[TOK * k : TOK * (k + 1)].astype(LOW)
            for step in steps:
                send(partial.at[step], self.pair_in.at[step], self.sent.at[step], self.got_sems.at[step], at.sibling)
            return 0

        lax.fori_loop(0, 2, to_sibling, 0)

        def along_z(p, _):
            steps = (2 + p, 1 - p)
            blocks = [plus(at.z, step, 4) * 2 + at.c for step in steps]
            for step in steps:
                got(self.pair_in.at[step], self.got_sems.at[step], at)
            for n in range(4):
                part = slice(256 * n, 256 * (n + 1))
                made = tiles(*blocks, part)
                first = made[0:TOK] + self.pair_in[steps[0], :, part].astype(WIDE)
                second = made[TOK:] + self.pair_in[steps[1], :, part].astype(WIDE)
                partial[3 + steps[0], :, part] = first.astype(LOW)

                @pl.when(p == 0)
                def _():
                    partial[3 + steps[1], :, part] = second.astype(LOW)

                @pl.when(p == 1)
                def _():
                    self.mine[:, part] = second

            def away(step):
                send(
                    partial.at[3 + step], self.line_in.at[step - 1], self.sent.at[3 + step],
                    self.got_sems.at[3 + step], z_peer(at, step),
                )

            away(steps[0])
            pl.when(p == 0)(lambda: away(steps[1]))
            return 0

        lax.fori_loop(0, 2, along_z, 0)

    def sent_all(self):
        for k in range(7):
            gone(self.r.partial.at[k], self.sent.at[k], self.at)

    def total(self):
        value = self.mine[...]
        for k in range(3):
            got(self.line_in.at[k], self.got_sems.at[4 + k], self.at)
            value = value + self.line_in[k].astype(WIDE)
        return value


def order_tokens(r, at):
    before = (
        lax.broadcasted_iota(jnp.int32, (TOK, TOK), 0) > lax.broadcasted_iota(jnp.int32, (TOK, TOK), 1)
    )
    before = jnp.where(before, 1.0, 0.0).astype(LOW)

    def block(b, earlier):
        here = pl.ds(pl.multiple_of(b * TOK, TOK), TOK)
        named = r.named[here, :]
        flags = named.astype(WIDE)
        order = jnp.where(flags > 0.0, dot(before, named) + earlier, -1.0)
        r.order_row[:, here] = jnp.transpose(order)[0:32]
        for e in range(4):
            mine = jnp.where(lanes((TOK, 128)) == 4 * at.j + e, order, 0.0)
            column = jnp.sum(mine, axis=-1, keepdims=True).astype(jnp.int32)
            r.places[here, SLOTS * e : SLOTS * (e + 1)] = jnp.where(
                column == lanes((TOK, SLOTS)), 1.0, 0.0
            ).astype(LOW)
        return earlier + jnp.sum(flags, axis=0, keepdims=True)

    lax.fori_loop(0, 8, block, jnp.zeros((1, 128), WIDE))


def share_tokens(r, at):
    def block(b, _):
        here = pl.ds(pl.multiple_of(b * TOK, TOK), TOK)
        named = r.named[here, :].astype(WIDE) > 0.0
        logits = jnp.where(named, dot(r.hidden_two[here, :], r.router[...]), -1e30)
        powers = jnp.where(named, jnp.exp(logits - jnp.max(logits, axis=-1, keepdims=True)), 0.0)
        shares = powers / jnp.sum(powers, axis=-1, keepdims=True)

        @pl.when(b == at.j)
        def _():
            r.shares[...] = shares

        r.shares_row[:, here] = jnp.transpose(shares)[0:32]
        return 0

    lax.fori_loop(0, 8, block, 0)


def hits(r, at, e, t):
    slot = lax.broadcasted_iota(jnp.int32, (TOK, SEQ), 0) + TOK * t
    return slot == r.order_row[pl.ds(4 * at.j + e, 1), :].astype(jnp.int32)


def pick_rows(r, at, e):
    def pick(t, _):
        r.partial[t] = jnp.where(hits(r, at, e, t), 1.0, 0.0).astype(LOW)
        return 0

    lax.fori_loop(0, 3, pick, 0)


def pick_upstream(r, at, e):
    pick_rows(r, at, e)
    here = pl.ds(pl.multiple_of(e * SLOTS, SLOTS), SLOTS)
    for n in range(4):
        part = slice(256 * n, 256 * (n + 1))
        r.slot_grad[here, part] = dot(r.partial[0:3].reshape(SLOTS, SEQ), r.upstream[:, part]).astype(LOW)
    return 0


def expert(r, at, e):
    row = pl.ds(4 * at.j + e, 1)
    here = pl.ds(pl.multiple_of(e * SLOTS, SLOTS), SLOTS)
    quarters = [slice(256 * n, 256 * (n + 1)) for n in range(4)]

    def strip(t):
        return pl.ds(pl.multiple_of(t * 32, 32), 32)

    def slot_strip(t):
        return pl.ds(pl.multiple_of(e * SLOTS + t * 32, 32), 32)

    def shares(t, _):
        share = jnp.sum(jnp.where(hits(r, at, e, t), r.shares_row[row, :], 0.0), axis=-1, keepdims=True)
        r.share[pl.ds(pl.multiple_of(t * TOK, TOK), TOK), :] = share
        return 0

    pick_rows(r, at, e)
    lax.fori_loop(0, 3, shares, 0)
    for n in quarters:
        r.rows[:, n] = dot(r.partial[0:3].reshape(SLOTS, SEQ), r.hidden_two[:, n]).astype(LOW)
    r.wide_a[:, 0:512] = dot(r.rows[...], r.gate[e].reshape(D, 512))
    r.wide_a[:, 512:1024] = dot(r.rows[...], r.up[e].reshape(D, 512))

    def activate(t, _):
        gate_pre = r.wide_a[strip(t), 0:512]
        silu = gate_pre / (1.0 + jnp.exp(-gate_pre))
        r.product[strip(t), :] = (silu * r.wide_a[strip(t), 512:1024]).astype(LOW)
        return 0

    lax.fori_loop(0, 12, activate, 0)
    for n in quarters:
        r.made[:, n] = dot(r.product[...], r.down[e, :, :, :, n].reshape(512, 256)).astype(LOW)

    def weigh(t, _):
        upstream = r.slot_grad[slot_strip(t), :].astype(WIDE)
        made, share = r.made[strip(t), :].astype(WIDE), r.share[strip(t), :]
        r.gate_dot[strip(t), :] = jnp.sum(upstream * made, axis=-1, keepdims=True)
        r.made[strip(t), :] = (share * made).astype(LOW)
        r.route_grad[strip(t), :] = (share * upstream).astype(LOW)
        return 0

    lax.fori_loop(0, 12, weigh, 0)
    keep = pltpu.make_async_copy(r.made, r.made_far.at[here], r.load.at[3])
    keep.start()
    r.wide_b[:, 0:512] = tail_dot(r.route_grad[...], r.down[e].reshape(512, D))
    for n in quarters:
        down_grad = lead_dot(r.product[...], r.route_grad[:, n])
        r.down[e, :, :, :, n] = down_grad.astype(LOW).reshape(4, 4, 32, 256)

    def activate_back(t, _):
        gate_pre, product_grad = r.wide_a[strip(t), 0:512], r.wide_b[strip(t), 0:512]
        sigmoid = 1.0 / (1.0 + jnp.exp(-gate_pre))
        slope = sigmoid * (1.0 + gate_pre * (1.0 - sigmoid))
        r.gate_low[strip(t), :] = (product_grad * r.wide_a[strip(t), 512:1024] * slope).astype(LOW)
        r.up_low[strip(t), :] = (product_grad * (gate_pre * sigmoid)).astype(LOW)
        return 0

    lax.fori_loop(0, 12, activate_back, 0)
    for m, n in enumerate(quarters):
        slot_grad = tail_dot(r.gate_low[...], r.gate[e, m].reshape(256, 512)) + tail_dot(
            r.up_low[...], r.up[e, m].reshape(256, 512)
        )
        r.slot_grad[here, n] = slot_grad.astype(LOW)
        r.gate[e, m] = lead_dot(r.rows[:, n], r.gate_low[...]).astype(LOW).reshape(4, 64, 512)
        r.up[e, m] = lead_dot(r.rows[:, n], r.up_low[...]).astype(LOW).reshape(4, 64, 512)

    def gate_rows(t, total):
        grads = r.gate_dot[pl.ds(pl.multiple_of(t * TOK, TOK), TOK), :]
        return total + jnp.sum(jnp.where(hits(r, at, e, t), grads, 0.0), axis=0, keepdims=True)

    gate_row = lax.fori_loop(0, 3, gate_rows, jnp.zeros((1, SEQ), WIDE))
    for b in range(8):
        r.gate_grad[b, pl.ds(e, 1), :] = gate_row[:, TOK * b : TOK * (b + 1)]
    keep.wait()


def expert_sums(r, at, e):
    left, right = pl.ds(0, 512), pl.ds(512, 512)
    made = []
    for n, (source, x_first, height) in enumerate(
        (
            (r.gate.at[e], True, 64),
            (r.up.at[e], False, 64),
            (r.down.at[e, :, :, :, left], True, 32),
            (r.down.at[e, :, :, :, right], False, 32),
        )
    ):
        ways = [
            (r.wide_ways if n < 2 else r.half_ways)[k].at[e, n % 2] for k in range(4)
        ]
        made.append(SumXY(at, source, ways, r.e_sent.at[e, n], r.e_got.at[e, n], x_first, height))
    return made


def back(r, attended):
    at = place()
    r.wide_ways = (r.wide1, r.wide2, r.wide3, r.wide4)
    r.half_ways = (r.half1, r.half2, r.half3, r.half4)
    r.gate_grad[...] = jnp.zeros((8, 8, 128), WIDE)
    share_tokens(r, at)

    def sums(e, name):
        for unit in expert_sums(r, at, e):
            getattr(unit, name)()

    def one(e, _):
        expert(r, at, e)
        sums(e, "step1")

        @pl.when(e > 0)
        def _():
            sums(e - 1, "step2")

        return 0

    lax.fori_loop(0, 4, one, 0)

    def share_out(source, target, sent, got_sems):
        copies = []
        for step in range(1, 8):
            other = plus(at.j, step, 8)
            copies.append(send(source(other), target, sent.at[step], got_sems.at[step], (at.i, other)))
        return copies

    gate_copies = share_out(lambda b: r.gate_grad.at[b], r.gate_back.at[at.j], r.c_sent, r.c_got)
    r.gate_back[pl.ds(at.j, 1)] = r.gate_grad[pl.ds(at.j, 1)]

    def two_blocks(ref, a, b):
        return jnp.concatenate([rows(ref, a)[...], rows(ref, b)[...]], axis=0)

    hidden_sum = SumExpert(at, r, r.pair1, r.line1, r.mine1, r.s1_sent, r.s1_got)
    hidden_sum.start(lambda a, b, n: dot(two_blocks(r.places, a, b), r.slot_grad[:, n]))
    made_load = pltpu.make_async_copy(r.made_far, r.slot_grad, r.load.at[3])
    made_load.start()
    own = pl.ds(pl.multiple_of(at.j * TOK, TOK), TOK)
    r.hidden_own[...] = r.hidden_two[own, :]
    out_load = pltpu.make_async_copy(r.out_far, r.hidden_two, r.load.at[0])
    out_load.start()
    hidden_load = pltpu.make_async_copy(r.hidden_far, r.upstream, r.load.at[1])
    hidden_load.start()
    sums(3, "step2")
    attended.forward()
    for copy in gate_copies:
        copy.wait_recv()
    gate_grad = jnp.concatenate(
        [r.gate_back[b][0:4] for b in range(8)] + [jnp.zeros((96, 128), WIDE)], axis=0
    )
    gate_grad = jnp.transpose(gate_grad)
    shares = r.shares[...]
    logit_grad = shares * (gate_grad - jnp.sum(shares * gate_grad, axis=-1, keepdims=True))
    logit_grad = logit_grad.astype(LOW)
    router_grad = lead_dot(r.hidden_own[...], logit_grad)
    hidden_grad = tail_dot(logit_grad, r.router[...])
    hidden_grad = hidden_grad + hidden_sum.total()
    residual, upstream = r.residual[...], r.cotangent[...].astype(WIDE)
    inverse = lax.rsqrt(jnp.mean(residual * residual, axis=-1, keepdims=True) + EPSILON)
    gain_two_grad = jnp.sum(hidden_grad * (residual * inverse), axis=0, keepdims=True)
    scaled = hidden_grad * r.gains[1:2, :]
    mean = jnp.mean(scaled * residual, axis=-1, keepdims=True)
    residual_grad = upstream + scaled * inverse - residual * (inverse * inverse * inverse * mean)
    r.residual_grad[...] = residual_grad
    r.branch[...] = residual_grad.astype(LOW)
    branch_copies = share_out(lambda b: columns(r.branch, b), rows(r.branch_part, at.j), r.b_sent, r.b_got)
    out_load.wait()
    for n in range(4):
        part = slice(256 * n, 256 * (n + 1))
        r.attended_grad[:, part] = tail_dot(r.branch[...], r.hidden_two[part, :]).astype(LOW)
    grad_copies = share_out(
        lambda b: columns(r.attended_grad, b), rows(r.attended_back, at.j), r.d_sent, r.d_got
    )
    rows(r.branch_part, at.j)[...] = columns(r.branch, at.j)[...]
    rows(r.attended_back, at.j)[...] = columns(r.attended_grad, at.j)[...]
    hidden_sum.sent_all()

    output_sum = SumExpert(at, r, r.pair2, r.line2, r.mine2, r.s2_sent, r.s2_got)
    made_load.wait()
    output_sum.start(lambda a, b, n: dot(two_blocks(r.places, a, b), r.slot_grad[:, n]))
    sums(0, "step3")
    sums(1, "step3")
    for copy in grad_copies:
        copy.wait_recv()

    low_lanes = lanes((TOK, 128)) < 64
    r.key_grad[...] = jnp.zeros((SEQ, 128), WIDE)
    r.value_grad[...] = jnp.zeros((SEQ, 128), WIDE)
    for b in range(8):
        length, here = TOK * (b + 1), slice(TOK * b, TOK * (b + 1))
        both = both_heads(r.queries[here, :], low_lanes)
        both_grad = both_heads(r.attended_back[here, :], low_lanes)
        r.wide_a[0:256, 0:length] = tail_dot(both, r.keys[0:length, :])
        r.wide_b[0:256, 0:length] = tail_dot(both_grad, r.values[0:length, :])
        for head in range(2):

            def strip(t, _):
                token = pl.ds(pl.multiple_of(TOK * b + 16 * t, 16), 16)
                line = pl.ds(pl.multiple_of(TOK * head + 16 * t, 16), 16)
                allowed = allowed_keys(r, token, TOK * b + 16 * t, length)
                powers = jnp.exp(r.wide_a[line, 0:length] * SCALE - r.log_total[token, head : head + 1])
                probs = jnp.where(allowed, powers, 0.0)
                prob_grad = r.wide_b[line, 0:length]
                inner = jnp.sum(probs * prob_grad, axis=-1, keepdims=True)
                r.rows[line, 0:length] = (probs * (prob_grad - inner)).astype(LOW)
                r.route_grad[line, 0:length] = probs.astype(LOW)
                return 0

            lax.fori_loop(0, 8, strip, 0, unroll=2)
        score_grad, probs = r.rows[0:256, 0:length], r.route_grad[0:256, 0:length]
        query_grad = dot(score_grad, r.keys[0:length, :]) * SCALE
        query_grad = jnp.where(low_lanes, query_grad[0:TOK], query_grad[TOK:])
        cosine, sine = angles(r, here, (TOK, 128))
        r.qkv_grad[here, 0:128] = turn(query_grad, cosine, -sine).astype(LOW)
        r.key_grad[0:length, :] += lead_dot(score_grad, both)
        r.value_grad[0:length, :] += lead_dot(probs, both_grad)
        if b == 4:
            sums(2, "step3")
            sums(0, "step4")
        if b == 6:
            sums(1, "step4")

    def finish_keys(b, _):
        here = pl.ds(pl.multiple_of(b * TOK, TOK), TOK)
        key_grad, value_grad = r.key_grad[here, :], r.value_grad[here, :]
        key_grad = (key_grad + pltpu.roll(key_grad, 64, axis=1)) * SCALE
        value_grad = value_grad + pltpu.roll(value_grad, 64, axis=1)
        cosine, sine = angles(r, here, (TOK, 128))
        key_grad = turn(key_grad, cosine, -sine)
        r.qkv_grad[here, 128:256] = jnp.where(low_lanes, key_grad, value_grad).astype(LOW)
        return 0

    lax.fori_loop(0, 8, finish_keys, 0)

    output_sum.sent_all()
    r.gain_sum[...] = jnp.zeros((8, D), WIDE)

    hidden_load.wait()

    def hidden_one_tile(a, b, n):
        made = tail_dot(two_blocks(r.qkv_grad, a, b), r.w_qkv[n, :])
        hidden = jnp.concatenate([rows(r.upstream, k).at[:, n][...] for k in (a, b)], axis=0)
        r.gain_sum[0:1, n] += jnp.sum(made * hidden.astype(WIDE), axis=0, keepdims=True)
        return made

    input_sum = SumExpert(at, r, r.pair3, r.line3, r.mine1, r.s3_sent, r.s3_got)
    input_sum.start(hidden_one_tile)

    for copy in branch_copies:
        copy.wait()
    attended.finish()
    gain_rows = jnp.concatenate(
        [
            jnp.zeros((32, D), WIDE), r.gain_sum[0:1, :] / r.gains[0:1, :], gain_two_grad, jnp.zeros((94, D), WIDE),
        ],
        axis=0,
    )
    for m in range(4):
        here = slice(256 * m, 256 * (m + 1))
        grads = lead_dot(r.upstream[:, here], r.qkv_grad[...]).astype(LOW)
        out_grads = lead_dot(r.attended_all[:, here], r.branch_part[...]).astype(LOW)
        others = [jnp.transpose(gain_rows[:, 256 * m + 128 * t : 256 * m + 128 * (t + 1)]) for t in range(2)]
        others = (router_grad[here] + jnp.concatenate(others, axis=0)).astype(LOW)
        for x in range(4):
            part = slice(64 * x, 64 * (x + 1))
            r.dense[0, m, x, 0:64] = grads[part, 0:128]
            r.dense[0, m, x, 64:128] = grads[part, 128:256]
            r.dense[1, m, x, 0:64] = out_grads[part]
            r.dense[1, m, x, 64:128] = others[part]
    dense_sums = [
        SumXY(
            at, r.dense.at[n], [r.dense1.at[n], r.dense2.at[n], r.dense3.at[n], r.dense4.at[n]],
            r.f_sent.at[n], r.f_got.at[n], n == 0, 128,
        )
        for n in range(2)
    ]
    for unit in dense_sums:
        unit.step1()
    sums(3, "step3")
    sums(2, "step4")
    for unit in dense_sums:
        unit.step2()

    def stores(e):
        high = pl.ds(pl.multiple_of(e * 64, 64), 64)
        low = pl.ds(pl.multiple_of(e * 32, 32), 32)
        return [
            pltpu.make_async_copy(r.wide_a.at[high, 0:512], r.gate_out.at[e], r.store.at[e, 0]),
            pltpu.make_async_copy(r.wide_a.at[high, 512:1024], r.up_out.at[e], r.store.at[e, 1]),
            pltpu.make_async_copy(r.wide_b.at[low], r.down_out.at[e], r.store.at[e, 2]),
        ]

    def finish_expert(e, _):
        gate, up, left, right = expert_sums(r, at, e)
        high = pl.ds(pl.multiple_of(e * 64, 64), 64)
        r.wide_a[high, 0:512] = gate.step5()
        r.wide_a[high, 512:1024] = up.step5()
        low = pl.ds(pl.multiple_of(e * 32, 32), 32)
        r.wide_b[low, 0:512] = left.step5()
        r.wide_b[low, 512:1024] = right.step5()
        for copy in stores(e):
            copy.start()
        return 0

    lax.fori_loop(0, 3, finish_expert, 0)
    sums(3, "step4")
    for unit in dense_sums:
        unit.step3()
    r.branch[...] = (r.residual[...] + output_sum.total()).astype(LOW)
    output_store = pltpu.make_async_copy(r.branch, r.output, r.load.at[0])
    output_store.start()
    finish_expert(3, 0)
    for unit in dense_sums:
        unit.step4()

    hidden_grad = input_sum.total()
    inputs = r.tokens[...].astype(WIDE)
    inverse = lax.rsqrt(jnp.mean(inputs * inputs, axis=-1, keepdims=True) + EPSILON)
    scaled = hidden_grad * r.gains[0:1, :]
    mean = jnp.mean(scaled * inputs, axis=-1, keepdims=True)
    r.residual_grad[...] = (
        r.residual_grad[...] + scaled * inverse - inputs * (inverse * inverse * inverse * mean)
    )
    input_store = pltpu.make_async_copy(r.residual_grad, r.input_grad, r.load.at[1])
    input_store.start()
    for n, unit in enumerate(dense_sums):
        r.dense_total[n] = unit.step5().reshape(2, 8, 8, 128)
    last_copies = share_out(lambda b: r.dense_total.at[:, :, b], r.dense_back.at[at.j], r.l_sent, r.l_got)
    r.dense_back[pl.ds(at.j, 1)] = r.dense_total[:, :, pl.ds(at.j, 1)].reshape(1, 2, 2, 8, 128)
    for copy in last_copies:
        copy.wait_recv()
    low_lanes = lanes((8, 128)) < 64
    others = jnp.zeros((8, 128), WIDE)
    for b in range(8):
        head = slice(128 * b, 128 * (b + 1))
        r.query_out[:, head] = r.dense_back[b, 0, 0]
        r.out_out[:, head] = r.dense_back[b, 1, 0]
        others = others + r.dense_back[b, 1, 1]
    for t in range(4):
        head = slice(128 * t, 128 * (t + 1))
        even, odd = r.dense_back[2 * t, 0, 1], r.dense_back[2 * t + 1, 0, 1]
        r.key_out[:, head] = jnp.where(low_lanes, even, pltpu.roll(odd, 64, axis=1))
        r.value_out[:, head] = jnp.where(low_lanes, pltpu.roll(even, 64, axis=1), odd)
    r.others_out[...] = others

    input_sum.sent_all()
    for copy in gate_copies + grad_copies + last_copies:
        copy.wait_send()
    output_store.wait()
    input_store.wait()

    def ended(e, _):
        for copy in stores(e):
            copy.wait()
        for unit in expert_sums(r, at, e):
            unit.finish()
        return 0

    lax.fori_loop(0, 4, ended, 0)
    for unit in dense_sums:
        unit.finish()

DMA = pltpu.SemaphoreType.DMA


def low(*shape):
    return pltpu.VMEM(shape, LOW)


def wide(*shape):
    return pltpu.VMEM(shape, WIDE)


def far(*shape, kind=WIDE):
    return pltpu.HBM(shape, kind)


OUTS = dict(
    output=far(TOK, D, kind=LOW), input_grad=far(TOK, D), query_out=wide(8, D), key_out=wide(8, 512),
    value_out=wide(8, 512), out_out=wide(8, D), others_out=wide(8, 128), gate_out=far(4, 64, 512),
    up_out=far(4, 64, 512), down_out=far(4, 32, D), made_far=far(4 * SLOTS, D, kind=LOW),
    hidden_far=far(SEQ, D, kind=LOW), out_far=far(D, D, kind=LOW),
)
SCRATCH = dict(
    w_qkv=low(D, 256), router=low(D, 128), gains=wide(8, D), queries=low(SEQ, 128), keys=low(SEQ, 128),
    values=low(SEQ, 128), log_total=wide(SEQ, 128), attended=low(TOK, D), residual=wide(TOK, D),
    hidden_two=low(SEQ, D), upstream=low(SEQ, D), named=low(SEQ, 128), seg_col=wide(SEQ, 1),
    pack=low(8, 32, 128), stage=low(2, 128, 128),
    gate=low(4, 4, 4, 64, 512), up=low(4, 4, 4, 64, 512), down=low(4, 4, 4, 32, D),
    shares=wide(TOK, 128), shares_row=wide(32, SEQ), order_row=wide(32, SEQ), places=low(SEQ, 4 * SLOTS),
    rows=low(SLOTS, D), route_grad=low(SLOTS, D), made=low(SLOTS, D), slot_grad=low(4 * SLOTS, D),
    gate_grad=wide(8, 8, 128), gate_back=wide(8, 8, 128), wide_a=wide(SLOTS, D), wide_b=wide(SLOTS, D),
    product=low(SLOTS, 512), gate_low=low(SLOTS, 512), up_low=low(SLOTS, 512), share=wide(SLOTS, 1),
    gate_dot=wide(SLOTS, 1), hidden_own=low(TOK, D),
    wide1=low(4, 2, 2, 2, 64, 512), wide2=low(4, 2, 2, 4, 64, 512), wide3=low(4, 2, 2, 32, 512),
    wide4=low(4, 2, 2, 64, 512), half1=low(4, 2, 2, 2, 32, 512), half2=low(4, 2, 2, 4, 32, 512),
    half3=low(4, 2, 2, 16, 512), half4=low(4, 2, 2, 32, 512), dense=low(2, 4, 4, 128, 128),
    dense1=low(2, 2, 2, 128, 128), dense2=low(2, 2, 4, 128, 128), dense3=low(2, 2, 64, 128),
    dense4=low(2, 2, 128, 128), dense_total=wide(2, 2, 8, 8, 128), dense_back=wide(8, 2, 2, 8, 128),
    partial=low(7, TOK, D), pair1=low(4, TOK, D), line1=low(3, TOK, D), mine1=wide(TOK, D),
    pair2=low(4, TOK, D), line2=low(3, TOK, D), mine2=wide(TOK, D), pair3=low(4, TOK, D), line3=low(3, TOK, D),
    residual_grad=wide(TOK, D), branch=low(TOK, D), branch_part=low(SEQ, 128), attended_grad=low(TOK, D),
    attended_back=low(SEQ, 128), attended_all=low(SEQ, D), key_grad=wide(SEQ, 128), value_grad=wide(SEQ, 128),
    qkv_grad=low(SEQ, 256), gain_sum=wide(8, D),
    x_sent=DMA((7,)), x_got=DMA((7,)), n_sent=DMA((7,)), n_got=DMA((7,)), g_sent=DMA((7,)), g_got=DMA((7,)),
    o_sent=DMA((7,)), o_got=DMA((7,)), h_sent=DMA((7,)), h_got=DMA((7,)), t_sent=DMA((7,)), t_got=DMA((7,)),
    p_sent=DMA((8,)), p_got=DMA((8,)), w_sent=DMA((16,)), w_got=DMA((16,)), a_sent=DMA((8,)), a_got=DMA((8,)),
    e_sent=DMA((4, 4, 8)), e_got=DMA((4, 4, 8)), f_sent=DMA((2, 8)), f_got=DMA((2, 8)), c_sent=DMA((8,)),
    c_got=DMA((8,)), b_sent=DMA((8,)), b_got=DMA((8,)), d_sent=DMA((8,)), d_got=DMA((8,)), l_sent=DMA((8,)),
    l_got=DMA((8,)), s1_sent=DMA((7,)), s1_got=DMA((7,)), s2_sent=DMA((7,)), s2_got=DMA((7,)),
    s3_sent=DMA((7,)), s3_got=DMA((7,)), load=DMA((5,)), store=DMA((4, 3)),
)


def is_far(name):
    return name in OUTS and OUTS[name].memory_space != pltpu.VMEM or name in ("gate_in", "up_in", "down_in")


def spec(name):
    return pl.BlockSpec(memory_space=pl.ANY if is_far(name) else pltpu.VMEM)


def layer(**arrays):
    names = list(arrays) + list(OUTS) + list(SCRATCH)

    def kernel(*refs):
        r = SimpleNamespace(**dict(zip(names, refs)))
        r.hidden_one, r.w_out_all = r.slot_grad.at[0:SEQ], r.places.at[:, 0:D]
        r.scores, r.probs = r.wide_a.at[0:256], r.rows.at[0:256]
        r.w_out_part, r.attended_head = r.qkv_grad.at[:, 0:128], r.qkv_grad.at[:, 128:256]
        r.extra_all = r.key_grad
        back(r, front(r))

    outs = pl.pallas_call(
        kernel,
        out_shape=[jax.ShapeDtypeStruct(OUTS[n].shape, OUTS[n].dtype) for n in OUTS],
        in_specs=[spec(n) for n in arrays],
        out_specs=[spec(n) for n in OUTS],
        scratch_shapes=list(SCRATCH.values()),
        name="layer",
        compiler_params=pltpu.CompilerParams(
            collective_id=0, has_side_effects=True, vmem_limit_bytes=510 << 17
        ),
    )(*arrays.values())
    return dict(zip(OUTS, outs))


def hand_on(*refs):
    come, go = refs[-2:]
    loads = [pltpu.make_async_copy(refs[n], refs[18 + n], come.at[n]) for n in range(9)]
    stores = [pltpu.make_async_copy(refs[18 + n], refs[9 + n], go.at[n]) for n in range(9)]
    for copy in loads:
        copy.start()
    for load, store in zip(loads, stores):
        load.wait()
        store.start()
    for copy in stores:
        copy.wait()


def handed_on(*arrays):
    return pl.pallas_call(
        hand_on,
        out_shape=[jax.ShapeDtypeStruct(a.shape, a.dtype) for a in arrays],
        in_specs=[pl.BlockSpec(memory_space=pl.ANY)] * 9,
        out_specs=[pl.BlockSpec(memory_space=pl.ANY)] * 9,
        scratch_shapes=[pltpu.VMEM(a.shape, a.dtype) for a in arrays] + [DMA((9,)), DMA((9,))],
        name="hand_on",
    )(*arrays)


def shards(
    tokens, segments, routes, gain_attn, gain_ffn, w_query, w_key, w_value, w_out, w_router, w_gate, w_up,
    w_down, cotangent,
):
    extra = jnp.concatenate(
        [w_router, gain_attn[:, None], gain_ffn[:, None], jnp.zeros((8, 94), LOW)], axis=1
    ).astype(WIDE)
    angle = np.arange(SEQ, dtype=np.float32)[:, None] * (
        np.float32(10000.0) ** (-np.arange(32, dtype=np.float32) / np.float32(32))
    )
    waves = np.concatenate([np.cos(angle), np.cos(angle), -np.sin(angle), np.sin(angle)], axis=1)
    made = layer(
        tokens=tokens, routes=routes.T, w_query=w_query, w_key=w_key, w_value=w_value, w_out=w_out,
        extra=extra, seg_row=segments, table=jnp.asarray(waves.astype(np.float32)), cotangent=cotangent,
        gate_in=w_gate.reshape(4, 4, 4, 64, 512), up_in=w_up.reshape(4, 4, 4, 64, 512),
        down_in=w_down.reshape(4, 4, 4, 32, D),
    )
    others = made["others_out"]
    output, input_grad, query, key, value, out, gate, up, down = handed_on(
        made["output"], made["input_grad"], made["query_out"], made["key_out"], made["value_out"],
        made["out_out"], made["gate_out"], made["up_out"], made["down_out"],
    )
    return (
        output, input_grad, others[:, 32], others[:, 33], query, key, value, out, others[:, 0:32], gate, up, down,
    )


def solution(mesh):
    line, dense = P(("dp", "expert")), P(("dp", "expert"), None)
    copied, summed = P("expert", None, None), P("expert", "dp", None)
    return jax.shard_map(
        shards,
        mesh=mesh,
        in_specs=(dense, P("dp", None), dense, line, line) + (dense,) * 5 + (copied,) * 3 + (dense,),
        out_specs=(dense, dense, line, line) + (dense,) * 5 + (summed,) * 3,
        check_vma=False,
    )
```

```python
import functools
from types import SimpleNamespace

import jax
import jax.numpy as jnp
import numpy as np
from jax import lax
from jax.experimental import pallas as pl
from jax.experimental.pallas import tpu as pltpu
from jax.sharding import PartitionSpec as P

MESH = pl.DeviceIdType.MESH
LOW, WIDE = jnp.bfloat16, jnp.float32
EPSILON = 1e-06
SCALE = 64 ** (-0.5)
TOK, SEQ, D, SLOTS = 128, 1024, 1024, 384
Z_STEPS = (2, 1, 3)


def dot(one, two):
    return lax.dot_general(one, two, (((1,), (0,)), ((), ())), preferred_element_type=WIDE)


def tail_dot(one, two):
    return lax.dot_general(one, two, (((1,), (1,)), ((), ())), preferred_element_type=WIDE)


def lead_dot(one, two):
    return lax.dot_general(one, two, (((0,), (0,)), ((), ())), preferred_element_type=WIDE)


def place():
    i, j = lax.axis_index("dp"), lax.axis_index("expert")
    at = SimpleNamespace(i=i, j=j, x=lax.rem(i, 4), y=lax.div(i, 4), z=lax.div(j, 2), c=lax.rem(j, 2))
    at.sibling = (i, at.z * 2 + 1 - at.c)
    return at


def plus(value, step, size):
    return lax.rem(value + step, size)


def z_peer(at, step):
    return (at.i, plus(at.z, step, 4) * 2 + at.c)


def xy_peer(at, x_step, y_step):
    return (plus(at.y, y_step, 4) * 4 + plus(at.x, x_step, 4), at.j)


def send(source, target, sent, got, device):
    copy = pltpu.make_async_remote_copy(
        src_ref=source, dst_ref=target, send_sem=sent, recv_sem=got, device_id=device, device_id_type=MESH
    )
    copy.start()
    return copy


def rows(ref, block, size=TOK):
    return ref.at[pl.ds(pl.multiple_of(block * size, size), size)]


def columns(ref, block, size=128):
    return ref.at[:, pl.ds(pl.multiple_of(block * size, size), size)]


def got(ref, semaphore, at):
    pltpu.make_async_remote_copy(
        src_ref=ref, dst_ref=ref, send_sem=semaphore, recv_sem=semaphore, device_id=at.sibling, device_id_type=MESH
    ).wait_recv()


def gone(ref, semaphore, at):
    pltpu.make_async_remote_copy(
        src_ref=ref, dst_ref=ref, send_sem=semaphore, recv_sem=semaphore, device_id=at.sibling, device_id_type=MESH
    ).wait_send()


class Gather:
    def __init__(self, at, source, target, sems):
        self.at, self.source, self.target, self.sems = at, source, target, sems

    def start(self):
        at, mine = self.at, rows(self.target, self.at.j)
        for k, step in enumerate(Z_STEPS):
            send(self.source, mine, self.sems.at[0], self.sems.at[1 + k], z_peer(at, step))
        send(self.source, mine, self.sems.at[0], self.sems.at[4], at.sibling)

    def forward(self):
        at = self.at
        for k, step in enumerate(Z_STEPS):
            block = rows(self.target, plus(at.z, 4 - step, 4) * 2 + at.c)
            got(block, self.sems.at[1 + k], at)
            send(block, block, self.sems.at[0], self.sems.at[4], at.sibling)

    def finish(self):
        got(self.target.at[0 : 4 * TOK], self.sems.at[4], self.at)
        gone(self.target.at[0 : 7 * TOK], self.sems.at[0], self.at)


class Shares:
    def __init__(self, at, source, target, seven, sems):
        self.at, self.seven, self.sems = at, seven, sems
        for step in range(1, 8):
            other = plus(at.j, step, 8)
            send(source(other), target, sems.at[0], sems.at[1], (at.i, other))

    def wait_recv(self):
        got(self.seven, self.sems.at[1], self.at)

    def wait_send(self):
        gone(self.seven, self.sems.at[0], self.at)


class Spread:
    def __init__(self, at, source, target, four, three, sems):
        self.at, self.four, self.three, self.sems = at, four, three, sems
        for step in range(1, 16):
            y = step // 4
            send(source, target, sems.at[0, y], sems.at[1, y], xy_peer(at, step % 4, y))

    def wait_recv(self):
        got(self.three, self.sems.at[1, 0], self.at)
        for step in range(1, 4):
            got(self.four(plus(self.at.y, 4 - step, 4)), self.sems.at[1, step], self.at)

    def wait_send(self):
        gone(self.three, self.sems.at[0, 0], self.at)
        for step in range(1, 4):
            gone(self.four(plus(self.at.y, 4 - step, 4)), self.sems.at[0, step], self.at)


def greet(devices):
    barrier = pltpu.get_barrier_semaphore()
    for device in devices:
        pl.semaphore_signal(barrier, inc=1, device_id=device, device_id_type=MESH)
    return lambda: pl.semaphore_wait(barrier, len(devices))


def expert_peers(at):
    return [(at.i, plus(at.j, step, 8)) for step in range(1, 8)]


def dp_peers(at):
    return [xy_peer(at, step % 4, step // 4) for step in range(1, 16)]


def lanes(shape):
    return lax.broadcasted_iota(jnp.int32, shape, len(shape) - 1)


def turn(values, cosine, signed_sine):
    lane = lanes(values.shape)
    swapped = jnp.where(
        lane % 64 < 32, pltpu.roll(values, 96, axis=1), pltpu.roll(values, 32, axis=1)
    )
    return values * cosine + swapped * signed_sine


def angles(r, here, shape):
    table = r.table[here, :]
    other, low_lanes = pltpu.roll(table, 64, axis=1), lanes(shape) < 64
    return jnp.where(low_lanes, table, other), jnp.where(low_lanes, other, table)


def allowed(r, b, c):
    keep = None
    if c == 0 or b == 3:
        keep = r.log_total[256 * b : 256 * (b + 1), 2:3] == r.seg_row[:, 256 * c : 256 * (c + 1)].astype(WIDE)
    if b == c:
        below = lanes((256, 256)) <= lax.broadcasted_iota(jnp.int32, (256, 256), 0)
        keep = below if keep is None else keep & below
    return keep


def one_head(values, head):
    return jnp.where((lanes(values.shape) < 64) == (head == 0), values, jnp.zeros_like(values))


def front(r):
    at = place()
    ready = greet(expert_peers(at) + dp_peers(at))

    query_w, key_w = r.w_query[...].astype(WIDE), r.w_key[...].astype(WIDE)
    value_w = r.w_value[...].astype(WIDE)
    low_lanes = lanes((8, 128)) < 64
    for j in range(8):
        tile = slice(128 * (j // 2), 128 * (j // 2) + 128)
        key_part, value_part = key_w[:, tile], value_w[:, tile]
        if j % 2:
            key_part = pltpu.roll(key_part, 64, axis=1)
        else:
            value_part = pltpu.roll(value_part, 64, axis=1)
        head = slice(128 * j, 128 * j + 128)
        r.pack[j] = jnp.concatenate(
            [query_w[:, head], jnp.where(low_lanes, key_part, value_part), r.extra[...]], axis=0
        )
    r.out_mine[...] = r.w_out[...].astype(WIDE)
    r.near[at.j] = r.pack[at.j]
    expert = lax.broadcasted_iota(jnp.int32, (128, TOK), 0)
    named = jnp.zeros((128, TOK), WIDE)
    for k in range(8):
        named = named + jnp.where(r.routes[k : k + 1, :] == expert, 1.0, 0.0)
    rows(r.named, at.j)[...] = jnp.transpose(named).astype(LOW)
    rows(r.hidden_one, at.j)[...] = r.tokens[...]
    for b in range(8):
        here = slice(TOK * b, TOK * (b + 1))
        across = jnp.broadcast_to(r.seg_row[:, here].astype(WIDE), (TOK, TOK))
        r.log_total[here, :] = jnp.transpose(across)

    ready()
    pair = send(r.out_mine, r.out_other, r.q_sems.at[0], r.q_sems.at[1], at.sibling)
    first = Shares(at, lambda b: r.pack.at[b], r.near.at[at.j], r.near.at[0:7], r.p_sems)
    tokens = Gather(at, r.tokens, r.hidden_one, r.x_sems)
    tokens.start()
    pair.wait_recv()
    mine, other = r.out_mine[...], r.out_other[...]
    both = jnp.where(
        at.c == 0,
        jnp.concatenate([mine[:, 0:512], other[:, 0:512]], axis=0),
        jnp.concatenate([other[:, 512:1024], mine[:, 512:1024]], axis=0),
    )
    line = rows(r.out_rows, at.z, 16)
    line[...] = both.astype(LOW)
    for step in Z_STEPS:
        send(line, line, r.q_sems.at[2], r.q_sems.at[3], z_peer(at, step))
    marks = Gather(at, rows(r.named, at.j), r.named, r.n_sems)
    marks.start()
    loads = []
    for n, (source, target) in enumerate(((r.gate_in, r.gate), (r.up_in, r.up), (r.down_in, r.down))):
        loads.append(pltpu.make_async_copy(source, target, r.load.at[n]))
        loads[-1].start()
    first.wait_recv()
    for b in range(8):
        r.stage[16 * b : 16 * (b + 1)] = r.near[b, 0:16].astype(LOW)
    r.stage[128:192] = jnp.concatenate([r.near[b, 16:24] for b in range(8)], axis=0).astype(LOW)
    second = Spread(
        at, r.stage, r.dense.at[at.y, at.x, 0:192], lambda y: r.dense.at[y, :, 0:192], r.dense.at[0, 0:3, 0:192],
        r.w_sems,
    )
    r.dense[at.y, at.x, 0:192] = r.stage[...]
    half = pl.ds(pl.multiple_of(at.c * 512, 512), 512)
    out_half = r.w_out_all.at[pl.ds(pl.multiple_of(at.i * 64, 64), 64), half]
    got(r.out_rows.at[0:48], r.q_sems.at[3], at)
    third = Spread(
        at, r.out_rows, out_half, lambda y: r.w_out_all.at[pl.ds(pl.multiple_of(y * 256, 256), 256), half],
        r.w_out_all.at[0:192, half], r.o_sems,
    )
    out_half[...] = r.out_rows[...]
    tokens.forward()
    rows(r.upstream, at.j)[...] = r.cotangent[...]
    upstream = Gather(at, r.cotangent, r.upstream, r.g_sems)
    upstream.start()
    second.wait_recv()

    def unpack(i, _):
        part = r.dense[lax.div(i, 4), lax.rem(i, 4), 0:192].astype(WIDE)
        here = pl.ds(pl.multiple_of(i * 64, 64), 64)
        heads = part[0:128].reshape(8, 16, 128)
        r.w_qkv[here, 0:128] = heads[:, 0:8, :].reshape(64, 128).astype(LOW)
        r.w_qkv[here, 128:256] = heads[:, 8:16, :].reshape(64, 128).astype(LOW)
        r.extra_all[here, :] = part[128:192]
        return 0

    lax.fori_loop(0, 16, unpack, 0)
    r.gains[...] = extra_rows(r)
    r.router[...] = jnp.where(lanes((D, 128)) < 32, r.extra_all[...], 0.0).astype(LOW)
    tokens.finish()

    low_lanes = lanes((256, 128)) < 64

    def project(b, _):
        here = pl.ds(pl.multiple_of(b * 256, 256), 256)
        x = r.hidden_one[here, :].astype(WIDE)
        inverse = lax.rsqrt(jnp.mean(x * x, axis=-1, keepdims=True) + EPSILON)
        hidden = (x * inverse * r.gains[0:1, :]).astype(LOW)
        r.hidden_one[here, :] = hidden
        made = dot(hidden, r.w_qkv[...])
        cosine, sine = angles(r, here, (256, 128))
        r.queries[here, :] = turn(made[:, 0:128], cosine, sine).astype(LOW)
        pair = turn(
            made[:, 128:256], jnp.where(low_lanes, cosine, 1.0), jnp.where(low_lanes, sine, 0.0)
        )
        turned = pltpu.roll(pair, 64, axis=1)
        r.keys[here, :] = jnp.where(low_lanes, pair, turned).astype(LOW)
        r.values[here, :] = jnp.where(low_lanes, turned, pair).astype(LOW)
        return 0

    lax.fori_loop(0, 4, project, 0)
    marks.forward()
    hidden_save = pltpu.make_async_copy(r.hidden_one, r.hidden_far, r.load.at[3])
    hidden_save.start()

    low_lanes = lanes((256, 128)) < 64
    scores = (r.wide_a, r.wide_b)
    for b in range(4):
        here = slice(256 * b, 256 * (b + 1))
        logs, heads = [], []
        for head in range(2):
            query = one_head(r.queries[here, :], head) * SCALE
            top = jnp.full((256, 256), -1e30, WIDE)
            for c in range(b + 1):
                part = slice(256 * c, 256 * (c + 1))
                score, keep = tail_dot(query, r.keys[part, :]), allowed(r, b, c)
                if keep is not None:
                    score = jnp.where(keep, score, -1e30)
                scores[head][0:256, part] = score
                top = jnp.maximum(top, score)
            top = jnp.max(top, axis=-1, keepdims=True)
            mixed = jnp.zeros((256, 128), WIDE)
            for c in range(b + 1):
                part = slice(256 * c, 256 * (c + 1))
                powers = jnp.exp(scores[head][0:256, part] - top).astype(LOW)
                value = r.values[part, :]
                mixed = mixed + dot(powers, jnp.where(low_lanes == (head == 0), value, jnp.ones_like(value)))
            total = mixed[:, 64:65] if head == 0 else mixed[:, 0:1]
            heads.append(mixed / total)
            logs.append(top + jnp.log(total))
        r.attended_head[here, :] = jnp.where(low_lanes, heads[0], heads[1]).astype(LOW)
        lane = lanes((256, 128))
        r.log_total[here, :] = jnp.where(
            lane == 0, logs[0], jnp.where(lane == 1, logs[1], r.log_total[here, :])
        )
        for n in (2 * b, 2 * b + 1):

            @pl.when(at.j != n)
            def _():
                send(
                    r.attended_head.at[TOK * n : TOK * (n + 1)], columns(r.attended, at.j), r.a_sems.at[0],
                    r.a_sems.at[1], (at.i, jnp.int32(n)),
                )

            @pl.when(at.j == n)
            def _():
                columns(r.attended, at.j)[...] = r.attended_head[TOK * n : TOK * (n + 1), :]

    third.wait_recv()
    out_mine = columns(r.w_out_all, at.c, 512)
    whole = send(out_mine, out_mine, r.q_sems.at[4], r.q_sems.at[5], at.sibling)
    upstream.forward()
    got(r.attended.at[:, 0 : 7 * 128], r.a_sems.at[1], at)
    whole.wait_recv()

    residual = r.tokens[...].astype(WIDE) + dot(r.attended[...], r.w_out_all[...])
    r.residual[...] = residual
    inverse = lax.rsqrt(jnp.mean(residual * residual, axis=-1, keepdims=True) + EPSILON)
    rows(r.hidden_two, at.j)[...] = (residual * inverse * r.gains[1:2, :]).astype(LOW)
    hidden = Gather(at, rows(r.hidden_two, at.j), r.hidden_two, r.h_sems)
    hidden.start()
    out_save = pltpu.make_async_copy(r.w_out_all, r.out_far, r.load.at[4])
    out_save.start()
    attended = Gather(at, r.attended, r.attended_all, r.t_sems)
    rows(r.attended_all, at.j)[...] = r.attended[...]
    for copy in (first, second, third, pair, whole):
        copy.wait_send()
    gone(r.out_rows.at[0:48], r.q_sems.at[2], at)
    gone(r.attended_head.at[0 : 7 * TOK], r.a_sems.at[0], at)
    upstream.finish()
    marks.finish()
    hidden_save.wait()
    out_save.wait()
    order_tokens(r, at)
    for copy in loads:
        copy.wait()
    lax.fori_loop(0, 4, lambda e, _: pick_upstream(r, at, e), 0)
    hidden.forward()
    hidden.finish()
    attended.start()
    return attended


def extra_rows(r):
    picked = [jnp.transpose(r.extra_all[TOK * b : TOK * (b + 1), :])[32:40, :] for b in range(8)]
    return jnp.concatenate(picked, axis=1)


class SumXY:
    def __init__(self, at, sources, ways, sems, height):
        self.at, self.sources, self.ways, self.sems, self.height = at, sources, ways, sems, height

    def place(self, n):
        return (self.at.x, self.at.y) if n == 0 else (self.at.y, self.at.x)

    def block(self, n, first, second):
        return self.sources[n].at[second, first] if n == 0 else self.sources[n].at[first, second]

    def out(self, n, k, way, ref, second, step):
        device = xy_peer(self.at, step, 0) if (n == 0) != second else xy_peer(self.at, 0, step)
        send(ref, self.ways[k].at[n, way], self.sems.at[k, 0], self.sems.at[k, 1], device)

    def take(self, k):
        got(self.ways[k], self.sems.at[k, 1], self.at)

    def step1(self):
        for n in range(2):
            far = plus(self.place(n)[0], 2, 4)
            self.out(n, 0, 0, self.block(n, far, pl.ds(0, 2)), False, 1)
            self.out(n, 0, 1, self.block(n, far, pl.ds(2, 2)), False, 3)

    def step2(self):
        self.take(0)
        for n in range(2):
            for k, step in enumerate((1, 3)):
                near = plus(self.place(n)[0], step, 4)
                part = self.block(n, near, pl.ds(2 * k, 2))
                part[...] = part[...] + self.ways[0][n, k]
                self.out(n, 1, k, self.block(n, near, pl.ds(0, 4)), False, step)

    def step3(self):
        self.take(1)
        half = self.height // 2
        for n in range(2):
            first, second = self.place(n)
            mine = self.block(n, first, pl.ds(0, 4))
            mine[...] = mine[...] + (self.ways[1][n, 0] + self.ways[1][n, 1])
            far = self.block(n, first, plus(second, 2, 4))
            self.out(n, 2, 0, far.at[pl.ds(0, half)], True, 1)
            self.out(n, 2, 1, far.at[pl.ds(half, half)], True, 3)

    def step4(self):
        self.take(2)
        half = self.height // 2
        for n in range(2):
            first, second = self.place(n)
            for k, step in enumerate((1, 3)):
                near = self.block(n, first, plus(second, step, 4))
                part = near.at[pl.ds(half * k, half)]
                part[...] = part[...] + self.ways[2][n, k]
                self.out(n, 3, k, near, True, step)

    def step5(self):
        self.take(3)
        totals = []
        for n in range(2):
            mine = self.block(n, *self.place(n))[...].astype(WIDE)
            totals.append(mine + self.ways[3][n, 0].astype(WIDE) + self.ways[3][n, 1].astype(WIDE))
        return totals

    def finish(self):
        for k in range(4):
            gone(self.ways[k], self.sems.at[k, 0], self.at)


class SumExpert:
    def __init__(self, at, r, pair_in, line_in, mine, sems):
        self.at, self.r, self.pair_in, self.line_in, self.mine, self.sems = at, r, pair_in, line_in, mine, sems

    def start(self, tiles):
        at, partial = self.at, self.r.partial

        def to_sibling(p, _):
            steps = (2 + p, 1 - p)
            blocks = [plus(at.z, step, 4) * 2 + 1 - at.c for step in steps]
            for n in range(4):
                part = slice(256 * n, 256 * (n + 1))
                made = tiles(*blocks, part)
                for k, step in enumerate(steps):
                    partial[step, :, part] = made[TOK * k : TOK * (k + 1)].astype(LOW)
            for step in steps:
                send(partial.at[step], self.pair_in.at[step], self.sems.at[0], self.sems.at[1 + step], at.sibling)
            return 0

        lax.fori_loop(0, 2, to_sibling, 0)

        def along_z(p, _):
            steps = (2 + p, 1 - p)
            blocks = [plus(at.z, step, 4) * 2 + at.c for step in steps]
            for step in steps:
                got(self.pair_in.at[step], self.sems.at[1 + step], at)
            for n in range(4):
                part = slice(256 * n, 256 * (n + 1))
                made = tiles(*blocks, part)
                first = made[0:TOK] + self.pair_in[steps[0], :, part].astype(WIDE)
                second = made[TOK:] + self.pair_in[steps[1], :, part].astype(WIDE)
                partial[3 + steps[0], :, part] = first.astype(LOW)

                @pl.when(p == 0)
                def _():
                    partial[3 + steps[1], :, part] = second.astype(LOW)

                @pl.when(p == 1)
                def _():
                    self.mine[:, part] = second

            def away(step):
                send(
                    partial.at[3 + step], self.line_in.at[step - 1], self.sems.at[0], self.sems.at[5],
                    z_peer(at, step),
                )

            away(steps[0])
            pl.when(p == 0)(lambda: away(steps[1]))
            return 0

        lax.fori_loop(0, 2, along_z, 0)

    def sent_all(self):
        gone(self.r.partial, self.sems.at[0], self.at)

    def total(self):
        value = self.mine[...]
        got(self.line_in, self.sems.at[5], self.at)
        for k in range(3):
            value = value + self.line_in[k].astype(WIDE)
        return value


def order_tokens(r, at):
    before = (
        lax.broadcasted_iota(jnp.int32, (TOK, TOK), 0) > lax.broadcasted_iota(jnp.int32, (TOK, TOK), 1)
    )
    before = jnp.where(before, 1.0, 0.0).astype(LOW)

    def block(b, earlier):
        here = pl.ds(pl.multiple_of(b * TOK, TOK), TOK)
        named = r.named[here, :]
        flags = named.astype(WIDE)
        order = jnp.where(flags > 0.0, dot(before, named) + earlier, -1.0)
        r.order_row[:, here] = jnp.transpose(order)[0:32]
        for e in range(4):
            mine = jnp.where(lanes((TOK, 128)) == 4 * at.j + e, order, 0.0)
            column = jnp.sum(mine, axis=-1, keepdims=True).astype(jnp.int32)
            r.places[here, SLOTS * e : SLOTS * (e + 1)] = jnp.where(
                column == lanes((TOK, SLOTS)), 1.0, 0.0
            ).astype(LOW)
        return earlier + jnp.sum(flags, axis=0, keepdims=True)

    lax.fori_loop(0, 8, block, jnp.zeros((1, 128), WIDE))


def share_tokens(r, at):
    def block(b, _):
        here = pl.ds(pl.multiple_of(b * TOK, TOK), TOK)
        named = r.named[here, :].astype(WIDE) > 0.0
        logits = jnp.where(named, dot(r.hidden_two[here, :], r.router[...]), -1e30)
        powers = jnp.where(named, jnp.exp(logits - jnp.max(logits, axis=-1, keepdims=True)), 0.0)
        shares = powers / jnp.sum(powers, axis=-1, keepdims=True)

        @pl.when(b == at.j)
        def _():
            r.shares[...] = shares

        r.shares_row[:, here] = jnp.transpose(shares)[0:32]
        return 0

    lax.fori_loop(0, 8, block, 0)


def hits(r, at, e, t):
    slot = lax.broadcasted_iota(jnp.int32, (TOK, SEQ), 0) + TOK * t
    return slot == r.order_row[pl.ds(4 * at.j + e, 1), :].astype(jnp.int32)


def pick_rows(r, at, e):
    def pick(t, _):
        r.partial[t] = jnp.where(hits(r, at, e, t), 1.0, 0.0).astype(LOW)
        return 0

    lax.fori_loop(0, 3, pick, 0)


def pick_upstream(r, at, e):
    pick_rows(r, at, e)
    here = pl.ds(pl.multiple_of(e * SLOTS, SLOTS), SLOTS)
    for n in range(4):
        part = slice(256 * n, 256 * (n + 1))
        r.slot_grad[here, part] = dot(r.partial[0:3].reshape(SLOTS, SEQ), r.upstream[:, part]).astype(LOW)
    return 0


def expert(r, at, e):
    row = pl.ds(4 * at.j + e, 1)
    here = pl.ds(pl.multiple_of(e * SLOTS, SLOTS), SLOTS)
    quarters = [slice(256 * n, 256 * (n + 1)) for n in range(4)]

    def strip(t):
        return pl.ds(pl.multiple_of(t * 32, 32), 32)

    def slot_strip(t):
        return pl.ds(pl.multiple_of(e * SLOTS + t * 32, 32), 32)

    def shares(t, _):
        share = jnp.sum(jnp.where(hits(r, at, e, t), r.shares_row[row, :], 0.0), axis=-1, keepdims=True)
        r.share[pl.ds(pl.multiple_of(t * TOK, TOK), TOK), :] = share
        return 0

    pick_rows(r, at, e)
    lax.fori_loop(0, 3, shares, 0)
    for n in quarters:
        r.rows[:, n] = dot(r.partial[0:3].reshape(SLOTS, SEQ), r.hidden_two[:, n]).astype(LOW)
    r.wide_a[:, 0:512] = dot(r.rows[...], r.gate[e].reshape(D, 512))
    r.wide_a[:, 512:1024] = dot(r.rows[...], r.up[e].reshape(D, 512))

    def activate(t, _):
        gate_pre = r.wide_a[strip(t), 0:512]
        silu = gate_pre / (1.0 + jnp.exp(-gate_pre))
        r.product[strip(t), :] = (silu * r.wide_a[strip(t), 512:1024]).astype(LOW)
        return 0

    lax.fori_loop(0, 12, activate, 0)
    for n in quarters:
        r.made[:, n] = dot(r.product[...], r.down[e, :, :, :, n].reshape(512, 256)).astype(LOW)

    def weigh(t, _):
        upstream = r.slot_grad[slot_strip(t), :].astype(WIDE)
        made, share = r.made[strip(t), :].astype(WIDE), r.share[strip(t), :]
        r.gate_dot[strip(t), :] = jnp.sum(upstream * made, axis=-1, keepdims=True)
        r.made[strip(t), :] = (share * made).astype(LOW)
        r.route_grad[strip(t), :] = (share * upstream).astype(LOW)
        return 0

    lax.fori_loop(0, 12, weigh, 0)
    keep = pltpu.make_async_copy(r.made, r.made_far.at[here], r.load.at[3])
    keep.start()
    r.wide_b[:, 0:512] = tail_dot(r.route_grad[...], r.down[e].reshape(512, D))
    for n in quarters:
        down_grad = lead_dot(r.product[...], r.route_grad[:, n])
        r.down[e, :, :, :, n] = down_grad.astype(LOW).reshape(4, 4, 32, 256)

    def activate_back(t, _):
        gate_pre, product_grad = r.wide_a[strip(t), 0:512], r.wide_b[strip(t), 0:512]
        sigmoid = 1.0 / (1.0 + jnp.exp(-gate_pre))
        slope = sigmoid * (1.0 + gate_pre * (1.0 - sigmoid))
        r.gate_low[strip(t), :] = (product_grad * r.wide_a[strip(t), 512:1024] * slope).astype(LOW)
        r.up_low[strip(t), :] = (product_grad * (gate_pre * sigmoid)).astype(LOW)
        return 0

    lax.fori_loop(0, 12, activate_back, 0)
    for m, n in enumerate(quarters):
        slot_grad = tail_dot(r.gate_low[...], r.gate[e, m].reshape(256, 512)) + tail_dot(
            r.up_low[...], r.up[e, m].reshape(256, 512)
        )
        r.slot_grad[here, n] = slot_grad.astype(LOW)
        r.gate[e, m] = lead_dot(r.rows[:, n], r.gate_low[...]).astype(LOW).reshape(4, 64, 512)
        r.up[e, m] = lead_dot(r.rows[:, n], r.up_low[...]).astype(LOW).reshape(4, 64, 512)

    def gate_rows(t, total):
        grads = r.gate_dot[pl.ds(pl.multiple_of(t * TOK, TOK), TOK), :]
        return total + jnp.sum(jnp.where(hits(r, at, e, t), grads, 0.0), axis=0, keepdims=True)

    gate_row = lax.fori_loop(0, 3, gate_rows, jnp.zeros((1, SEQ), WIDE))
    for b in range(8):
        r.gate_grad[b, pl.ds(e, 1), :] = gate_row[:, TOK * b : TOK * (b + 1)]
    keep.wait()


def expert_sums(r, at, e):
    halves = [r.down.at[e, :, :, :, pl.ds(512 * n, 512)] for n in range(2)]
    return (
        SumXY(at, [r.gate.at[e], r.up.at[e]], [way.at[e] for way in r.wide_ways], r.e_sems.at[e, 0], 64),
        SumXY(at, halves, [way.at[e] for way in r.half_ways], r.e_sems.at[e, 1], 32),
    )


def back(r, attended):
    at = place()
    r.wide_ways = (r.wide1, r.wide2, r.wide3, r.wide4)
    r.half_ways = (r.half1, r.half2, r.half3, r.half4)
    r.gate_grad[...] = jnp.zeros((8, 8, 128), WIDE)
    share_tokens(r, at)

    def sums(e, name):
        for unit in expert_sums(r, at, e):
            getattr(unit, name)()

    def one(e, _):
        expert(r, at, e)
        sums(e, "step1")

        @pl.when(e > 0)
        def _():
            sums(e - 1, "step2")

        return 0

    lax.fori_loop(0, 4, one, 0)

    gate_copies = Shares(at, lambda b: r.gate_grad.at[b], r.gate_back.at[at.j], r.gate_back.at[0:7], r.c_sems)
    r.gate_back[pl.ds(at.j, 1)] = r.gate_grad[pl.ds(at.j, 1)]

    def two_blocks(ref, a, b):
        return jnp.concatenate([rows(ref, a)[...], rows(ref, b)[...]], axis=0)

    hidden_sum = SumExpert(at, r, r.pair1, r.line1, r.mine1, r.s_sems.at[0])
    hidden_sum.start(lambda a, b, n: dot(two_blocks(r.places, a, b), r.slot_grad[:, n]))
    made_load = pltpu.make_async_copy(r.made_far, r.slot_grad, r.load.at[3])
    made_load.start()
    own = pl.ds(pl.multiple_of(at.j * TOK, TOK), TOK)
    r.hidden_own[...] = r.hidden_two[own, :]
    out_load = pltpu.make_async_copy(r.out_far, r.hidden_two, r.load.at[0])
    out_load.start()
    hidden_load = pltpu.make_async_copy(r.hidden_far, r.upstream, r.load.at[1])
    hidden_load.start()
    sums(3, "step2")
    attended.forward()
    gate_copies.wait_recv()
    gate_grad = jnp.concatenate(
        [r.gate_back[b][0:4] for b in range(8)] + [jnp.zeros((96, 128), WIDE)], axis=0
    )
    gate_grad = jnp.transpose(gate_grad)
    shares = r.shares[...]
    logit_grad = shares * (gate_grad - jnp.sum(shares * gate_grad, axis=-1, keepdims=True))
    logit_grad = logit_grad.astype(LOW)
    router_grad = lead_dot(r.hidden_own[...], logit_grad)
    hidden_grad = tail_dot(logit_grad, r.router[...])
    hidden_grad = hidden_grad + hidden_sum.total()
    residual, upstream = r.residual[...], r.cotangent[...].astype(WIDE)
    inverse = lax.rsqrt(jnp.mean(residual * residual, axis=-1, keepdims=True) + EPSILON)
    gain_two_grad = jnp.sum(hidden_grad * (residual * inverse), axis=0, keepdims=True)
    scaled = hidden_grad * r.gains[1:2, :]
    mean = jnp.mean(scaled * residual, axis=-1, keepdims=True)
    residual_grad = upstream + scaled * inverse - residual * (inverse * inverse * inverse * mean)
    r.residual_grad[...] = residual_grad
    r.branch[...] = residual_grad.astype(LOW)
    branch_copies = Shares(
        at, lambda b: columns(r.branch, b), rows(r.branch_part, at.j), r.branch_part.at[0 : 7 * TOK], r.b_sems
    )
    out_load.wait()
    for n in range(4):
        part = slice(256 * n, 256 * (n + 1))
        r.attended_grad[:, part] = tail_dot(r.branch[...], r.hidden_two[part, :]).astype(LOW)
    grad_copies = Shares(
        at, lambda b: columns(r.attended_grad, b), rows(r.attended_back, at.j), r.attended_back.at[0 : 7 * TOK],
        r.d_sems,
    )
    rows(r.branch_part, at.j)[...] = columns(r.branch, at.j)[...]
    rows(r.attended_back, at.j)[...] = columns(r.attended_grad, at.j)[...]
    hidden_sum.sent_all()

    output_sum = SumExpert(at, r, r.pair2, r.line2, r.mine2, r.s_sems.at[1])
    made_load.wait()
    output_sum.start(lambda a, b, n: dot(two_blocks(r.places, a, b), r.slot_grad[:, n]))
    sums(0, "step3")
    sums(1, "step3")
    grad_copies.wait_recv()

    low_lanes = lanes((256, 128)) < 64
    r.key_grad[...] = jnp.zeros((SEQ, 128), WIDE)
    r.value_grad[...] = jnp.zeros((SEQ, 128), WIDE)
    for b in range(4):
        here = slice(256 * b, 256 * (b + 1))
        heads = []
        for head in range(2):
            query = one_head(r.queries[here, :], head) * SCALE
            grad = one_head(r.attended_back[here, :], head)
            inner = grad.astype(WIDE) * r.attended_head[here, :].astype(WIDE)
            inner = jnp.sum(inner, axis=-1, keepdims=True)
            log_total = r.log_total[here, head : head + 1]
            query_grad = jnp.zeros((256, 128), WIDE)
            for c in range(b + 1):
                part = slice(256 * c, 256 * (c + 1))
                probs = jnp.exp(tail_dot(query, r.keys[part, :]) - log_total)
                keep = allowed(r, b, c)
                if keep is not None:
                    probs = jnp.where(keep, probs, 0.0)
                prob_grad = tail_dot(grad, r.values[part, :])
                score_grad = (probs * (prob_grad - inner)).astype(LOW)
                query_grad = query_grad + dot(score_grad, r.keys[part, :])
                r.key_grad[part, :] += lead_dot(score_grad, query)
                r.value_grad[part, :] += lead_dot(probs.astype(LOW), grad)
            heads.append(query_grad)
        query_grad = jnp.where(low_lanes, heads[0], heads[1]) * SCALE
        cosine, sine = angles(r, here, (256, 128))
        r.qkv_grad[here, 0:128] = turn(query_grad, cosine, -sine).astype(LOW)
        if b == 2:
            sums(2, "step3")
            sums(0, "step4")
    sums(1, "step4")
    low_lanes = lanes((TOK, 128)) < 64

    def finish_keys(b, _):
        here = pl.ds(pl.multiple_of(b * TOK, TOK), TOK)
        key_grad, value_grad = r.key_grad[here, :], r.value_grad[here, :]
        key_grad = key_grad + pltpu.roll(key_grad, 64, axis=1)
        value_grad = value_grad + pltpu.roll(value_grad, 64, axis=1)
        cosine, sine = angles(r, here, (TOK, 128))
        key_grad = turn(key_grad, cosine, -sine)
        r.qkv_grad[here, 128:256] = jnp.where(low_lanes, key_grad, value_grad).astype(LOW)
        return 0

    lax.fori_loop(0, 8, finish_keys, 0)

    output_sum.sent_all()
    r.gain_sum[...] = jnp.zeros((8, D), WIDE)

    hidden_load.wait()

    def hidden_one_tile(a, b, n):
        made = tail_dot(two_blocks(r.qkv_grad, a, b), r.w_qkv[n, :])
        hidden = jnp.concatenate([rows(r.upstream, k).at[:, n][...] for k in (a, b)], axis=0)
        r.gain_sum[0:1, n] += jnp.sum(made * hidden.astype(WIDE), axis=0, keepdims=True)
        return made

    input_sum = SumExpert(at, r, r.pair3, r.line3, r.mine1, r.s_sems.at[2])
    input_sum.start(hidden_one_tile)

    branch_copies.wait_recv()
    branch_copies.wait_send()
    attended.finish()
    gain_rows = jnp.concatenate(
        [
            jnp.zeros((32, D), WIDE), r.gain_sum[0:1, :] / r.gains[0:1, :], gain_two_grad, jnp.zeros((94, D), WIDE),
        ],
        axis=0,
    )
    for m in range(4):
        here = slice(256 * m, 256 * (m + 1))
        grads = lead_dot(r.upstream[:, here], r.qkv_grad[...]).astype(LOW)
        out_grads = lead_dot(r.attended_all[:, here], r.branch_part[...]).astype(LOW)
        others = [jnp.transpose(gain_rows[:, 256 * m + 128 * t : 256 * m + 128 * (t + 1)]) for t in range(2)]
        others = (router_grad[here] + jnp.concatenate(others, axis=0)).astype(LOW)
        for x in range(4):
            part = slice(64 * x, 64 * (x + 1))
            r.dense[m, x, 0:64] = grads[part, 0:128]
            r.dense[m, x, 64:128] = grads[part, 128:256]
            r.dense[m, x, 128:192] = out_grads[part]
            r.dense[m, x, 192:256] = others[part]
    dense_sum = SumXY(
        at, [r.dense.at[:, :, pl.ds(128 * n, 128)] for n in range(2)], (r.dense1, r.dense2, r.dense3, r.dense4),
        r.f_sems, 128,
    )
    dense_sum.step1()
    sums(3, "step3")
    sums(2, "step4")
    dense_sum.step2()

    def stores(e):
        high = pl.ds(pl.multiple_of(e * 64, 64), 64)
        low = pl.ds(pl.multiple_of(e * 32, 32), 32)
        return [
            pltpu.make_async_copy(r.wide_a.at[high, 0:512], r.gate_out.at[e], r.store.at[e, 0]),
            pltpu.make_async_copy(r.wide_a.at[high, 512:1024], r.up_out.at[e], r.store.at[e, 1]),
            pltpu.make_async_copy(r.wide_b.at[low], r.down_out.at[e], r.store.at[e, 2]),
        ]

    def finish_expert(e, _):
        wide_sum, half_sum = expert_sums(r, at, e)
        gate, up = wide_sum.step5()
        left, right = half_sum.step5()
        high = pl.ds(pl.multiple_of(e * 64, 64), 64)
        r.wide_a[high, 0:512] = gate
        r.wide_a[high, 512:1024] = up
        low = pl.ds(pl.multiple_of(e * 32, 32), 32)
        r.wide_b[low, 0:512] = left
        r.wide_b[low, 512:1024] = right
        for copy in stores(e):
            copy.start()
        return 0

    lax.fori_loop(0, 3, finish_expert, 0)
    sums(3, "step4")
    dense_sum.step3()
    r.branch[...] = (r.residual[...] + output_sum.total()).astype(LOW)
    output_store = pltpu.make_async_copy(r.branch, r.output, r.load.at[0])
    output_store.start()
    finish_expert(3, 0)
    dense_sum.step4()

    hidden_grad = input_sum.total()
    inputs = r.tokens[...].astype(WIDE)
    inverse = lax.rsqrt(jnp.mean(inputs * inputs, axis=-1, keepdims=True) + EPSILON)
    scaled = hidden_grad * r.gains[0:1, :]
    mean = jnp.mean(scaled * inputs, axis=-1, keepdims=True)
    r.residual_grad[...] = (
        r.residual_grad[...] + scaled * inverse - inputs * (inverse * inverse * inverse * mean)
    )
    input_store = pltpu.make_async_copy(r.residual_grad, r.input_grad, r.load.at[1])
    input_store.start()
    for n, total in enumerate(dense_sum.step5()):
        r.dense_total[n] = total.reshape(2, 8, 8, 128)
    last_copies = Shares(
        at, lambda b: r.dense_total.at[:, :, b], r.dense_back.at[at.j], r.dense_back.at[0:7], r.l_sems
    )
    r.dense_back[pl.ds(at.j, 1)] = r.dense_total[:, :, pl.ds(at.j, 1)].reshape(1, 2, 2, 8, 128)
    last_copies.wait_recv()
    low_lanes = lanes((8, 128)) < 64
    others = jnp.zeros((8, 128), WIDE)
    for b in range(8):
        head = slice(128 * b, 128 * (b + 1))
        r.query_out[:, head] = r.dense_back[b, 0, 0]
        r.out_out[:, head] = r.dense_back[b, 1, 0]
        others = others + r.dense_back[b, 1, 1]
    for t in range(4):
        head = slice(128 * t, 128 * (t + 1))
        even, odd = r.dense_back[2 * t, 0, 1], r.dense_back[2 * t + 1, 0, 1]
        r.key_out[:, head] = jnp.where(low_lanes, even, pltpu.roll(odd, 64, axis=1))
        r.value_out[:, head] = jnp.where(low_lanes, pltpu.roll(even, 64, axis=1), odd)
    r.others_out[...] = others

    input_sum.sent_all()
    for copy in (gate_copies, grad_copies, last_copies):
        copy.wait_send()
    output_store.wait()
    input_store.wait()

    def ended(e, _):
        for copy in stores(e):
            copy.wait()
        for unit in expert_sums(r, at, e):
            unit.finish()
        return 0

    lax.fori_loop(0, 4, ended, 0)
    dense_sum.finish()

DMA = pltpu.SemaphoreType.DMA


def low(*shape):
    return pltpu.VMEM(shape, LOW)


def wide(*shape):
    return pltpu.VMEM(shape, WIDE)


def far(*shape, kind=WIDE):
    return pltpu.HBM(shape, kind)


OUTS = dict(
    output=far(TOK, D, kind=LOW), input_grad=far(TOK, D), query_out=wide(8, D), key_out=wide(8, 512),
    value_out=wide(8, 512), out_out=wide(8, D), others_out=wide(8, 128), gate_out=far(4, 64, 512),
    up_out=far(4, 64, 512), down_out=far(4, 32, D), made_far=far(4 * SLOTS, D, kind=LOW),
    hidden_far=far(SEQ, D, kind=LOW), out_far=far(D, D, kind=LOW),
)
SCRATCH = dict(
    w_qkv=low(D, 256), router=low(D, 128), gains=wide(8, D), queries=low(SEQ, 128), keys=low(SEQ, 128),
    values=low(SEQ, 128), log_total=wide(SEQ, 128), attended=low(TOK, D), residual=wide(TOK, D),
    hidden_two=low(SEQ, D), upstream=low(SEQ, D), named=low(SEQ, 128),
    pack=wide(8, 24, 128), near=wide(8, 24, 128), stage=low(192, 128),
    out_mine=wide(8, D), out_other=wide(8, D), out_rows=low(64, 512),
    gate=low(4, 4, 4, 64, 512), up=low(4, 4, 4, 64, 512), down=low(4, 4, 4, 32, D),
    shares=wide(TOK, 128), shares_row=wide(32, SEQ), order_row=wide(32, SEQ), places=low(SEQ, 4 * SLOTS),
    rows=low(SLOTS, D), route_grad=low(SLOTS, D), made=low(SLOTS, D), slot_grad=low(4 * SLOTS, D),
    gate_grad=wide(8, 8, 128), gate_back=wide(8, 8, 128), wide_a=wide(SLOTS, D), wide_b=wide(SLOTS, D),
    product=low(SLOTS, 512), gate_low=low(SLOTS, 512), up_low=low(SLOTS, 512), share=wide(SLOTS, 1),
    gate_dot=wide(SLOTS, 1), hidden_own=low(TOK, D),
    wide1=low(4, 2, 2, 2, 64, 512), wide2=low(4, 2, 2, 4, 64, 512), wide3=low(4, 2, 2, 32, 512),
    wide4=low(4, 2, 2, 64, 512), half1=low(4, 2, 2, 2, 32, 512), half2=low(4, 2, 2, 4, 32, 512),
    half3=low(4, 2, 2, 16, 512), half4=low(4, 2, 2, 32, 512), dense=low(4, 4, 256, 128),
    dense1=low(2, 2, 2, 128, 128), dense2=low(2, 2, 4, 128, 128), dense3=low(2, 2, 64, 128),
    dense4=low(2, 2, 128, 128), dense_total=wide(2, 2, 8, 8, 128), dense_back=wide(8, 2, 2, 8, 128),
    partial=low(7, TOK, D), pair1=low(4, TOK, D), line1=low(3, TOK, D), mine1=wide(TOK, D),
    pair2=low(4, TOK, D), line2=low(3, TOK, D), mine2=wide(TOK, D), pair3=low(4, TOK, D), line3=low(3, TOK, D),
    residual_grad=wide(TOK, D), branch=low(TOK, D), branch_part=low(SEQ, 128), attended_grad=low(TOK, D),
    attended_back=low(SEQ, 128), attended_all=low(SEQ, D), key_grad=wide(SEQ, 128), value_grad=wide(SEQ, 128),
    qkv_grad=low(SEQ, 256), gain_sum=wide(8, D),
    x_sems=DMA((5,)), n_sems=DMA((5,)), g_sems=DMA((5,)), h_sems=DMA((5,)), t_sems=DMA((5,)), p_sems=DMA((2,)),
    c_sems=DMA((2,)), b_sems=DMA((2,)), d_sems=DMA((2,)), l_sems=DMA((2,)), w_sems=DMA((2, 4)),
    o_sems=DMA((2, 4)), a_sems=DMA((2,)), q_sems=DMA((6,)), e_sems=DMA((4, 2, 4, 2)), f_sems=DMA((4, 2)),
    s_sems=DMA((3, 6)), load=DMA((5,)), store=DMA((4, 3)),
)


def is_far(name):
    return name in OUTS and OUTS[name].memory_space != pltpu.VMEM or name in ("gate_in", "up_in", "down_in")


def spec(name):
    return pl.BlockSpec(memory_space=pl.ANY if is_far(name) else pltpu.VMEM)


def layer(**arrays):
    names = list(arrays) + list(OUTS) + list(SCRATCH)

    def kernel(*refs):
        r = SimpleNamespace(**dict(zip(names, refs)))
        r.hidden_one, r.w_out_all = r.slot_grad.at[0:SEQ], r.places.at[:, 0:D]
        r.attended_head = r.qkv_grad.at[:, 128:256]
        r.extra_all = r.key_grad
        back(r, front(r))

    outs = pl.pallas_call(
        kernel,
        out_shape=[jax.ShapeDtypeStruct(OUTS[n].shape, OUTS[n].dtype) for n in OUTS],
        in_specs=[spec(n) for n in arrays],
        out_specs=[spec(n) for n in OUTS],
        scratch_shapes=list(SCRATCH.values()),
        name="layer",
        compiler_params=pltpu.CompilerParams(
            collective_id=0, has_side_effects=True, vmem_limit_bytes=510 << 17
        ),
    )(*arrays.values())
    return dict(zip(OUTS, outs))


def hand_on(*refs):
    come, go = refs[-2:]
    loads = [pltpu.make_async_copy(refs[n], refs[18 + n], come.at[n]) for n in range(9)]
    stores = [pltpu.make_async_copy(refs[18 + n], refs[9 + n], go.at[n]) for n in range(9)]
    for copy in loads:
        copy.start()
    for load, store in zip(loads, stores):
        load.wait()
        store.start()
    for copy in stores:
        copy.wait()


def handed_on(*arrays):
    return pl.pallas_call(
        hand_on,
        out_shape=[jax.ShapeDtypeStruct(a.shape, a.dtype) for a in arrays],
        in_specs=[pl.BlockSpec(memory_space=pl.ANY)] * 9,
        out_specs=[pl.BlockSpec(memory_space=pl.ANY)] * 9,
        scratch_shapes=[pltpu.VMEM(a.shape, a.dtype) for a in arrays] + [DMA((9,)), DMA((9,))],
        name="hand_on",
    )(*arrays)


def shards(
    tokens, segments, routes, gain_attn, gain_ffn, w_query, w_key, w_value, w_out, w_router, w_gate, w_up,
    w_down, cotangent,
):
    extra = jnp.concatenate(
        [w_router, gain_attn[:, None], gain_ffn[:, None], jnp.zeros((8, 94), LOW)], axis=1
    ).astype(WIDE)
    angle = np.arange(SEQ, dtype=np.float32)[:, None] * (
        np.float32(10000.0) ** (-np.arange(32, dtype=np.float32) / np.float32(32))
    )
    waves = np.concatenate([np.cos(angle), np.cos(angle), -np.sin(angle), np.sin(angle)], axis=1)
    made = layer(
        tokens=tokens, routes=routes.T, w_query=w_query, w_key=w_key, w_value=w_value, w_out=w_out,
        extra=extra, seg_row=segments, table=jnp.asarray(waves.astype(np.float32)), cotangent=cotangent,
        gate_in=w_gate.reshape(4, 4, 4, 64, 512), up_in=w_up.reshape(4, 4, 4, 64, 512),
        down_in=w_down.reshape(4, 4, 4, 32, D),
    )
    others = made["others_out"]
    output, input_grad, query, key, value, out, gate, up, down = handed_on(
        made["output"], made["input_grad"], made["query_out"], made["key_out"], made["value_out"],
        made["out_out"], made["gate_out"], made["up_out"], made["down_out"],
    )
    return (
        output, input_grad, others[:, 32], others[:, 33], query, key, value, out, others[:, 0:32], gate, up, down,
    )


def solution(mesh):
    line, dense = P(("dp", "expert")), P(("dp", "expert"), None)
    copied, summed = P("expert", None, None), P("expert", "dp", None)
    return jax.shard_map(
        shards,
        mesh=mesh,
        in_specs=(dense, P("dp", None), dense, line, line) + (dense,) * 5 + (copied,) * 3 + (dense,),
        out_specs=(dense, dense, line, line) + (dense,) * 5 + (summed,) * 3,
        check_vma=False,
    )
```

```python
import functools
from types import SimpleNamespace

import jax
import jax.numpy as jnp
import numpy as np
from jax import lax
from jax.experimental import pallas as pl
from jax.experimental.pallas import tpu as pltpu
from jax.sharding import PartitionSpec as P

MESH = pl.DeviceIdType.MESH
LOW, WIDE = jnp.bfloat16, jnp.float32
EPSILON = 1e-06
SCALE = 64 ** (-0.5)
TOK, SEQ, D, SLOTS = 128, 1024, 1024, 384
Z_STEPS = (2, 1, 3)


def dot(one, two):
    return lax.dot_general(one, two, (((1,), (0,)), ((), ())), preferred_element_type=WIDE)


def tail_dot(one, two):
    return lax.dot_general(one, two, (((1,), (1,)), ((), ())), preferred_element_type=WIDE)


def lead_dot(one, two):
    return lax.dot_general(one, two, (((0,), (0,)), ((), ())), preferred_element_type=WIDE)


def place():
    i, j = lax.axis_index("dp"), lax.axis_index("expert")
    at = SimpleNamespace(i=i, j=j, x=lax.rem(i, 4), y=lax.div(i, 4), z=lax.div(j, 2), c=lax.rem(j, 2))
    at.sibling = (i, at.z * 2 + 1 - at.c)
    return at


def plus(value, step, size):
    return lax.rem(value + step, size)


def z_peer(at, step):
    return (at.i, plus(at.z, step, 4) * 2 + at.c)


def xy_peer(at, x_step, y_step):
    return (plus(at.y, y_step, 4) * 4 + plus(at.x, x_step, 4), at.j)


def send(source, target, sent, got, device):
    copy = pltpu.make_async_remote_copy(
        src_ref=source, dst_ref=target, send_sem=sent, recv_sem=got, device_id=device, device_id_type=MESH
    )
    copy.start()
    return copy


def rows(ref, block, size=TOK):
    return ref.at[pl.ds(pl.multiple_of(block * size, size), size)]


def columns(ref, block, size=128):
    return ref.at[:, pl.ds(pl.multiple_of(block * size, size), size)]


def got(ref, semaphore, at):
    pltpu.make_async_remote_copy(
        src_ref=ref, dst_ref=ref, send_sem=semaphore, recv_sem=semaphore, device_id=at.sibling, device_id_type=MESH
    ).wait_recv()


def gone(ref, semaphore, at):
    pltpu.make_async_remote_copy(
        src_ref=ref, dst_ref=ref, send_sem=semaphore, recv_sem=semaphore, device_id=at.sibling, device_id_type=MESH
    ).wait_send()


class Gather:
    def __init__(self, at, source, target, sems):
        self.at, self.source, self.target, self.sems = at, source, target, sems

    def start(self):
        at, mine = self.at, rows(self.target, self.at.j)
        for k, step in enumerate(Z_STEPS):
            send(self.source, mine, self.sems.at[0], self.sems.at[1 + k], z_peer(at, step))
        send(self.source, mine, self.sems.at[0], self.sems.at[4], at.sibling)

    def forward(self):
        at = self.at
        for k, step in enumerate(Z_STEPS):
            block = rows(self.target, plus(at.z, 4 - step, 4) * 2 + at.c)
            got(block, self.sems.at[1 + k], at)
            send(block, block, self.sems.at[0], self.sems.at[4], at.sibling)

    def finish(self):
        got(self.target.at[0 : 4 * TOK], self.sems.at[4], self.at)
        gone(self.target.at[0 : 7 * TOK], self.sems.at[0], self.at)


class Shares:
    def __init__(self, at, source, target, seven, sems):
        self.at, self.seven, self.sems = at, seven, sems
        for step in range(1, 8):
            other = plus(at.j, step, 8)
            send(source(other), target, sems.at[0], sems.at[1], (at.i, other))

    def wait_recv(self):
        got(self.seven, self.sems.at[1], self.at)

    def wait_send(self):
        gone(self.seven, self.sems.at[0], self.at)


class Spread:
    def __init__(self, at, source, target, four, three, sems):
        self.at, self.four, self.three, self.sems = at, four, three, sems
        for step in range(1, 16):
            y = step // 4
            send(source, target, sems.at[0, y], sems.at[1, y], xy_peer(at, step % 4, y))

    def wait_recv(self):
        got(self.three, self.sems.at[1, 0], self.at)
        for step in range(1, 4):
            got(self.four(plus(self.at.y, 4 - step, 4)), self.sems.at[1, step], self.at)

    def wait_send(self):
        gone(self.three, self.sems.at[0, 0], self.at)
        for step in range(1, 4):
            gone(self.four(plus(self.at.y, 4 - step, 4)), self.sems.at[0, step], self.at)


def greet(devices):
    barrier = pltpu.get_barrier_semaphore()
    for device in devices:
        pl.semaphore_signal(barrier, inc=1, device_id=device, device_id_type=MESH)
    return lambda: pl.semaphore_wait(barrier, len(devices))


def expert_peers(at):
    return [(at.i, plus(at.j, step, 8)) for step in range(1, 8)]


def dp_peers(at):
    return [xy_peer(at, step % 4, step // 4) for step in range(1, 16)]


def lanes(shape):
    return lax.broadcasted_iota(jnp.int32, shape, len(shape) - 1)


def turn(values, cosine, signed_sine):
    lane = lanes(values.shape)
    swapped = jnp.where(
        lane % 64 < 32, pltpu.roll(values, 96, axis=1), pltpu.roll(values, 32, axis=1)
    )
    return values * cosine + swapped * signed_sine


def angles(r, here, shape):
    table = r.table[here, :]
    other, low_lanes = pltpu.roll(table, 64, axis=1), lanes(shape) < 64
    return jnp.where(low_lanes, table, other), jnp.where(low_lanes, other, table)


def allowed(r, b, c):
    keep = None
    if c == 0 or b == 3:
        keep = r.log_total[256 * b : 256 * (b + 1), 2:3] == r.seg_row[:, 256 * c : 256 * (c + 1)].astype(WIDE)
    if b == c:
        below = lanes((256, 256)) <= lax.broadcasted_iota(jnp.int32, (256, 256), 0)
        keep = below if keep is None else keep & below
    return keep


def one_head(values, head):
    return jnp.where((lanes(values.shape) < 64) == (head == 0), values, jnp.zeros_like(values))


def front(r):
    at = place()
    ready = greet(expert_peers(at) + dp_peers(at))

    query_w, key_w = r.w_query[...].astype(WIDE), r.w_key[...].astype(WIDE)
    value_w = r.w_value[...].astype(WIDE)
    r.corner[...] = jnp.zeros((128, 128), WIDE)
    r.corner[32:33, 0:8] = r.gain_attn[...].astype(WIDE)
    r.corner[33:34, 0:8] = r.gain_ffn[...].astype(WIDE)
    r.extra[...] = jnp.transpose(r.corner[...])[0:8]
    r.extra[:, 0:32] = r.w_router[...].astype(WIDE)
    low_lanes = lanes((8, 128)) < 64
    for j in range(8):
        tile = slice(128 * (j // 2), 128 * (j // 2) + 128)
        key_part, value_part = key_w[:, tile], value_w[:, tile]
        if j % 2:
            key_part = pltpu.roll(key_part, 64, axis=1)
        else:
            value_part = pltpu.roll(value_part, 64, axis=1)
        head = slice(128 * j, 128 * j + 128)
        r.pack[j] = jnp.concatenate(
            [query_w[:, head], jnp.where(low_lanes, key_part, value_part), r.extra[...]], axis=0
        )
    r.out_mine[...] = r.w_out[...].astype(WIDE)
    r.near[at.j] = r.pack[at.j]
    expert = lax.broadcasted_iota(jnp.int32, (128, TOK), 0)
    named = jnp.zeros((128, TOK), WIDE)
    for k in range(8):
        named = named + jnp.where(r.routes[k : k + 1, :] == expert, 1.0, 0.0)
    rows(r.named, at.j)[...] = jnp.transpose(named).astype(LOW)
    rows(r.hidden_one, at.j)[...] = r.tokens[...]
    for b in range(8):
        here = slice(TOK * b, TOK * (b + 1))
        across = jnp.broadcast_to(r.seg_row[:, here].astype(WIDE), (TOK, TOK))
        r.log_total[here, :] = jnp.transpose(across)

    ready()
    pair = send(r.out_mine, r.out_other, r.q_sems.at[0], r.q_sems.at[1], at.sibling)
    first = Shares(at, lambda b: r.pack.at[b], r.near.at[at.j], r.near.at[0:7], r.p_sems)
    tokens = Gather(at, r.tokens, r.hidden_one, r.x_sems)
    tokens.start()
    pair.wait_recv()
    mine, other = r.out_mine[...], r.out_other[...]
    both = jnp.where(
        at.c == 0,
        jnp.concatenate([mine[:, 0:512], other[:, 0:512]], axis=0),
        jnp.concatenate([other[:, 512:1024], mine[:, 512:1024]], axis=0),
    )
    line = rows(r.out_rows, at.z, 16)
    line[...] = both.astype(LOW)
    for step in Z_STEPS:
        send(line, line, r.q_sems.at[2], r.q_sems.at[3], z_peer(at, step))
    marks = Gather(at, rows(r.named, at.j), r.named, r.n_sems)
    marks.start()
    loads = []
    for n, (source, target) in enumerate(((r.gate_in, r.gate), (r.up_in, r.up), (r.down_in, r.down))):
        loads.append(pltpu.make_async_copy(source, target, r.load.at[n]))
        loads[-1].start()
    first.wait_recv()
    for b in range(8):
        r.stage[16 * b : 16 * (b + 1)] = r.near[b, 0:16].astype(LOW)
    r.stage[128:192] = jnp.concatenate([r.near[b, 16:24] for b in range(8)], axis=0).astype(LOW)
    second = Spread(
        at, r.stage, r.dense.at[at.y, at.x, 0:192], lambda y: r.dense.at[y, :, 0:192], r.dense.at[0, 0:3, 0:192],
        r.w_sems,
    )
    r.dense[at.y, at.x, 0:192] = r.stage[...]
    half = pl.ds(pl.multiple_of(at.c * 512, 512), 512)
    out_half = r.w_out_all.at[pl.ds(pl.multiple_of(at.i * 64, 64), 64), half]
    got(r.out_rows.at[0:48], r.q_sems.at[3], at)
    third = Spread(
        at, r.out_rows, out_half, lambda y: r.w_out_all.at[pl.ds(pl.multiple_of(y * 256, 256), 256), half],
        r.w_out_all.at[0:192, half], r.o_sems,
    )
    out_half[...] = r.out_rows[...]
    tokens.forward()
    rows(r.upstream, at.j)[...] = r.cotangent[...]
    upstream = Gather(at, r.cotangent, r.upstream, r.g_sems)
    upstream.start()
    second.wait_recv()

    def unpack(i, _):
        part = r.dense[lax.div(i, 4), lax.rem(i, 4), 0:192].astype(WIDE)
        here = pl.ds(pl.multiple_of(i * 64, 64), 64)
        heads = part[0:128].reshape(8, 16, 128)
        r.w_qkv[here, 0:128] = heads[:, 0:8, :].reshape(64, 128).astype(LOW)
        r.w_qkv[here, 128:256] = heads[:, 8:16, :].reshape(64, 128).astype(LOW)
        r.extra_all[here, :] = part[128:192]
        return 0

    lax.fori_loop(0, 16, unpack, 0)
    r.gains[...] = extra_rows(r)
    r.router[...] = r.extra_all[...].astype(LOW)
    tokens.finish()

    low_lanes = lanes((256, 128)) < 64

    def project(b, _):
        here = pl.ds(pl.multiple_of(b * 256, 256), 256)
        x = r.hidden_one[here, :].astype(WIDE)
        inverse = lax.rsqrt(jnp.mean(x * x, axis=-1, keepdims=True) + EPSILON)
        hidden = (x * inverse * r.gains[0:1, :]).astype(LOW)
        r.hidden_one[here, :] = hidden
        made = dot(hidden, r.w_qkv[...])
        cosine, sine = angles(r, here, (256, 128))
        r.queries[here, :] = turn(made[:, 0:128], cosine, sine).astype(LOW)
        pair = turn(
            made[:, 128:256], jnp.where(low_lanes, cosine, 1.0), jnp.where(low_lanes, sine, 0.0)
        )
        turned = pltpu.roll(pair, 64, axis=1)
        r.keys[here, :] = jnp.where(low_lanes, pair, turned).astype(LOW)
        r.values[here, :] = jnp.where(low_lanes, turned, pair).astype(LOW)
        return 0

    lax.fori_loop(0, 4, project, 0)
    marks.forward()
    hidden_save = pltpu.make_async_copy(r.hidden_one, r.hidden_far, r.load.at[3])
    hidden_save.start()

    low_lanes = lanes((256, 128)) < 64
    scores = ((r.mine1, r.mine2), (r.residual, r.residual_grad))
    for b in range(4):
        here = slice(256 * b, 256 * (b + 1))
        logs, heads = [], []
        for head in range(2):
            query = one_head(r.queries[here, :], head) * SCALE
            top = jnp.full((256, 256), -1e30, WIDE)
            for c in range(b + 1):
                part = slice(256 * c, 256 * (c + 1))
                score, keep = tail_dot(query, r.keys[part, :]), allowed(r, b, c)
                if keep is not None:
                    score = jnp.where(keep, score, -1e30)
                scores[head][0][:, part], scores[head][1][:, part] = score[0:TOK], score[TOK:256]
                top = jnp.maximum(top, score)
            top = jnp.max(top, axis=-1, keepdims=True)
            mixed = jnp.zeros((256, 128), WIDE)
            for c in range(b + 1):
                part = slice(256 * c, 256 * (c + 1))
                score = jnp.concatenate([scores[head][0][:, part], scores[head][1][:, part]], axis=0)
                powers = jnp.exp(score - top).astype(LOW)
                value = r.values[part, :]
                mixed = mixed + dot(powers, jnp.where(low_lanes == (head == 0), value, jnp.ones_like(value)))
            total = mixed[:, 64:65] if head == 0 else mixed[:, 0:1]
            heads.append(mixed / total)
            logs.append(top + jnp.log(total))
        r.attended_head[here, :] = jnp.where(low_lanes, heads[0], heads[1]).astype(LOW)
        lane = lanes((256, 128))
        r.log_total[here, :] = jnp.where(
            lane == 0, logs[0], jnp.where(lane == 1, logs[1], r.log_total[here, :])
        )
        for n in (2 * b, 2 * b + 1):

            @pl.when(at.j != n)
            def _():
                send(
                    r.attended_head.at[TOK * n : TOK * (n + 1)], columns(r.attended, at.j), r.a_sems.at[0],
                    r.a_sems.at[1], (at.i, jnp.int32(n)),
                )

            @pl.when(at.j == n)
            def _():
                columns(r.attended, at.j)[...] = r.attended_head[TOK * n : TOK * (n + 1), :]

    third.wait_recv()
    out_mine = columns(r.w_out_all, at.c, 512)
    whole = send(out_mine, out_mine, r.q_sems.at[4], r.q_sems.at[5], at.sibling)
    upstream.forward()
    got(r.attended.at[:, 0 : 7 * 128], r.a_sems.at[1], at)
    whole.wait_recv()

    residual = r.tokens[...].astype(WIDE) + dot(r.attended[...], r.w_out_all[...])
    r.residual[...] = residual
    inverse = lax.rsqrt(jnp.mean(residual * residual, axis=-1, keepdims=True) + EPSILON)
    rows(r.hidden_two, at.j)[...] = (residual * inverse * r.gains[1:2, :]).astype(LOW)
    hidden = Gather(at, rows(r.hidden_two, at.j), r.hidden_two, r.h_sems)
    hidden.start()
    out_save = pltpu.make_async_copy(r.w_out_all, r.out_far, r.load.at[4])
    out_save.start()
    attended = Gather(at, r.attended, r.attended_all, r.t_sems)
    rows(r.attended_all, at.j)[...] = r.attended[...]
    for copy in (first, second, third, pair, whole):
        copy.wait_send()
    gone(r.out_rows.at[0:48], r.q_sems.at[2], at)
    gone(r.attended_head.at[0 : 7 * TOK], r.a_sems.at[0], at)
    upstream.finish()
    marks.finish()
    hidden_save.wait()
    out_save.wait()
    order_tokens(r, at)
    for copy in loads:
        copy.wait()
    lax.fori_loop(0, 4, lambda e, _: pick_upstream(r, at, e), 0)
    hidden.forward()
    hidden.finish()
    attended.start()
    return attended


def extra_rows(r):
    picked = [jnp.transpose(r.extra_all[TOK * b : TOK * (b + 1), :])[32:40, :] for b in range(8)]
    return jnp.concatenate(picked, axis=1)


class SumXY:
    def __init__(self, at, sources, ways, sems, height):
        self.at, self.sources, self.ways, self.sems, self.height = at, sources, ways, sems, height

    def place(self, n):
        return (self.at.x, self.at.y) if n == 0 else (self.at.y, self.at.x)

    def block(self, n, first, second):
        return self.sources[n].at[second, first] if n == 0 else self.sources[n].at[first, second]

    def out(self, n, k, way, ref, second, step):
        device = xy_peer(self.at, step, 0) if (n == 0) != second else xy_peer(self.at, 0, step)
        send(ref, self.ways[k].at[n, way], self.sems.at[k, 0], self.sems.at[k, 1], device)

    def take(self, k):
        got(self.ways[k], self.sems.at[k, 1], self.at)

    def step1(self):
        for n in range(2):
            far = plus(self.place(n)[0], 2, 4)
            self.out(n, 0, 0, self.block(n, far, pl.ds(0, 2)), False, 1)
            self.out(n, 0, 1, self.block(n, far, pl.ds(2, 2)), False, 3)

    def step2(self):
        self.take(0)
        for n in range(2):
            for k, step in enumerate((1, 3)):
                near = plus(self.place(n)[0], step, 4)
                part = self.block(n, near, pl.ds(2 * k, 2))
                part[...] = part[...] + self.ways[0][n, k]
                self.out(n, 1, k, self.block(n, near, pl.ds(0, 4)), False, step)

    def step3(self):
        self.take(1)
        half = self.height // 2
        for n in range(2):
            first, second = self.place(n)
            mine = self.block(n, first, pl.ds(0, 4))
            mine[...] = mine[...] + (self.ways[1][n, 0] + self.ways[1][n, 1])
            far = self.block(n, first, plus(second, 2, 4))
            self.out(n, 2, 0, far.at[pl.ds(0, half)], True, 1)
            self.out(n, 2, 1, far.at[pl.ds(half, half)], True, 3)

    def step4(self):
        self.take(2)
        half = self.height // 2
        for n in range(2):
            first, second = self.place(n)
            for k, step in enumerate((1, 3)):
                near = self.block(n, first, plus(second, step, 4))
                part = near.at[pl.ds(half * k, half)]
                part[...] = part[...] + self.ways[2][n, k]
                self.out(n, 3, k, near, True, step)

    def step5(self):
        self.take(3)
        totals = []
        for n in range(2):
            mine = self.block(n, *self.place(n))[...].astype(WIDE)
            totals.append(mine + self.ways[3][n, 0].astype(WIDE) + self.ways[3][n, 1].astype(WIDE))
        return totals

    def finish(self):
        for k in range(4):
            gone(self.ways[k], self.sems.at[k, 0], self.at)


class SumExpert:
    def __init__(self, at, partial, seven, pair_in, line_in, mine, sems):
        self.at, self.partial, self.seven = at, partial, seven
        self.pair_in, self.line_in, self.mine, self.sems = pair_in, line_in, mine, sems

    def across(self, tiles, n):
        at, part = self.at, slice(256 * n, 256 * (n + 1))

        def one(p, _):
            steps = (2 + p, 1 - p)
            made = tiles(*[plus(at.z, step, 4) * 2 + 1 - at.c for step in steps], part)
            for k, step in enumerate(steps):
                ref = self.partial(step).at[:, part]
                ref[...] = made[TOK * k : TOK * (k + 1)].astype(LOW)
                send(ref, self.pair_in.at[step, :, part], self.sems.at[0], self.sems.at[1 + n], at.sibling)
            return 0

        lax.fori_loop(0, 2, one, 0)

    def along(self, tiles, n):
        at, part = self.at, slice(256 * n, 256 * (n + 1))

        def away(step, total):
            ref = self.partial(3 + step).at[:, part]
            ref[...] = total.astype(LOW)
            send(ref, self.line_in.at[step - 1, :, part], self.sems.at[0], self.sems.at[5], z_peer(at, step))

        def one(p, _):
            steps = (2 + p, 1 - p)
            made = tiles(*[plus(at.z, step, 4) * 2 + at.c for step in steps], part)
            first = made[0:TOK] + self.pair_in[steps[0], :, part].astype(WIDE)
            second = made[TOK:] + self.pair_in[steps[1], :, part].astype(WIDE)
            away(steps[0], first)

            @pl.when(p == 0)
            def _():
                away(steps[1], second)

            @pl.when(p == 1)
            def _():
                self.mine[:, part] = second

            return 0

        got(self.pair_in.at[:, :, part], self.sems.at[1 + n], at)
        lax.fori_loop(0, 2, one, 0)

    def sent_all(self):
        gone(self.seven, self.sems.at[0], self.at)

    def arrived(self):
        got(self.line_in, self.sems.at[5], self.at)

    def total(self, here):
        value = self.mine[here, :]
        for k in range(3):
            value = value + self.line_in[k, here, :].astype(WIDE)
        return value


def order_tokens(r, at):
    before = (
        lax.broadcasted_iota(jnp.int32, (TOK, TOK), 0) > lax.broadcasted_iota(jnp.int32, (TOK, TOK), 1)
    )
    before = jnp.where(before, 1.0, 0.0).astype(LOW)

    def block(b, earlier):
        here = pl.ds(pl.multiple_of(b * TOK, TOK), TOK)
        named = r.named[here, :]
        flags = named.astype(WIDE)
        order = jnp.where(flags > 0.0, dot(before, named) + earlier, -1.0)
        r.order_row[:, here] = jnp.transpose(order)[0:32]
        for e in range(4):
            mine = jnp.where(lanes((TOK, 128)) == 4 * at.j + e, order, 0.0)
            column = jnp.sum(mine, axis=-1, keepdims=True).astype(jnp.int32)
            r.places[here, SLOTS * e : SLOTS * (e + 1)] = jnp.where(
                column == lanes((TOK, SLOTS)), 1.0, 0.0
            ).astype(LOW)
        return earlier + jnp.sum(flags, axis=0, keepdims=True)

    lax.fori_loop(0, 8, block, jnp.zeros((1, 128), WIDE))


def share_tokens(r, at):
    def block(b, _):
        here = pl.ds(pl.multiple_of(b * 256, 256), 256)
        named = r.named[here, :].astype(WIDE) > 0.0
        logits = jnp.where(named, dot(r.hidden_two[here, :], r.router[...]), -1e30)
        powers = jnp.where(named, jnp.exp(logits - jnp.max(logits, axis=-1, keepdims=True)), 0.0)
        shares = powers / jnp.sum(powers, axis=-1, keepdims=True)
        high, middle, lowest = three_parts(shares)
        parts = high + pltpu.roll(middle, 32, axis=1) + pltpu.roll(lowest, 64, axis=1)
        r.share_parts[here, :] = parts.astype(LOW)

        @pl.when(b == at.z)
        def _():
            r.shares[...] = jnp.where(at.c == 0, shares[0:TOK], shares[TOK:])

        return 0

    lax.fori_loop(0, 4, block, 0)


def three_parts(values):
    high = values.astype(LOW).astype(WIDE)
    middle = (values - high).astype(LOW).astype(WIDE)
    return high, middle, (values - high - middle).astype(LOW).astype(WIDE)


def hits(r, at, e, t):
    slot = lax.broadcasted_iota(jnp.int32, (TOK, SEQ), 0) + TOK * t
    return slot == r.order_row[pl.ds(4 * at.j + e, 1), :].astype(jnp.int32)


def pick_rows(r, at, e):
    def pick(t, _):
        r.partial[t] = jnp.where(hits(r, at, e, t), 1.0, 0.0).astype(LOW)
        return 0

    lax.fori_loop(0, 3, pick, 0)


def pick_upstream(r, at, e):
    pick_rows(r, at, e)
    here = pl.ds(pl.multiple_of(e * SLOTS, SLOTS), SLOTS)
    for n in range(4):
        part = slice(256 * n, 256 * (n + 1))
        r.slot_grad[here, part] = dot(r.partial[0:3].reshape(SLOTS, SEQ), r.upstream[:, part]).astype(LOW)
    r.low_grad[here, 512:1024] = tail_dot(r.slot_grad[here, :], r.down[e].reshape(512, D)).astype(LOW)
    return 0


def expert(r, at, e):
    here = pl.ds(pl.multiple_of(e * SLOTS, SLOTS), SLOTS)
    quarters = [slice(256 * n, 256 * (n + 1)) for n in range(4)]
    pick_rows(r, at, e)
    lane = lanes((SLOTS, 128))
    share = dot(r.partial[0:3].reshape(SLOTS, SEQ), r.share_parts[...])
    share = jnp.where((lane % 32 == 4 * at.j + e) & (lane < 96), share, 0.0)
    share = jnp.sum(share, axis=-1, keepdims=True)
    for n in quarters:
        r.rows[here, n] = dot(r.partial[0:3].reshape(SLOTS, SEQ), r.hidden_two[:, n]).astype(LOW)
    gate_dot = jnp.zeros((SLOTS, 1), WIDE)
    for n in range(2):
        part = slice(256 * n, 256 * (n + 1))
        gate_pre = dot(r.rows[here, :], r.gate[e, :, :, :, part].reshape(D, 256))
        up_pre = dot(r.rows[here, :], r.up[e, :, :, :, part].reshape(D, 256))
        later = slice(512 + 256 * n, 768 + 256 * n)
        product_grad = r.low_grad[here, later].astype(WIDE)
        sigmoid = 1.0 / (1.0 + jnp.exp(-gate_pre))
        silu = gate_pre * sigmoid
        product = silu * up_pre
        gate_dot = gate_dot + jnp.sum(product * product_grad, axis=-1, keepdims=True)
        product_grad = share * product_grad
        r.product[:, part] = (share * product).astype(LOW)
        r.low_grad[here, part] = (product_grad * up_pre * (sigmoid + silu * (1.0 - sigmoid))).astype(LOW)
        r.low_grad[here, later] = (product_grad * silu).astype(LOW)
    for n in quarters:
        r.made[:, n] = dot(r.product[...], r.down[e, :, :, :, n].reshape(512, 256)).astype(LOW)
    keep = pltpu.make_async_copy(r.made, r.made_far.at[here], r.load.at[3])
    keep.start()
    for n in quarters:
        down_grad = lead_dot(r.product[...], r.slot_grad[here, n])
        r.down[e, :, :, :, n] = down_grad.astype(LOW).reshape(4, 4, 32, 256)
    high, middle, lowest = three_parts(gate_dot)
    parts = jnp.where(lane == 0, high, jnp.where(lane == 1, middle, jnp.where(lane == 2, lowest, 0.0)))
    gate_rows = lead_dot(parts.astype(LOW), r.partial[0:3].reshape(SLOTS, SEQ))
    gate_row = gate_rows[0:1] + gate_rows[1:2] + gate_rows[2:3]
    for b in range(8):
        r.gate_grad[b, pl.ds(e, 1), :] = gate_row[:, TOK * b : TOK * (b + 1)]
    keep.wait()


def slot_grads(r, m):
    def one(e, _):
        here = pl.ds(pl.multiple_of(e * SLOTS, SLOTS), SLOTS)
        gate, up = r.gate[e, m].reshape(256, 512), r.up[e, m].reshape(256, 512)
        slot_grad = tail_dot(r.low_grad[here, 0:512], gate) + tail_dot(r.low_grad[here, 512:1024], up)
        r.slot_grad[here, 256 * m : 256 * (m + 1)] = slot_grad.astype(LOW)
        return 0

    lax.fori_loop(0, 4, one, 0)


def gate_up_grads(r, e):
    here = pl.ds(pl.multiple_of(e * SLOTS, SLOTS), SLOTS)
    for m in range(4):
        grads = lead_dot(r.rows[here, 256 * m : 256 * (m + 1)], r.low_grad[here, :]).astype(LOW)
        r.gate[e, m], r.up[e, m] = grads[:, 0:512].reshape(4, 64, 512), grads[:, 512:1024].reshape(4, 64, 512)


def expert_sums(r, at, e):
    halves = [r.down.at[e, :, :, :, pl.ds(512 * n, 512)] for n in range(2)]
    return (
        SumXY(at, [r.gate.at[e], r.up.at[e]], [way.at[e] for way in r.wide_ways], r.e_sems.at[e, 0], 64),
        SumXY(at, halves, [way.at[e] for way in r.half_ways], r.e_sems.at[e, 1], 32),
    )


def back(r, attended):
    at = place()
    r.wide_ways = (r.wide1, r.wide2, r.wide3, r.wide4)
    r.half_ways = (r.half1, r.half2, r.half3, r.half4)
    r.gate_grad[...] = jnp.zeros((8, 8, 128), WIDE)
    share_tokens(r, at)

    def wide(name, *experts):
        for e in experts:
            getattr(expert_sums(r, at, e)[0], name)()

    def half(name, *experts):
        for e in experts:
            getattr(expert_sums(r, at, e)[1], name)()

    def one(e, _):
        expert(r, at, e)
        half("step1", e)

        @pl.when(e > 0)
        def _():
            half("step2", e - 1)

        return 0

    lax.fori_loop(0, 4, one, 0)

    gate_copies = Shares(at, lambda b: r.gate_grad.at[b], r.gate_back.at[at.j], r.gate_back.at[0:7], r.c_sems)
    r.gate_back[pl.ds(at.j, 1)] = r.gate_grad[pl.ds(at.j, 1)]

    def two_blocks(ref, a, b):
        return jnp.concatenate([rows(ref, a)[...], rows(ref, b)[...]], axis=0)

    def partial(k):
        return r.partial.at[k]

    def slot_sums(a, b, n):
        return dot(two_blocks(r.places, a, b), r.slot_grad[:, n])

    hidden_sum = SumExpert(at, partial, r.partial, r.pair1, r.line1, r.mine1, r.s_sems.at[0])
    for n in range(4):
        slot_grads(r, n)
        hidden_sum.across(slot_sums, n)
        if n > 0:
            hidden_sum.along(slot_sums, n - 1)
        if n == 1:
            half("step2", 3)
            half("step3", 0)
    hidden_sum.along(slot_sums, 3)
    made_load = pltpu.make_async_copy(r.made_far, r.slot_grad, r.load.at[3])
    made_load.start()
    own = pl.ds(pl.multiple_of(at.j * TOK, TOK), TOK)
    r.hidden_own[...] = r.hidden_two[own, :]
    out_load = pltpu.make_async_copy(r.out_far, r.hidden_two, r.load.at[0])
    out_load.start()

    def two(e, _):
        gate_up_grads(r, e)
        wide("step1", e)
        return 0

    lax.fori_loop(0, 4, two, 0)
    half("step3", 1, 2, 3)
    attended.forward()
    gate_copies.wait_recv()
    gate_grad = jnp.concatenate(
        [r.gate_back[b][0:4] for b in range(8)] + [jnp.zeros((96, 128), WIDE)], axis=0
    )
    gate_grad = jnp.transpose(gate_grad)
    shares = r.shares[...]
    logit_grad = shares * (gate_grad - jnp.sum(shares * gate_grad, axis=-1, keepdims=True))
    logit_grad = logit_grad.astype(LOW)
    for m in range(4):
        router_grad = lead_dot(r.hidden_own[:, 256 * m : 256 * (m + 1)], logit_grad).astype(LOW)
        for x in range(4):
            r.dense[m, x, 192:256] = router_grad[64 * x : 64 * (x + 1)]
    for n in range(4):
        part = slice(256 * n, 256 * (n + 1))
        r.mine1[:, part] += tail_dot(logit_grad, r.router[part, :])
    made_load.wait()
    output_sum = SumExpert(
        at, lambda k: rows(r.upstream, k), r.upstream.at[0 : 7 * TOK], r.pair2, r.line2, r.mine2, r.s_sems.at[1]
    )
    for n in range(4):
        output_sum.across(slot_sums, n)
    hidden_sum.arrived()

    def norm_back(values, hidden_grad, gain):
        inverse = lax.rsqrt(jnp.mean(values * values, axis=-1, keepdims=True) + EPSILON)
        scaled = hidden_grad * gain
        mean = jnp.mean(scaled * values, axis=-1, keepdims=True)
        return inverse, scaled * inverse - values * (inverse * inverse * inverse * mean)

    def strip_back(t, gain_grad):
        here = pl.ds(pl.multiple_of(t * 32, 32), 32)
        residual, hidden_grad = r.residual[here, :], hidden_sum.total(here)
        inverse, residual_grad = norm_back(residual, hidden_grad, r.gains[1:2, :])
        residual_grad = residual_grad + r.cotangent[here, :].astype(WIDE)
        r.residual_grad[here, :] = residual_grad
        r.branch[here, :] = residual_grad.astype(LOW)
        return gain_grad + jnp.sum(hidden_grad * (residual * inverse), axis=0, keepdims=True)

    r.gains[2:3, :] = lax.fori_loop(0, 4, strip_back, jnp.zeros((1, D), WIDE))
    branch_copies = Shares(
        at, lambda b: columns(r.branch, b), rows(r.branch_part, at.j), r.branch_part.at[0 : 7 * TOK], r.b_sems
    )
    out_load.wait()
    for n in range(4):
        part = slice(256 * n, 256 * (n + 1))
        r.attended_grad[:, part] = tail_dot(r.branch[...], r.hidden_two[part, :]).astype(LOW)
    grad_copies = Shares(
        at, lambda b: columns(r.attended_grad, b), rows(r.attended_back, at.j), r.attended_back.at[0 : 7 * TOK],
        r.d_sems,
    )
    rows(r.branch_part, at.j)[...] = columns(r.branch, at.j)[...]
    rows(r.attended_back, at.j)[...] = columns(r.attended_grad, at.j)[...]
    hidden_sum.sent_all()

    wide("step2", 0)
    half("step4", 0, 1)
    for n in range(4):
        output_sum.along(slot_sums, n)
    for b in range(8):
        here = slice(TOK * b, TOK * (b + 1))
        gain_grad = jnp.concatenate(
            [jnp.zeros((33, TOK), WIDE), r.gains[2:3, here], jnp.zeros((94, TOK), WIDE)], axis=0
        )
        gain_grad = jnp.transpose(gain_grad)
        for t in range(2):
            m, x = b // 2, 2 * (b % 2) + t
            others = r.dense[m, x, 192:256].astype(WIDE) + gain_grad[64 * t : 64 * (t + 1)]
            r.dense[m, x, 192:256] = others.astype(LOW)
    half("step4", 2, 3)
    grad_copies.wait_recv()

    low_lanes = lanes((256, 128)) < 64
    r.key_grad[...] = jnp.zeros((SEQ, 128), WIDE)
    r.value_grad[...] = jnp.zeros((SEQ, 128), WIDE)
    for b in range(4):
        here = slice(256 * b, 256 * (b + 1))
        heads = []
        for head in range(2):
            query = one_head(r.queries[here, :], head) * SCALE
            grad = one_head(r.attended_back[here, :], head)
            inner = grad.astype(WIDE) * r.attended_head[here, :].astype(WIDE)
            inner = jnp.sum(inner, axis=-1, keepdims=True)
            log_total = r.log_total[here, head : head + 1]
            query_grad = jnp.zeros((256, 128), WIDE)
            for c in range(b + 1):
                part = slice(256 * c, 256 * (c + 1))
                probs = jnp.exp(tail_dot(query, r.keys[part, :]) - log_total)
                keep = allowed(r, b, c)
                if keep is not None:
                    probs = jnp.where(keep, probs, 0.0)
                prob_grad = tail_dot(grad, r.values[part, :])
                score_grad = (probs * (prob_grad - inner)).astype(LOW)
                query_grad = query_grad + dot(score_grad, r.keys[part, :])
                r.key_grad[part, :] += lead_dot(score_grad, query)
                r.value_grad[part, :] += lead_dot(probs.astype(LOW), grad)
            heads.append(query_grad)
        query_grad = jnp.where(low_lanes, heads[0], heads[1]) * SCALE
        cosine, sine = angles(r, here, (256, 128))
        r.qkv_grad[here, 0:128] = turn(query_grad, cosine, -sine).astype(LOW)
        if b > 0:
            wide("step2", b)
    low_lanes = lanes((TOK, 128)) < 64

    def finish_keys(b, _):
        here = pl.ds(pl.multiple_of(b * TOK, TOK), TOK)
        key_grad, value_grad = r.key_grad[here, :], r.value_grad[here, :]
        key_grad = key_grad + pltpu.roll(key_grad, 64, axis=1)
        value_grad = value_grad + pltpu.roll(value_grad, 64, axis=1)
        cosine, sine = angles(r, here, (TOK, 128))
        key_grad = turn(key_grad, cosine, -sine)
        r.qkv_grad[here, 128:256] = jnp.where(low_lanes, key_grad, value_grad).astype(LOW)
        return 0

    lax.fori_loop(0, 8, finish_keys, 0)

    output_sum.sent_all()
    hidden_load = pltpu.make_async_copy(r.hidden_far, r.upstream, r.load.at[1])
    hidden_load.start()

    branch_copies.wait_recv()
    attended.finish()
    hidden_load.wait()
    for m in range(4):
        here = slice(256 * m, 256 * (m + 1))
        grads = lead_dot(r.upstream[:, here], r.qkv_grad[...])
        gains = jnp.sum(grads * r.w_qkv[here, :].astype(WIDE), axis=-1, keepdims=True)
        gains = gains / r.router[here, 32:33].astype(WIDE)
        grads = grads.astype(LOW)
        out_grads = lead_dot(r.attended_all[:, here], r.branch_part[...]).astype(LOW)
        for x in range(4):
            part = slice(64 * x, 64 * (x + 1))
            r.dense[m, x, 0:64] = grads[part, 0:128]
            r.dense[m, x, 64:128] = grads[part, 128:256]
            r.dense[m, x, 128:192] = out_grads[part]
            others = r.dense[m, x, 192:256].astype(WIDE)
            r.dense[m, x, 192:256] = jnp.where(lanes((64, 128)) == 32, gains[part], others).astype(LOW)
    dense_sum = SumXY(
        at, [r.dense.at[:, :, pl.ds(128 * n, 128)] for n in range(2)], (r.dense1, r.dense2, r.dense3, r.dense4),
        r.f_sems, 128,
    )
    dense_sum.step1()

    def hidden_one_tile(a, b, n):
        return tail_dot(two_blocks(r.qkv_grad, a, b), r.w_qkv[n, :])

    input_sum = SumExpert(at, partial, r.partial, r.pair3, r.line3, r.mine1, r.s_sems.at[2])
    for n in range(4):
        input_sum.across(hidden_one_tile, n)
    wide("step3", 0, 1)
    dense_sum.step2()
    for n in range(4):
        input_sum.along(hidden_one_tile, n)
    branch_copies.wait_send()
    wide("step3", 2)
    wide("step4", 0)
    dense_sum.step3()
    wide("step3", 3)
    wide("step4", 1)
    dense_sum.step4()
    wide("step4", 2, 3)

    def own_shard(ref, e):
        return ref.at[e, at.y, at.x]

    def stores(e):
        arrays = ((r.gate, r.gate_out), (r.up, r.up_out), (r.down, r.down_out))
        return [
            pltpu.make_async_copy(own_shard(ref, e), out.at[e], r.store.at[e, n])
            for n, (ref, out) in enumerate(arrays)
        ]

    def finish_expert(e, _):
        wide_sum, half_sum = expert_sums(r, at, e)
        gate, up = wide_sum.step5()
        left, right = half_sum.step5()
        own_shard(r.gate, e)[...], own_shard(r.up, e)[...] = gate.astype(LOW), up.astype(LOW)
        down = own_shard(r.down, e)
        down[:, 0:512], down[:, 512:1024] = left.astype(LOW), right.astype(LOW)
        for copy in stores(e):
            copy.start()
        return 0

    output_sum.arrived()

    def strip_out(t, _):
        here = pl.ds(pl.multiple_of(t * 32, 32), 32)
        r.branch[here, :] = (r.residual[here, :] + output_sum.total(here)).astype(LOW)
        return 0

    lax.fori_loop(0, 4, strip_out, 0)
    output_store = pltpu.make_async_copy(r.branch, r.output, r.load.at[0])
    output_store.start()
    for n, total in enumerate(dense_sum.step5()):
        r.dense_total[n] = total.reshape(2, 8, 8, 128)
    last_copies = Shares(
        at, lambda b: r.dense_total.at[:, :, b], r.dense_back.at[at.j], r.dense_back.at[0:7], r.l_sems
    )
    r.dense_back[pl.ds(at.j, 1)] = r.dense_total[:, :, pl.ds(at.j, 1)].reshape(1, 2, 2, 8, 128)
    lax.fori_loop(0, 4, finish_expert, 0)

    input_sum.arrived()

    def strip_in(t, _):
        here = pl.ds(pl.multiple_of(t * 32, 32), 32)
        _, input_grad = norm_back(r.tokens[here, :].astype(WIDE), input_sum.total(here), r.gains[0:1, :])
        r.residual_grad[here, :] += input_grad
        return 0

    lax.fori_loop(0, 4, strip_in, 0)
    input_store = pltpu.make_async_copy(r.residual_grad, r.input_grad, r.load.at[1])
    input_store.start()
    last_copies.wait_recv()
    low_lanes = lanes((8, 128)) < 64
    others = jnp.zeros((8, 128), WIDE)
    for b in range(8):
        head = slice(128 * b, 128 * (b + 1))
        r.query_out[:, head] = r.dense_back[b, 0, 0]
        r.out_out[:, head] = r.dense_back[b, 1, 0]
        others = others + r.dense_back[b, 1, 1]
    for t in range(4):
        head = slice(128 * t, 128 * (t + 1))
        even, odd = r.dense_back[2 * t, 0, 1], r.dense_back[2 * t + 1, 0, 1]
        r.key_out[:, head] = jnp.where(low_lanes, even, pltpu.roll(odd, 64, axis=1))
        r.value_out[:, head] = jnp.where(low_lanes, pltpu.roll(even, 64, axis=1), odd)
    r.others_out[...] = others

    input_sum.sent_all()
    for copy in (gate_copies, grad_copies, last_copies):
        copy.wait_send()
    output_store.wait()
    input_store.wait()

    def ended(e, _):
        for copy in stores(e):
            copy.wait()
        for unit in expert_sums(r, at, e):
            unit.finish()
        return 0

    lax.fori_loop(0, 4, ended, 0)
    dense_sum.finish()

DMA = pltpu.SemaphoreType.DMA


def low(*shape):
    return pltpu.VMEM(shape, LOW)


def wide(*shape):
    return pltpu.VMEM(shape, WIDE)


def far(*shape, kind=WIDE):
    return pltpu.HBM(shape, kind)


OUTS = dict(
    output=far(TOK, D, kind=LOW), input_grad=far(TOK, D), query_out=wide(8, D), key_out=wide(8, 512),
    value_out=wide(8, 512), out_out=wide(8, D), others_out=wide(8, 128), gate_out=far(4, 64, 512, kind=LOW),
    up_out=far(4, 64, 512, kind=LOW), down_out=far(4, 32, D, kind=LOW), made_far=far(4 * SLOTS, D, kind=LOW),
    hidden_far=far(SEQ, D, kind=LOW), out_far=far(D, D, kind=LOW),
)
SCRATCH = dict(
    w_qkv=low(D, 256), router=low(D, 128), gains=wide(8, D), queries=low(SEQ, 128), keys=low(SEQ, 128),
    values=low(SEQ, 128), log_total=wide(SEQ, 128), attended=low(TOK, D), residual=wide(TOK, D),
    hidden_two=low(SEQ, D), upstream=low(SEQ, D), named=low(SEQ, 128),
    pack=wide(8, 24, 128), near=wide(8, 24, 128), stage=low(192, 128),
    out_mine=wide(8, D), out_other=wide(8, D), out_rows=low(64, 512),
    gate=low(4, 4, 4, 64, 512), up=low(4, 4, 4, 64, 512), down=low(4, 4, 4, 32, D),
    shares=wide(TOK, 128), order_row=wide(32, SEQ), places=low(SEQ, 4 * SLOTS),
    rows=low(4 * SLOTS, D), low_grad=low(4 * SLOTS, D), made=low(SLOTS, D), slot_grad=low(4 * SLOTS, D),
    gate_grad=wide(8, 8, 128), gate_back=wide(8, 8, 128),
    product=low(SLOTS, 512),
    wide1=low(4, 2, 2, 2, 64, 512), wide2=low(4, 2, 2, 4, 64, 512), wide3=low(4, 2, 2, 32, 512),
    wide4=low(4, 2, 2, 64, 512), half1=low(4, 2, 2, 2, 32, 512), half2=low(4, 2, 2, 4, 32, 512),
    half3=low(4, 2, 2, 16, 512), half4=low(4, 2, 2, 32, 512), dense=low(4, 4, 256, 128),
    dense1=low(2, 2, 2, 128, 128), dense2=low(2, 2, 4, 128, 128), dense3=low(2, 2, 64, 128),
    dense4=low(2, 2, 128, 128), dense_total=wide(2, 2, 8, 8, 128), dense_back=wide(8, 2, 2, 8, 128),
    partial=low(7, TOK, D), pair1=low(4, TOK, D), line1=low(3, TOK, D), mine1=wide(TOK, D),
    pair2=low(4, TOK, D), line2=low(3, TOK, D), mine2=wide(TOK, D), pair3=low(4, TOK, D), line3=low(3, TOK, D),
    residual_grad=wide(TOK, D), branch=low(TOK, D), branch_part=low(SEQ, 128), attended_grad=low(TOK, D),
    attended_back=low(SEQ, 128), attended_all=low(SEQ, D), key_grad=wide(SEQ, 128), value_grad=wide(SEQ, 128),
    qkv_grad=low(SEQ, 256), extra=wide(8, 128),
    x_sems=DMA((5,)), n_sems=DMA((5,)), g_sems=DMA((5,)), h_sems=DMA((5,)), t_sems=DMA((5,)), p_sems=DMA((2,)),
    c_sems=DMA((2,)), b_sems=DMA((2,)), d_sems=DMA((2,)), l_sems=DMA((2,)), w_sems=DMA((2, 4)),
    o_sems=DMA((2, 4)), a_sems=DMA((2,)), q_sems=DMA((6,)), e_sems=DMA((4, 2, 4, 2)), f_sems=DMA((4, 2)),
    s_sems=DMA((3, 6)), load=DMA((5,)), store=DMA((4, 3)),
)


def is_far(name):
    return name in OUTS and OUTS[name].memory_space != pltpu.VMEM or name in ("gate_in", "up_in", "down_in")


def spec(name):
    return pl.BlockSpec(memory_space=pl.ANY if is_far(name) else pltpu.VMEM)


def layer(**arrays):
    names = list(arrays) + list(OUTS) + list(SCRATCH)

    def kernel(*refs):
        r = SimpleNamespace(**dict(zip(names, refs)))
        r.hidden_one, r.w_out_all = r.slot_grad.at[0:SEQ], r.places.at[:, 0:D]
        r.attended_head = r.qkv_grad.at[:, 128:256]
        r.extra_all, r.corner = r.key_grad, r.value_grad.at[0:128]
        r.share_parts, r.hidden_own = r.qkv_grad.at[:, 0:128], r.attended_grad
        back(r, front(r))

    outs = pl.pallas_call(
        kernel,
        out_shape=[jax.ShapeDtypeStruct(OUTS[n].shape, OUTS[n].dtype) for n in OUTS],
        in_specs=[spec(n) for n in arrays],
        out_specs=[spec(n) for n in OUTS],
        scratch_shapes=list(SCRATCH.values()),
        name="layer",
        compiler_params=pltpu.CompilerParams(
            collective_id=0, has_side_effects=True, vmem_limit_bytes=510 << 17
        ),
    )(*arrays.values())
    return dict(zip(OUTS, outs))


def hand_on(*refs):
    others, sources, router, gains = refs[0], refs[1:10], refs[10], refs[11:13]
    targets, between, (come, go) = refs[13:22], refs[22:31], refs[31:33]
    narrow = refs[33:36]
    loads = [
        pltpu.make_async_copy(sources[n], narrow[n - 6] if n > 5 else between[n], come.at[n]) for n in range(9)
    ]
    stores = [pltpu.make_async_copy(between[n], targets[n], go.at[n]) for n in range(9)]
    for copy in loads:
        copy.start()
    router[...] = others[:, 0:32]
    turned = jnp.transpose(jnp.concatenate([others[...], jnp.zeros((120, 128), WIDE)], axis=0))
    for n in range(2):
        gains[n][...] = turned[32 + n : 33 + n, 0:8]
    for n, (load, store) in enumerate(zip(loads, stores)):
        load.wait()
        if n > 5:
            between[n][...] = narrow[n - 6][...].astype(WIDE)
        store.start()
    for copy in stores:
        copy.wait()


def handed_on(others, *arrays):
    near, away = pl.BlockSpec(memory_space=pltpu.VMEM), pl.BlockSpec(memory_space=pl.ANY)
    small = [jax.ShapeDtypeStruct(shape, WIDE) for shape in ((8, 32), (1, 8), (1, 8))]
    kinds = [LOW] + [WIDE] * 8
    return pl.pallas_call(
        hand_on,
        out_shape=small + [jax.ShapeDtypeStruct(a.shape, kind) for a, kind in zip(arrays, kinds)],
        in_specs=[near] + [away] * 9,
        out_specs=[near] * 3 + [away] * 9,
        scratch_shapes=[pltpu.VMEM(a.shape, kind) for a, kind in zip(arrays, kinds)]
        + [DMA((9,)), DMA((9,))]
        + [pltpu.VMEM(a.shape, LOW) for a in arrays[6:]],
        name="hand_on",
    )(others, *arrays)


def shards(
    tokens, segments, routes, gain_attn, gain_ffn, w_query, w_key, w_value, w_out, w_router, w_gate, w_up,
    w_down, cotangent,
):
    angle = np.arange(SEQ, dtype=np.float32)[:, None] * (
        np.float32(10000.0) ** (-np.arange(32, dtype=np.float32) / np.float32(32))
    )
    waves = np.concatenate([np.cos(angle), np.cos(angle), -np.sin(angle), np.sin(angle)], axis=1)
    made = layer(
        tokens=tokens, routes=routes.T, w_query=w_query, w_key=w_key, w_value=w_value, w_out=w_out,
        w_router=w_router, gain_attn=gain_attn.reshape(1, 8), gain_ffn=gain_ffn.reshape(1, 8),
        seg_row=segments, table=jnp.asarray(waves.astype(np.float32)), cotangent=cotangent,
        gate_in=w_gate.reshape(4, 4, 4, 64, 512), up_in=w_up.reshape(4, 4, 4, 64, 512),
        down_in=w_down.reshape(4, 4, 4, 32, D),
    )
    router, gain_one, gain_two, output, input_grad, query, key, value, out, gate, up, down = handed_on(
        made["others_out"], made["output"], made["input_grad"], made["query_out"], made["key_out"],
        made["value_out"], made["out_out"], made["gate_out"], made["up_out"], made["down_out"],
    )
    return (
        output, input_grad, gain_one.reshape(8), gain_two.reshape(8), query, key, value, out, router, gate, up, down,
    )


def solution(mesh):
    line, dense = P(("dp", "expert")), P(("dp", "expert"), None)
    copied, summed = P("expert", None, None), P("expert", "dp", None)
    return jax.shard_map(
        shards,
        mesh=mesh,
        in_specs=(dense, P("dp", None), dense, line, line) + (dense,) * 5 + (copied,) * 3 + (dense,),
        out_specs=(dense, dense, line, line) + (dense,) * 5 + (summed,) * 3,
        check_vma=False,
    )
```

```python
import functools
from types import SimpleNamespace

import jax
import jax.numpy as jnp
import numpy as np
from jax import lax
from jax.experimental import pallas as pl
from jax.experimental.pallas import tpu as pltpu
from jax.sharding import PartitionSpec as P

MESH = pl.DeviceIdType.MESH
LOW, WIDE = jnp.bfloat16, jnp.float32
EPSILON = 1e-06
SCALE = 64 ** (-0.5)
TOK, SEQ, D, SLOTS = 128, 1024, 1024, 384
Z_STEPS = (1, 3, 2)
EARLY = 1


def dot(one, two):
    return lax.dot_general(one, two, (((1,), (0,)), ((), ())), preferred_element_type=WIDE)


def tail_dot(one, two):
    return lax.dot_general(one, two, (((1,), (1,)), ((), ())), preferred_element_type=WIDE)


def lead_dot(one, two):
    return lax.dot_general(one, two, (((0,), (0,)), ((), ())), preferred_element_type=WIDE)


def place():
    i, j = lax.axis_index("dp"), lax.axis_index("expert")
    at = SimpleNamespace(i=i, j=j, x=lax.rem(i, 4), y=lax.div(i, 4), z=lax.div(j, 2), c=lax.rem(j, 2))
    at.sibling = (i, at.z * 2 + 1 - at.c)
    return at


def plus(value, step, size):
    return lax.rem(value + step, size)


def z_peer(at, step):
    return (at.i, plus(at.z, step, 4) * 2 + at.c)


def xy_peer(at, x_step, y_step):
    return (plus(at.y, y_step, 4) * 4 + plus(at.x, x_step, 4), at.j)


def send(source, target, sent, got, device):
    copy = pltpu.make_async_remote_copy(
        src_ref=source, dst_ref=target, send_sem=sent, recv_sem=got, device_id=device, device_id_type=MESH
    )
    copy.start()
    return copy


def rows(ref, block, size=TOK):
    return ref.at[pl.ds(pl.multiple_of(block * size, size), size)]


def columns(ref, block, size=128):
    return ref.at[:, pl.ds(pl.multiple_of(block * size, size), size)]


def got(ref, semaphore, at):
    pltpu.make_async_remote_copy(
        src_ref=ref, dst_ref=ref, send_sem=semaphore, recv_sem=semaphore, device_id=at.sibling, device_id_type=MESH
    ).wait_recv()


def gone(ref, semaphore, at):
    pltpu.make_async_remote_copy(
        src_ref=ref, dst_ref=ref, send_sem=semaphore, recv_sem=semaphore, device_id=at.sibling, device_id_type=MESH
    ).wait_send()


class Gather:
    def __init__(self, at, source, target, sems):
        self.at, self.source, self.target, self.sems = at, source, target, sems

    def start(self):
        at, mine = self.at, rows(self.target, self.at.j)
        for k, step in enumerate(Z_STEPS):
            send(self.source, mine, self.sems.at[0], self.sems.at[1 + k], z_peer(at, step))
        send(self.source, mine, self.sems.at[0], self.sems.at[4], at.sibling)

    def block(self, k):
        return plus(self.at.z, 4 - Z_STEPS[k], 4)

    def forward(self, *which):
        at = self.at
        for k in which or range(3):
            block = rows(self.target, self.block(k) * 2 + at.c)
            got(block, self.sems.at[1 + k], at)
            send(block, block, self.sems.at[0], self.sems.at[5 + k], at.sibling)

    def chip(self, k):
        got(self.target.at[0:TOK], self.sems.at[5 + k], self.at)
        return self.at.z if k < 0 else self.block(k)

    def finish(self, arrived=False):
        for k in range(-1, 3):
            if not arrived:
                self.chip(k)
        gone(self.target.at[0 : 7 * TOK], self.sems.at[0], self.at)


class Shares:
    def __init__(self, at, source, target, seven, sems):
        self.at, self.seven, self.sems = at, seven, sems
        for step in range(1, 8):
            other = plus(at.j, step, 8)
            send(source(other), target, sems.at[0], sems.at[1], (at.i, other))

    def wait_recv(self):
        got(self.seven, self.sems.at[1], self.at)

    def wait_send(self):
        gone(self.seven, self.sems.at[0], self.at)


class Spread:
    def __init__(self, at, source, target, four, three, sems):
        self.at, self.four, self.three, self.sems = at, four, three, sems
        for step in range(1, 16):
            y = step // 4
            send(source, target, sems.at[0, y], sems.at[1, y], xy_peer(at, step % 4, y))

    def wait_recv(self):
        got(self.three, self.sems.at[1, 0], self.at)
        for step in range(1, 4):
            got(self.four(plus(self.at.y, 4 - step, 4)), self.sems.at[1, step], self.at)

    def wait_send(self):
        gone(self.three, self.sems.at[0, 0], self.at)
        for step in range(1, 4):
            gone(self.four(plus(self.at.y, 4 - step, 4)), self.sems.at[0, step], self.at)


def greet(devices):
    barrier = pltpu.get_barrier_semaphore()
    for device in devices:
        pl.semaphore_signal(barrier, inc=1, device_id=device, device_id_type=MESH)
    return lambda: pl.semaphore_wait(barrier, len(devices))


def expert_peers(at):
    return [(at.i, plus(at.j, step, 8)) for step in range(1, 8)]


def dp_peers(at):
    return [xy_peer(at, step % 4, step // 4) for step in range(1, 16)]


def lanes(shape):
    return lax.broadcasted_iota(jnp.int32, shape, len(shape) - 1)


def turn(values, cosine, signed_sine):
    lane = lanes(values.shape)
    swapped = jnp.where(
        lane % 64 < 32, pltpu.roll(values, 96, axis=1), pltpu.roll(values, 32, axis=1)
    )
    return values * cosine + swapped * signed_sine


def angles(r, here, shape):
    table = r.table[here, :]
    other, low_lanes = pltpu.roll(table, 64, axis=1), lanes(shape) < 64
    return jnp.where(low_lanes, table, other), jnp.where(low_lanes, other, table)


def allowed(r, b, c):
    keep = None
    if c == 0 or b == 3:
        keep = r.log_total[256 * b : 256 * (b + 1), 2:3] == r.seg_row[:, 256 * c : 256 * (c + 1)].astype(WIDE)
    if b == c:
        below = lanes((256, 256)) <= lax.broadcasted_iota(jnp.int32, (256, 256), 0)
        keep = below if keep is None else keep & below
    return keep


def one_head(values, head):
    return jnp.where((lanes(values.shape) < 64) == (head == 0), values, jnp.zeros_like(values))


def front(r):
    at = place()
    ready = greet(expert_peers(at) + dp_peers(at))

    query_w, key_w = r.w_query[...].astype(WIDE), r.w_key[...].astype(WIDE)
    value_w = r.w_value[...].astype(WIDE)
    r.corner[...] = jnp.zeros((128, 128), WIDE)
    r.corner[32:33, 0:8] = r.gain_attn[...].astype(WIDE)
    r.corner[33:34, 0:8] = r.gain_ffn[...].astype(WIDE)
    r.extra[...] = jnp.transpose(r.corner[...])[0:8]
    r.extra[:, 0:32] = r.w_router[...].astype(WIDE)
    low_lanes = lanes((8, 128)) < 64
    for j in range(8):
        tile = slice(128 * (j // 2), 128 * (j // 2) + 128)
        key_part, value_part = key_w[:, tile], value_w[:, tile]
        if j % 2:
            key_part = pltpu.roll(key_part, 64, axis=1)
        else:
            value_part = pltpu.roll(value_part, 64, axis=1)
        head = slice(128 * j, 128 * j + 128)
        r.pack[j] = jnp.concatenate(
            [query_w[:, head], jnp.where(low_lanes, key_part, value_part), r.extra[...]], axis=0
        )
    r.out_mine[...] = r.w_out[...].astype(WIDE)
    r.near[at.j] = r.pack[at.j]
    expert = lax.broadcasted_iota(jnp.int32, (128, TOK), 0)
    named = jnp.zeros((128, TOK), WIDE)
    for k in range(8):
        named = named + jnp.where(r.routes[k : k + 1, :] == expert, 1.0, 0.0)
    rows(r.named, at.j)[...] = jnp.transpose(named).astype(LOW)
    rows(r.x_all, at.j)[...] = r.tokens[...]
    for b in range(8):
        here = slice(TOK * b, TOK * (b + 1))
        across = jnp.broadcast_to(r.seg_row[:, here].astype(WIDE), (TOK, TOK))
        r.log_total[here, :] = jnp.transpose(across)

    ready()
    pair = send(r.out_mine, r.out_other, r.q_sems.at[0], r.q_sems.at[1], at.sibling)
    first = Shares(at, lambda b: r.pack.at[b], r.near.at[at.j], r.near.at[0:7], r.p_sems)
    tokens = Gather(at, r.tokens, r.x_all, r.x_sems)
    tokens.start()
    pair.wait_recv()
    mine, other = r.out_mine[...], r.out_other[...]
    both = jnp.where(
        at.c == 0,
        jnp.concatenate([mine[:, 0:512], other[:, 0:512]], axis=0),
        jnp.concatenate([other[:, 512:1024], mine[:, 512:1024]], axis=0),
    )
    line = rows(r.out_rows, at.z, 16)
    line[...] = both.astype(LOW)
    for step in Z_STEPS:
        send(line, line, r.q_sems.at[2], r.q_sems.at[3], z_peer(at, step))
    marks = Gather(at, rows(r.named, at.j), r.named, r.n_sems)
    marks.start()
    loads = []
    for n, (source, target) in enumerate(((r.gate_in, r.gate), (r.up_in, r.up), (r.down_in, r.down))):
        loads.append(pltpu.make_async_copy(source, target, r.load.at[n]))
        loads[-1].start()
    first.wait_recv()
    for b in range(8):
        r.stage[16 * b : 16 * (b + 1)] = r.near[b, 0:16].astype(LOW)
    extras = [jnp.concatenate([r.near[b, 16:24] for b in some], axis=0) for some in (range(4), range(4, 8))]
    extras = jnp.where(lanes((32, 128)) < 64, extras[0], pltpu.roll(extras[1], 64, axis=1))
    r.stage[128:160] = extras.astype(LOW)
    second = Spread(
        at, r.stage, r.dense.at[at.y, at.x, 0:160], lambda y: r.dense.at[y, :, 0:160], r.dense.at[0, 0:3, 0:160],
        r.w_sems,
    )
    r.dense[at.y, at.x, 0:160] = r.stage[...]
    half = pl.ds(pl.multiple_of(at.c * 512, 512), 512)
    out_half = r.w_out_all.at[pl.ds(pl.multiple_of(at.i * 64, 64), 64), half]
    got(r.out_rows.at[0:48], r.q_sems.at[3], at)
    third = Spread(
        at, r.out_rows, out_half, lambda y: r.w_out_all.at[pl.ds(pl.multiple_of(y * 256, 256), 256), half],
        r.w_out_all.at[0:192, half], r.o_sems,
    )
    out_half[...] = r.out_rows[...]
    tokens.forward(0, 1)
    second.wait_recv()

    def unpack(i, _):
        part = r.dense[lax.div(i, 4), lax.rem(i, 4), 0:160].astype(WIDE)
        here = pl.ds(pl.multiple_of(i * 64, 64), 64)
        heads = part[0:128].reshape(8, 16, 128)
        r.w_qkv[here, 0:128] = heads[:, 0:8, :].reshape(64, 128).astype(LOW)
        r.w_qkv[here, 128:256] = heads[:, 8:16, :].reshape(64, 128).astype(LOW)
        extras = part[128:160]
        r.extra_all[here, :] = jnp.concatenate([extras, pltpu.roll(extras, 64, axis=1)], axis=0)
        return 0

    lax.fori_loop(0, 16, unpack, 0)
    r.gains[...] = extra_rows(r)
    r.router[...] = r.extra_all[...].astype(LOW)

    low_lanes = lanes((256, 128)) < 64

    def project(b):
        here = pl.ds(pl.multiple_of(b * 256, 256), 256)
        x = r.x_all[here, :].astype(WIDE)
        inverse = lax.rsqrt(jnp.mean(x * x, axis=-1, keepdims=True) + EPSILON)
        hidden = (x * inverse * r.gains[0:1, :]).astype(LOW)
        r.hidden_one[here, :] = hidden
        made = dot(hidden, r.w_qkv[...])
        cosine, sine = angles(r, here, (256, 128))
        r.queries[here, :] = turn(made[:, 0:128], cosine, sine).astype(LOW)
        pair = turn(
            made[:, 128:256], jnp.where(low_lanes, cosine, 1.0), jnp.where(low_lanes, sine, 0.0)
        )
        turned = pltpu.roll(pair, 64, axis=1)
        r.keys[here, :] = jnp.where(low_lanes, pair, turned).astype(LOW)
        r.values[here, :] = jnp.where(low_lanes, turned, pair).astype(LOW)

    for k in range(-1, 2):
        project(tokens.chip(k))
    tokens.forward(2)
    rows(r.upstream, at.j)[...] = r.cotangent[...]
    upstream = Gather(at, r.cotangent, r.upstream, r.g_sems)
    upstream.start()
    project(tokens.chip(2))
    tokens.finish(arrived=True)
    marks.forward()
    hidden_save = pltpu.make_async_copy(r.hidden_one, r.hidden_far, r.load.at[3])
    hidden_save.start()

    low_lanes = lanes((256, 128)) < 64
    scores = ((r.mine1, r.mine2), (r.residual, r.residual_grad))
    for b in range(4):
        here = slice(256 * b, 256 * (b + 1))
        logs, heads = [], []
        for head in range(2):
            query = one_head(r.queries[here, :], head) * SCALE
            top = jnp.full((256, 256), -1e30, WIDE)
            for c in range(b + 1):
                part = slice(256 * c, 256 * (c + 1))
                score, keep = tail_dot(query, r.keys[part, :]), allowed(r, b, c)
                if keep is not None:
                    score = jnp.where(keep, score, -1e30)
                scores[head][0][:, part], scores[head][1][:, part] = score[0:TOK], score[TOK:256]
                top = jnp.maximum(top, score)
            top = jnp.max(top, axis=-1, keepdims=True)
            mixed = jnp.zeros((256, 128), WIDE)
            for c in range(b + 1):
                part = slice(256 * c, 256 * (c + 1))
                score = jnp.concatenate([scores[head][0][:, part], scores[head][1][:, part]], axis=0)
                powers = jnp.exp(score - top).astype(LOW)
                value = r.values[part, :]
                mixed = mixed + dot(powers, jnp.where(low_lanes == (head == 0), value, jnp.ones_like(value)))
            total = mixed[:, 64:65] if head == 0 else mixed[:, 0:1]
            heads.append(mixed / total)
            logs.append(top + jnp.log(total))
        r.attended_head[here, :] = jnp.where(low_lanes, heads[0], heads[1]).astype(LOW)
        lane = lanes((256, 128))
        r.log_total[here, :] = jnp.where(
            lane == 0, logs[0], jnp.where(lane == 1, logs[1], r.log_total[here, :])
        )
        for n in (2 * b, 2 * b + 1):

            @pl.when(at.j != n)
            def _():
                send(
                    r.attended_head.at[TOK * n : TOK * (n + 1)], columns(r.attended, at.j), r.a_sems.at[0],
                    r.a_sems.at[1], (at.i, jnp.int32(n)),
                )

            @pl.when(at.j == n)
            def _():
                columns(r.attended, at.j)[...] = r.attended_head[TOK * n : TOK * (n + 1), :]

    third.wait_recv()
    out_mine = columns(r.w_out_all, at.c, 512)
    whole = send(out_mine, out_mine, r.q_sems.at[4], r.q_sems.at[5], at.sibling)
    upstream.forward()
    got(r.attended.at[:, 0 : 7 * 128], r.a_sems.at[1], at)
    whole.wait_recv()

    residual = r.tokens[...].astype(WIDE) + dot(r.attended[...], r.w_out_all[...])
    r.residual[...] = residual
    inverse = lax.rsqrt(jnp.mean(residual * residual, axis=-1, keepdims=True) + EPSILON)
    rows(r.hidden_two, at.j)[...] = (residual * inverse * r.gains[1:2, :]).astype(LOW)
    hidden = Gather(at, rows(r.hidden_two, at.j), r.hidden_two, r.h_sems)
    hidden.start()
    out_save = pltpu.make_async_copy(r.w_out_all, r.out_far, r.load.at[4])
    out_save.start()
    attended = Gather(at, r.attended, r.attended_all, r.t_sems)
    rows(r.attended_all, at.j)[...] = r.attended[...]
    for copy in (first, second, third, pair, whole):
        copy.wait_send()
    gone(r.out_rows.at[0:48], r.q_sems.at[2], at)
    gone(r.attended_head.at[0 : 7 * TOK], r.a_sems.at[0], at)
    upstream.finish()
    marks.finish()
    hidden_save.wait()
    out_save.wait()
    order_tokens(r, at)
    for copy in loads:
        copy.wait()
    lax.fori_loop(0, 4, lambda e, _: pick_upstream(r, at, e), 0)
    hidden.forward(0, 1)
    for k in range(-1, 2):
        share_tokens(r, at, hidden.chip(k))
    hidden.forward(2)
    share_tokens(r, at, hidden.chip(2))
    hidden.finish(arrived=True)
    attended.start()
    return attended


def extra_rows(r):
    picked = [jnp.transpose(r.extra_all[TOK * b : TOK * (b + 1), :])[32:40, :] for b in range(8)]
    return jnp.concatenate(picked, axis=1)


class SumXY:
    def __init__(self, at, sources, ways, sems, height):
        self.at, self.sources, self.ways, self.sems, self.height = at, sources, ways, sems, height

    def place(self, n):
        return (self.at.x, self.at.y) if n == 0 else (self.at.y, self.at.x)

    def block(self, n, first, second):
        return self.sources[n].at[second, first] if n == 0 else self.sources[n].at[first, second]

    def out(self, n, k, way, ref, second, step):
        device = xy_peer(self.at, step, 0) if (n == 0) != second else xy_peer(self.at, 0, step)
        send(ref, self.ways[k].at[n, way], self.sems.at[k, 0], self.sems.at[k, 1], device)

    def take(self, k):
        got(self.ways[k], self.sems.at[k, 1], self.at)

    def step1(self):
        for n in range(2):
            far = plus(self.place(n)[0], 2, 4)
            self.out(n, 0, 0, self.block(n, far, pl.ds(0, 2)), False, 1)
            self.out(n, 0, 1, self.block(n, far, pl.ds(2, 2)), False, 3)

    def step2(self):
        self.take(0)
        for n in range(2):
            for k, step in enumerate((1, 3)):
                near = plus(self.place(n)[0], step, 4)
                part = self.block(n, near, pl.ds(2 * k, 2))
                part[...] = part[...] + self.ways[0][n, k]
                self.out(n, 1, k, self.block(n, near, pl.ds(0, 4)), False, step)

    def step3(self):
        self.take(1)
        half = self.height // 2
        for n in range(2):
            first, second = self.place(n)
            mine = self.block(n, first, pl.ds(0, 4))
            mine[...] = mine[...] + (self.ways[1][n, 0] + self.ways[1][n, 1])
            far = self.block(n, first, plus(second, 2, 4))
            self.out(n, 2, 0, far.at[pl.ds(0, half)], True, 1)
            self.out(n, 2, 1, far.at[pl.ds(half, half)], True, 3)

    def step4(self):
        self.take(2)
        half = self.height // 2
        for n in range(2):
            first, second = self.place(n)
            for k, step in enumerate((1, 3)):
                near = self.block(n, first, plus(second, step, 4))
                part = near.at[pl.ds(half * k, half)]
                part[...] = part[...] + self.ways[2][n, k]
                self.out(n, 3, k, near, True, step)

    def step5(self):
        self.take(3)
        totals = []
        for n in range(2):
            mine = self.block(n, *self.place(n))[...].astype(WIDE)
            totals.append(mine + self.ways[3][n, 0].astype(WIDE) + self.ways[3][n, 1].astype(WIDE))
        return totals

    def finish(self):
        for k in range(4):
            gone(self.ways[k], self.sems.at[k, 0], self.at)


class SumExpert:
    def __init__(self, at, partial, seven, pair_in, line_in, mine, sems):
        self.at, self.partial, self.seven = at, partial, seven
        self.pair_in, self.line_in, self.mine, self.sems = pair_in, line_in, mine, sems

    def across(self, tiles, n):
        at, part = self.at, slice(256 * n, 256 * (n + 1))

        def one(p, _):
            steps = (2 + p, 1 - p)
            made = tiles(*[plus(at.z, step, 4) * 2 + 1 - at.c for step in steps], part)
            for k, step in enumerate(steps):
                ref = self.partial(step).at[:, part]
                ref[...] = made[TOK * k : TOK * (k + 1)].astype(LOW)
                send(ref, self.pair_in.at[step, :, part], self.sems.at[0], self.sems.at[1 + n], at.sibling)
            return 0

        lax.fori_loop(0, 2, one, 0)

    def along(self, tiles, n):
        at, part = self.at, slice(256 * n, 256 * (n + 1))

        def away(step, total):
            ref = self.partial(3 + step).at[:, part]
            ref[...] = total.astype(LOW)
            send(ref, self.line_in.at[step - 1, :, part], self.sems.at[0], self.sems.at[5], z_peer(at, step))

        def one(p, _):
            steps = (2 + p, 1 - p)
            made = tiles(*[plus(at.z, step, 4) * 2 + at.c for step in steps], part)
            first = made[0:TOK] + self.pair_in[steps[0], :, part].astype(WIDE)
            second = made[TOK:] + self.pair_in[steps[1], :, part].astype(WIDE)
            away(steps[0], first)

            @pl.when(p == 0)
            def _():
                away(steps[1], second)

            @pl.when(p == 1)
            def _():
                self.mine[:, part] = second

            return 0

        got(self.pair_in.at[:, :, part], self.sems.at[1 + n], at)
        lax.fori_loop(0, 2, one, 0)

    def sent_all(self):
        gone(self.seven, self.sems.at[0], self.at)

    def arrived(self):
        got(self.line_in, self.sems.at[5], self.at)

    def total(self, here):
        value = self.mine[here, :]
        for k in range(3):
            value = value + self.line_in[k, here, :].astype(WIDE)
        return value


def order_tokens(r, at):
    before = (
        lax.broadcasted_iota(jnp.int32, (TOK, TOK), 0) > lax.broadcasted_iota(jnp.int32, (TOK, TOK), 1)
    )
    before = jnp.where(before, 1.0, 0.0).astype(LOW)

    def block(b, earlier):
        here = pl.ds(pl.multiple_of(b * TOK, TOK), TOK)
        named = r.named[here, :]
        flags = named.astype(WIDE)
        order = jnp.where(flags > 0.0, dot(before, named) + earlier, -1.0)
        r.order_row[:, here] = jnp.transpose(order)[0:32]
        for e in range(4):
            mine = jnp.where(lanes((TOK, 128)) == 4 * at.j + e, order, 0.0)
            column = jnp.sum(mine, axis=-1, keepdims=True).astype(jnp.int32)
            r.places[here, SLOTS * e : SLOTS * (e + 1)] = jnp.where(
                column == lanes((TOK, SLOTS)), 1.0, 0.0
            ).astype(LOW)
        return earlier + jnp.sum(flags, axis=0, keepdims=True)

    lax.fori_loop(0, 8, block, jnp.zeros((1, 128), WIDE))


def share_tokens(r, at, b):
    here = pl.ds(pl.multiple_of(b * 256, 256), 256)
    named = r.named[here, :].astype(WIDE) > 0.0
    logits = jnp.where(named, dot(r.hidden_two[here, :], r.router[...]), -1e30)
    powers = jnp.where(named, jnp.exp(logits - jnp.max(logits, axis=-1, keepdims=True)), 0.0)
    shares = powers / jnp.sum(powers, axis=-1, keepdims=True)
    high, middle, lowest = three_parts(shares)
    parts = high + pltpu.roll(middle, 32, axis=1) + pltpu.roll(lowest, 64, axis=1)
    r.share_parts[here, :] = parts.astype(LOW)

    @pl.when(b == at.z)
    def _():
        r.shares[...] = jnp.where(at.c == 0, shares[0:TOK], shares[TOK:])


def three_parts(values):
    high = values.astype(LOW).astype(WIDE)
    middle = (values - high).astype(LOW).astype(WIDE)
    return high, middle, (values - high - middle).astype(LOW).astype(WIDE)


def hits(r, at, e, t):
    slot = lax.broadcasted_iota(jnp.int32, (TOK, SEQ), 0) + TOK * t
    return slot == r.order_row[pl.ds(4 * at.j + e, 1), :].astype(jnp.int32)


def pick_rows(r, at, e):
    def pick(t, _):
        r.partial[t] = jnp.where(hits(r, at, e, t), 1.0, 0.0).astype(LOW)
        return 0

    lax.fori_loop(0, 3, pick, 0)


def pick_upstream(r, at, e):
    pick_rows(r, at, e)
    here = pl.ds(pl.multiple_of(e * SLOTS, SLOTS), SLOTS)
    for n in range(4):
        part = slice(256 * n, 256 * (n + 1))
        r.slot_grad[here, part] = dot(r.partial[0:3].reshape(SLOTS, SEQ), r.upstream[:, part]).astype(LOW)
    r.low_grad[here, 512:1024] = tail_dot(r.slot_grad[here, :], r.down[e].reshape(512, D)).astype(LOW)
    return 0


def expert(r, at, e):
    here = pl.ds(pl.multiple_of(e * SLOTS, SLOTS), SLOTS)
    quarters = [slice(256 * n, 256 * (n + 1)) for n in range(4)]
    pick_rows(r, at, e)
    lane = lanes((SLOTS, 128))
    share = dot(r.partial[0:3].reshape(SLOTS, SEQ), r.share_parts[...])
    share = jnp.where((lane % 32 == 4 * at.j + e) & (lane < 96), share, 0.0)
    share = jnp.sum(share, axis=-1, keepdims=True)
    for n in quarters:
        r.rows[here, n] = dot(r.partial[0:3].reshape(SLOTS, SEQ), r.hidden_two[:, n]).astype(LOW)
    gate_dot = jnp.zeros((SLOTS, 1), WIDE)
    for n in range(2):
        part = slice(256 * n, 256 * (n + 1))
        gate_pre = dot(r.rows[here, :], r.gate[e, :, :, :, part].reshape(D, 256))
        up_pre = dot(r.rows[here, :], r.up[e, :, :, :, part].reshape(D, 256))
        later = slice(512 + 256 * n, 768 + 256 * n)
        product_grad = r.low_grad[here, later].astype(WIDE)
        sigmoid = 1.0 / (1.0 + jnp.exp(-gate_pre))
        silu = gate_pre * sigmoid
        product = silu * up_pre
        gate_dot = gate_dot + jnp.sum(product * product_grad, axis=-1, keepdims=True)
        product_grad = share * product_grad
        r.product[:, part] = (share * product).astype(LOW)
        r.low_grad[here, part] = (product_grad * up_pre * (sigmoid + silu * (1.0 - sigmoid))).astype(LOW)
        r.low_grad[here, later] = (product_grad * silu).astype(LOW)
    for n in quarters:
        made = dot(r.product[...], r.down[e, :, :, :, n].reshape(512, 256)).astype(LOW)
        r.partial[3:6, :, n] = made.reshape(3, TOK, 256)
    keep = [
        pltpu.make_async_copy(r.partial.at[3 + k], rows(r.made_far, 3 * e + k), r.keep.at[k]) for k in range(3)
    ]
    for copy in keep:
        copy.start()
    for n in quarters:
        down_grad = lead_dot(r.product[...], r.slot_grad[here, n])
        r.down[e, :, :, :, n] = down_grad.astype(LOW).reshape(4, 4, 32, 256)
    high, middle, lowest = three_parts(gate_dot)
    parts = jnp.where(lane == 0, high, jnp.where(lane == 1, middle, jnp.where(lane == 2, lowest, 0.0)))
    gate_rows = lead_dot(parts.astype(LOW), r.partial[0:3].reshape(SLOTS, SEQ))
    gate_row = gate_rows[0:1] + gate_rows[1:2] + gate_rows[2:3]
    for b in range(8):
        r.gate_grad[b, pl.ds(e, 1), :] = gate_row[:, TOK * b : TOK * (b + 1)]
    for copy in keep:
        copy.wait()


def slot_grads(r, e, m):
    here = pl.ds(pl.multiple_of(e * SLOTS, SLOTS), SLOTS)
    gate, up = r.gate[e, m].reshape(256, 512), r.up[e, m].reshape(256, 512)
    slot_grad = tail_dot(r.low_grad[here, 0:512], gate) + tail_dot(r.low_grad[here, 512:1024], up)
    r.slot_grad[here, 256 * m : 256 * (m + 1)] = slot_grad.astype(LOW)


def gate_up_grads(r, e):
    here = pl.ds(pl.multiple_of(e * SLOTS, SLOTS), SLOTS)
    for m in range(4):
        grads = lead_dot(r.rows[here, 256 * m : 256 * (m + 1)], r.low_grad[here, :]).astype(LOW)
        r.gate[e, m], r.up[e, m] = grads[:, 0:512].reshape(4, 64, 512), grads[:, 512:1024].reshape(4, 64, 512)


def expert_sums(r, at, e):
    halves = [r.down.at[e, :, :, :, pl.ds(512 * n, 512)] for n in range(2)]
    return (
        SumXY(at, [r.gate.at[e], r.up.at[e]], [way.at[e] for way in r.wide_ways], r.e_sems.at[e, 0], 64),
        SumXY(at, halves, [way.at[e] for way in r.half_ways], r.e_sems.at[e, 1], 32),
    )


def back(r, attended):
    at = place()
    r.wide_ways = (r.wide1, r.wide2, r.wide3, r.wide4)
    r.half_ways = (r.half1, r.half2, r.half3, r.half4)
    r.gate_grad[...] = jnp.zeros((8, 8, 128), WIDE)

    def wide(name, *experts):
        if len(experts) == 1:
            getattr(expert_sums(r, at, experts[0])[0], name)()
            return

        def one(e, _):
            getattr(expert_sums(r, at, e)[0], name)()
            return 0

        lax.fori_loop(experts[0], experts[-1] + 1, one, 0)

    def half(name, *experts):
        if len(experts) == 1:
            getattr(expert_sums(r, at, experts[0])[1], name)()
            return

        def one(e, _):
            getattr(expert_sums(r, at, e)[1], name)()
            return 0

        lax.fori_loop(experts[0], experts[-1] + 1, one, 0)

    def one(e, _):
        expert(r, at, e)
        half("step1", e)

        @pl.when(e < EARLY)
        def _():
            for m in range(4):
                slot_grads(r, e, m)
            gate_up_grads(r, e)
            wide("step1", e)

        @pl.when(e > 0)
        def _():
            half("step2", e - 1)

        @pl.when((e > 0) & (e <= EARLY))
        def _():
            wide("step2", e - 1)

        return 0

    lax.fori_loop(0, 4, one, 0)

    gate_copies = Shares(at, lambda b: r.gate_grad.at[b], r.gate_back.at[at.j], r.gate_back.at[0:7], r.c_sems)
    r.gate_back[pl.ds(at.j, 1)] = r.gate_grad[pl.ds(at.j, 1)]

    def two_blocks(ref, a, b):
        return jnp.concatenate([rows(ref, a)[...], rows(ref, b)[...]], axis=0)

    def partial(k):
        return r.partial.at[k]

    def slot_sums(a, b, n):
        return dot(two_blocks(r.places, a, b), r.slot_grad[:, n])

    hidden_sum = SumExpert(at, partial, r.partial, r.pair1, r.line1, r.mine1, r.s_sems.at[0])
    for n in range(4):
        for e in range(EARLY, 4):
            slot_grads(r, e, n)
        hidden_sum.across(slot_sums, n)
        if n > 0:
            hidden_sum.along(slot_sums, n - 1)
        if n == 1:
            half("step2", 3)
            half("step3", 0)
    hidden_sum.along(slot_sums, 3)
    made_load = pltpu.make_async_copy(r.made_far, r.slot_grad, r.load.at[3])
    made_load.start()
    own = pl.ds(pl.multiple_of(at.j * TOK, TOK), TOK)
    r.hidden_own[...] = r.hidden_two[own, :]
    out_load = pltpu.make_async_copy(r.out_far, r.hidden_two, r.load.at[0])
    out_load.start()

    def two(e, _):
        gate_up_grads(r, e)
        wide("step1", e)
        return 0

    lax.fori_loop(EARLY, 4, two, 0)
    hidden_load = pltpu.make_async_copy(r.hidden_far, r.rows.at[0:SEQ], r.load.at[1])
    hidden_load.start()
    half("step3", 1, 2, 3)
    attended.forward()
    wide("step3", 0)
    gate_copies.wait_recv()
    gate_grad = jnp.concatenate(
        [r.gate_back[b][0:4] for b in range(8)] + [jnp.zeros((96, 128), WIDE)], axis=0
    )
    gate_grad = jnp.transpose(gate_grad)
    shares = r.shares[...]
    logit_grad = shares * (gate_grad - jnp.sum(shares * gate_grad, axis=-1, keepdims=True))
    logit_grad = logit_grad.astype(LOW)
    for m in range(4):
        router_grad = lead_dot(r.hidden_own[:, 256 * m : 256 * (m + 1)], logit_grad).astype(LOW)
        for x in range(4):
            r.dense[m, x, 192:256] = router_grad[64 * x : 64 * (x + 1)]
    for n in range(4):
        part = slice(256 * n, 256 * (n + 1))
        r.mine1[:, part] += tail_dot(logit_grad, r.router[part, :])
    made_load.wait()
    output_sum = SumExpert(
        at, lambda k: rows(r.upstream, k), r.upstream.at[0 : 7 * TOK], r.pair2, r.line2, r.mine2, r.s_sems.at[1]
    )
    for n in range(4):
        output_sum.across(slot_sums, n)
    wide("step2", 1)
    hidden_sum.arrived()

    def norm_back(values, hidden_grad, gain):
        inverse = lax.rsqrt(jnp.mean(values * values, axis=-1, keepdims=True) + EPSILON)
        scaled = hidden_grad * gain
        mean = jnp.mean(scaled * values, axis=-1, keepdims=True)
        return inverse, scaled * inverse - values * (inverse * inverse * inverse * mean)

    def strip_back(t, gain_grad):
        here = pl.ds(pl.multiple_of(t * 32, 32), 32)
        residual, hidden_grad = r.residual[here, :], hidden_sum.total(here)
        inverse, residual_grad = norm_back(residual, hidden_grad, r.gains[1:2, :])
        residual_grad = residual_grad + r.cotangent[here, :].astype(WIDE)
        r.residual_grad[here, :] = residual_grad
        r.branch[here, :] = residual_grad.astype(LOW)
        return gain_grad + jnp.sum(hidden_grad * (residual * inverse), axis=0, keepdims=True)

    r.gains[2:3, :] = lax.fori_loop(0, 4, strip_back, jnp.zeros((1, D), WIDE))
    branch_copies = Shares(
        at, lambda b: columns(r.branch, b), rows(r.branch_part, at.j), r.branch_part.at[0 : 7 * TOK], r.b_sems
    )
    out_load.wait()
    for n in range(4):
        part = slice(256 * n, 256 * (n + 1))
        r.attended_grad[:, part] = tail_dot(r.branch[...], r.hidden_two[part, :]).astype(LOW)
    grad_copies = Shares(
        at, lambda b: columns(r.attended_grad, b), rows(r.attended_back, at.j), r.attended_back.at[0 : 7 * TOK],
        r.d_sems,
    )
    rows(r.branch_part, at.j)[...] = columns(r.branch, at.j)[...]
    rows(r.attended_back, at.j)[...] = columns(r.attended_grad, at.j)[...]
    hidden_sum.sent_all()

    wide("step4", 0)
    wide("step2", 2, 3)
    half("step4", 0, 1)
    for n in range(4):
        output_sum.along(slot_sums, n)
    for b in range(8):
        here = slice(TOK * b, TOK * (b + 1))
        gain_grad = jnp.concatenate(
            [jnp.zeros((33, TOK), WIDE), r.gains[2:3, here], jnp.zeros((94, TOK), WIDE)], axis=0
        )
        gain_grad = jnp.transpose(gain_grad)
        for t in range(2):
            m, x = b // 2, 2 * (b % 2) + t
            others = r.dense[m, x, 192:256].astype(WIDE) + gain_grad[64 * t : 64 * (t + 1)]
            r.dense[m, x, 192:256] = others.astype(LOW)
    half("step4", 2, 3)
    grad_copies.wait_recv()

    low_lanes = lanes((256, 128)) < 64
    r.key_grad[...] = jnp.zeros((SEQ, 128), WIDE)
    r.value_grad[...] = jnp.zeros((SEQ, 128), WIDE)
    for b in range(4):
        here = slice(256 * b, 256 * (b + 1))
        heads = []
        for head in range(2):
            query = one_head(r.queries[here, :], head) * SCALE
            grad = one_head(r.attended_back[here, :], head)
            inner = grad.astype(WIDE) * r.attended_head[here, :].astype(WIDE)
            inner = jnp.sum(inner, axis=-1, keepdims=True)
            log_total = r.log_total[here, head : head + 1]
            query_grad = jnp.zeros((256, 128), WIDE)
            for c in range(b + 1):
                part = slice(256 * c, 256 * (c + 1))
                probs = jnp.exp(tail_dot(query, r.keys[part, :]) - log_total)
                keep = allowed(r, b, c)
                if keep is not None:
                    probs = jnp.where(keep, probs, 0.0)
                prob_grad = tail_dot(grad, r.values[part, :])
                score_grad = (probs * (prob_grad - inner)).astype(LOW)
                query_grad = query_grad + dot(score_grad, r.keys[part, :])
                r.key_grad[part, :] += lead_dot(score_grad, query)
                r.value_grad[part, :] += lead_dot(probs.astype(LOW), grad)
            heads.append(query_grad)
        query_grad = jnp.where(low_lanes, heads[0], heads[1]) * SCALE
        cosine, sine = angles(r, here, (256, 128))
        r.qkv_grad[here, 0:128] = turn(query_grad, cosine, -sine).astype(LOW)
        if b == 3:
            wide("step3", 1)
    low_lanes = lanes((TOK, 128)) < 64

    def finish_keys(b, _):
        here = pl.ds(pl.multiple_of(b * TOK, TOK), TOK)
        key_grad, value_grad = r.key_grad[here, :], r.value_grad[here, :]
        key_grad = key_grad + pltpu.roll(key_grad, 64, axis=1)
        value_grad = value_grad + pltpu.roll(value_grad, 64, axis=1)
        cosine, sine = angles(r, here, (TOK, 128))
        key_grad = turn(key_grad, cosine, -sine)
        r.qkv_grad[here, 128:256] = jnp.where(low_lanes, key_grad, value_grad).astype(LOW)
        return 0

    lax.fori_loop(0, 8, finish_keys, 0)


    branch_copies.wait_recv()
    attended.finish()
    hidden_load.wait()
    for m in range(4):
        here = slice(256 * m, 256 * (m + 1))
        grads = lead_dot(r.rows[0:SEQ, here], r.qkv_grad[...])
        gains = jnp.sum(grads * r.w_qkv[here, :].astype(WIDE), axis=-1, keepdims=True)
        gains = gains / r.router[here, 32:33].astype(WIDE)
        grads = grads.astype(LOW)
        out_grads = lead_dot(r.attended_all[:, here], r.branch_part[...]).astype(LOW)
        for x in range(4):
            part = slice(64 * x, 64 * (x + 1))
            r.dense[m, x, 0:64] = grads[part, 0:128]
            r.dense[m, x, 64:128] = grads[part, 128:256]
            r.dense[m, x, 128:192] = out_grads[part]
            others = r.dense[m, x, 192:256].astype(WIDE)
            r.dense[m, x, 192:256] = jnp.where(lanes((64, 128)) == 32, gains[part], others).astype(LOW)
    dense_sum = SumXY(
        at, [r.dense.at[:, :, pl.ds(128 * n, 128)] for n in range(2)], (r.dense1, r.dense2, r.dense3, r.dense4),
        r.f_sems, 128,
    )
    dense_sum.step1()

    def hidden_one_tile(a, b, n):
        return tail_dot(two_blocks(r.qkv_grad, a, b), r.w_qkv[n, :])

    input_sum = SumExpert(at, partial, r.partial, r.pair3, r.line3, r.mine1, r.s_sems.at[2])
    for n in range(4):
        input_sum.across(hidden_one_tile, n)
    for n in range(4):
        input_sum.along(hidden_one_tile, n)
    branch_copies.wait_send()
    wide("step3", 2, 3)
    dense_sum.step2()
    wide("step4", 1, 2, 3)
    dense_sum.step3()
    dense_sum.step4()

    def own_shard(ref, e):
        return ref.at[e, at.y, at.x]

    def stores(e):
        arrays = ((r.gate, r.gate_out), (r.up, r.up_out), (r.down, r.down_out))
        return [
            pltpu.make_async_copy(own_shard(ref, e), out.at[e], r.store.at[e, n])
            for n, (ref, out) in enumerate(arrays)
        ]

    def finish_expert(e, _):
        wide_sum, half_sum = expert_sums(r, at, e)
        gate, up = wide_sum.step5()
        left, right = half_sum.step5()
        own_shard(r.gate, e)[...], own_shard(r.up, e)[...] = gate.astype(LOW), up.astype(LOW)
        down = own_shard(r.down, e)
        down[:, 0:512], down[:, 512:1024] = left.astype(LOW), right.astype(LOW)
        for copy in stores(e):
            copy.start()
        return 0

    output_sum.arrived()

    def strip_out(t, _):
        here = pl.ds(pl.multiple_of(t * 32, 32), 32)
        r.branch[here, :] = (r.residual[here, :] + output_sum.total(here)).astype(LOW)
        return 0

    lax.fori_loop(0, 4, strip_out, 0)
    output_store = pltpu.make_async_copy(r.branch, r.output, r.load.at[0])
    output_store.start()
    for n, total in enumerate(dense_sum.step5()):
        r.dense_total[n] = total.reshape(2, 8, 8, 128)
    last_copies = Shares(
        at, lambda b: r.dense_total.at[:, :, b], r.dense_back.at[at.j], r.dense_back.at[0:7], r.l_sems
    )
    r.dense_back[pl.ds(at.j, 1)] = r.dense_total[:, :, pl.ds(at.j, 1)].reshape(1, 2, 2, 8, 128)
    lax.fori_loop(0, 4, finish_expert, 0)

    input_sum.arrived()

    def strip_in(t, _):
        here = pl.ds(pl.multiple_of(t * 32, 32), 32)
        _, input_grad = norm_back(r.tokens[here, :].astype(WIDE), input_sum.total(here), r.gains[0:1, :])
        r.residual_grad[here, :] += input_grad
        return 0

    lax.fori_loop(0, 4, strip_in, 0)
    input_store = pltpu.make_async_copy(r.residual_grad, r.input_grad, r.load.at[1])
    input_store.start()
    last_copies.wait_recv()
    low_lanes = lanes((8, 128)) < 64
    others = jnp.zeros((8, 128), WIDE)
    for b in range(8):
        head = slice(128 * b, 128 * (b + 1))
        r.query_out[:, head] = r.dense_back[b, 0, 0]
        r.out_out[:, head] = r.dense_back[b, 1, 0]
        others = others + r.dense_back[b, 1, 1]
    for t in range(4):
        head = slice(128 * t, 128 * (t + 1))
        even, odd = r.dense_back[2 * t, 0, 1], r.dense_back[2 * t + 1, 0, 1]
        r.key_out[:, head] = jnp.where(low_lanes, even, pltpu.roll(odd, 64, axis=1))
        r.value_out[:, head] = jnp.where(low_lanes, pltpu.roll(even, 64, axis=1), odd)
    r.others_out[...] = others

    output_sum.sent_all()
    input_sum.sent_all()
    for copy in (gate_copies, grad_copies, last_copies):
        copy.wait_send()
    output_store.wait()
    input_store.wait()

    def ended(e, _):
        for copy in stores(e):
            copy.wait()
        for unit in expert_sums(r, at, e):
            unit.finish()
        return 0

    lax.fori_loop(0, 4, ended, 0)
    dense_sum.finish()

DMA = pltpu.SemaphoreType.DMA


def low(*shape):
    return pltpu.VMEM(shape, LOW)


def wide(*shape):
    return pltpu.VMEM(shape, WIDE)


def far(*shape, kind=WIDE):
    return pltpu.HBM(shape, kind)


OUTS = dict(
    output=far(TOK, D, kind=LOW), input_grad=far(TOK, D), query_out=wide(8, D), key_out=wide(8, 512),
    value_out=wide(8, 512), out_out=wide(8, D), others_out=wide(8, 128), gate_out=far(4, 64, 512, kind=LOW),
    up_out=far(4, 64, 512, kind=LOW), down_out=far(4, 32, D, kind=LOW), made_far=far(4 * SLOTS, D, kind=LOW),
    hidden_far=far(SEQ, D, kind=LOW), out_far=far(D, D, kind=LOW),
)
SCRATCH = dict(
    w_qkv=low(D, 256), router=low(D, 128), gains=wide(8, D), queries=low(SEQ, 128), keys=low(SEQ, 128),
    values=low(SEQ, 128), log_total=wide(SEQ, 128), attended=low(TOK, D), residual=wide(TOK, D),
    hidden_two=low(SEQ, D), upstream=low(SEQ, D), named=low(SEQ, 128),
    pack=wide(8, 24, 128), near=wide(8, 24, 128), stage=low(160, 128),
    out_mine=wide(8, D), out_other=wide(8, D), out_rows=low(64, 512),
    gate=low(4, 4, 4, 64, 512), up=low(4, 4, 4, 64, 512), down=low(4, 4, 4, 32, D),
    shares=wide(TOK, 128), order_row=wide(32, SEQ), places=low(SEQ, 4 * SLOTS),
    rows=low(4 * SLOTS, D), low_grad=low(4 * SLOTS, D), slot_grad=low(4 * SLOTS, D),
    gate_grad=wide(8, 8, 128), gate_back=wide(8, 8, 128),
    product=low(SLOTS, 512),
    wide1=low(4, 2, 2, 2, 64, 512), wide2=low(4, 2, 2, 4, 64, 512), wide3=low(4, 2, 2, 32, 512),
    wide4=low(4, 2, 2, 64, 512), half1=low(4, 2, 2, 2, 32, 512), half2=low(4, 2, 2, 4, 32, 512),
    half3=low(4, 2, 2, 16, 512), half4=low(4, 2, 2, 32, 512), dense=low(4, 4, 256, 128),
    dense1=low(2, 2, 2, 128, 128), dense2=low(2, 2, 4, 128, 128), dense3=low(2, 2, 64, 128),
    dense4=low(2, 2, 128, 128), dense_total=wide(2, 2, 8, 8, 128), dense_back=wide(8, 2, 2, 8, 128),
    partial=low(7, TOK, D), pair1=low(4, TOK, D), line1=low(3, TOK, D), mine1=wide(TOK, D),
    pair2=low(4, TOK, D), line2=low(3, TOK, D), mine2=wide(TOK, D), pair3=low(4, TOK, D), line3=low(3, TOK, D),
    residual_grad=wide(TOK, D), branch=low(TOK, D), branch_part=low(SEQ, 128), attended_grad=low(TOK, D),
    attended_back=low(SEQ, 128), attended_all=low(SEQ, D), key_grad=wide(SEQ, 128), value_grad=wide(SEQ, 128),
    qkv_grad=low(SEQ, 256), extra=wide(8, 128),
    x_sems=DMA((8,)), n_sems=DMA((8,)), g_sems=DMA((8,)), h_sems=DMA((8,)), t_sems=DMA((8,)), p_sems=DMA((2,)),
    c_sems=DMA((2,)), b_sems=DMA((2,)), d_sems=DMA((2,)), l_sems=DMA((2,)), w_sems=DMA((2, 4)),
    o_sems=DMA((2, 4)), a_sems=DMA((2,)), q_sems=DMA((6,)), e_sems=DMA((4, 2, 4, 2)), f_sems=DMA((4, 2)),
    s_sems=DMA((3, 6)), load=DMA((5,)), keep=DMA((3,)), store=DMA((4, 3)),
)


def is_far(name):
    return name in OUTS and OUTS[name].memory_space != pltpu.VMEM or name in ("gate_in", "up_in", "down_in")


def spec(name):
    return pl.BlockSpec(memory_space=pl.ANY if is_far(name) else pltpu.VMEM)


def layer(**arrays):
    names = list(arrays) + list(OUTS) + list(SCRATCH)

    def kernel(*refs):
        r = SimpleNamespace(**dict(zip(names, refs)))
        r.x_all = r.rows.at[0:SEQ]
        r.hidden_one, r.w_out_all = r.slot_grad.at[0:SEQ], r.places.at[:, 0:D]
        r.attended_head = r.qkv_grad.at[:, 128:256]
        r.extra_all, r.corner = r.key_grad, r.value_grad.at[0:128]
        r.share_parts, r.hidden_own = r.qkv_grad.at[:, 0:128], r.attended_grad
        back(r, front(r))

    outs = pl.pallas_call(
        kernel,
        out_shape=[jax.ShapeDtypeStruct(OUTS[n].shape, OUTS[n].dtype) for n in OUTS],
        in_specs=[spec(n) for n in arrays],
        out_specs=[spec(n) for n in OUTS],
        scratch_shapes=list(SCRATCH.values()),
        name="layer",
        compiler_params=pltpu.CompilerParams(
            collective_id=0, has_side_effects=True, vmem_limit_bytes=510 << 17
        ),
    )(*arrays.values())
    return dict(zip(OUTS, outs))


def hand_on(*refs):
    others, sources, router, gains = refs[0], refs[1:10], refs[10], refs[11:13]
    targets, between, (come, go) = refs[13:22], refs[22:31], refs[31:33]
    narrow = refs[33:36]
    loads = [
        pltpu.make_async_copy(sources[n], narrow[n - 6] if n > 5 else between[n], come.at[n]) for n in range(9)
    ]
    stores = [pltpu.make_async_copy(between[n], targets[n], go.at[n]) for n in range(9)]
    for copy in loads:
        copy.start()
    router[...] = others[:, 0:32]
    turned = jnp.transpose(jnp.concatenate([others[...], jnp.zeros((120, 128), WIDE)], axis=0))
    for n in range(2):
        gains[n][...] = turned[32 + n : 33 + n, 0:8]
    for n, (load, store) in enumerate(zip(loads, stores)):
        load.wait()
        if n > 5:
            between[n][...] = narrow[n - 6][...].astype(WIDE)
        store.start()
    for copy in stores:
        copy.wait()


def handed_on(others, *arrays):
    near, away = pl.BlockSpec(memory_space=pltpu.VMEM), pl.BlockSpec(memory_space=pl.ANY)
    small = [jax.ShapeDtypeStruct(shape, WIDE) for shape in ((8, 32), (1, 8), (1, 8))]
    kinds = [LOW] + [WIDE] * 8
    return pl.pallas_call(
        hand_on,
        out_shape=small + [jax.ShapeDtypeStruct(a.shape, kind) for a, kind in zip(arrays, kinds)],
        in_specs=[near] + [away] * 9,
        out_specs=[near] * 3 + [away] * 9,
        scratch_shapes=[pltpu.VMEM(a.shape, kind) for a, kind in zip(arrays, kinds)]
        + [DMA((9,)), DMA((9,))]
        + [pltpu.VMEM(a.shape, LOW) for a in arrays[6:]],
        name="hand_on",
    )(others, *arrays)


def shards(
    tokens, segments, routes, gain_attn, gain_ffn, w_query, w_key, w_value, w_out, w_router, w_gate, w_up,
    w_down, cotangent,
):
    angle = np.arange(SEQ, dtype=np.float32)[:, None] * (
        np.float32(10000.0) ** (-np.arange(32, dtype=np.float32) / np.float32(32))
    )
    waves = np.concatenate([np.cos(angle), np.cos(angle), -np.sin(angle), np.sin(angle)], axis=1)
    made = layer(
        tokens=tokens, routes=routes.T, w_query=w_query, w_key=w_key, w_value=w_value, w_out=w_out,
        w_router=w_router, gain_attn=gain_attn.reshape(1, 8), gain_ffn=gain_ffn.reshape(1, 8),
        seg_row=segments, table=jnp.asarray(waves.astype(np.float32)), cotangent=cotangent,
        gate_in=w_gate.reshape(4, 4, 4, 64, 512), up_in=w_up.reshape(4, 4, 4, 64, 512),
        down_in=w_down.reshape(4, 4, 4, 32, D),
    )
    router, gain_one, gain_two, output, input_grad, query, key, value, out, gate, up, down = handed_on(
        made["others_out"], made["output"], made["input_grad"], made["query_out"], made["key_out"],
        made["value_out"], made["out_out"], made["gate_out"], made["up_out"], made["down_out"],
    )
    return (
        output, input_grad, gain_one.reshape(8), gain_two.reshape(8), query, key, value, out, router, gate, up, down,
    )


def solution(mesh):
    line, dense = P(("dp", "expert")), P(("dp", "expert"), None)
    copied, summed = P("expert", None, None), P("expert", "dp", None)
    return jax.shard_map(
        shards,
        mesh=mesh,
        in_specs=(dense, P("dp", None), dense, line, line) + (dense,) * 5 + (copied,) * 3 + (dense,),
        out_specs=(dense, dense, line, line) + (dense,) * 5 + (summed,) * 3,
        check_vma=False,
    )
```
